32 devices in a mesh: dp: 8 (over z, core), tensor: 4 (over y, x).
Axes of the slice: x: 2, y: 2, z: 4, core: 2. Of those that a mesh axis runs over, the one named last changes fastest.
Arguments:
- hidden: bfloat16 [16, 1024, 2048], P('dp', 'tensor'), may hold values from -6 to 6
- cotangent: bfloat16 [16, 1024, 2048], P('dp', 'tensor'), may hold values from -6 to 6
- norm_gain: bfloat16 [2, 2048], P(None, 'dp'), may hold values from 0.5 to 1.5
- in_weights: bfloat16 [2, 2, 2048, 4096], P(None, None, 'dp', 'tensor'), may hold values from -0.125 to 0.125
- state_weight: bfloat16 [2, 2048, 256], P(None, 'dp'), may hold values from -0.125 to 0.125
- step_weight: bfloat16 [2, 2048, 64], P(None, 'dp', 'tensor'), may hold values from -0.0625 to 0.0625
- channel_taps: float32 [2, 5, 4096], P(None, None, 'tensor'), may hold values from -3 to 3
- state_taps: float32 [2, 5, 256], replicated, may hold values from -3 to 3
- step_bias: float32 [2, 64], P(None, 'tensor'), may hold values from -6 to -2
- decay_log: float32 [2, 64], P(None, 'tensor'), may hold values from -1 to 2
- skip_gain: float32 [2, 64], P(None, 'tensor'), may hold values from 0.5 to 1.5
- inner_gain: float32 [2, 4096], P(None, 'tensor'), may hold values from 0.5 to 1.5
- out_weight: bfloat16 [2, 4096, 2048], P(None, 'tensor', 'dp'), may hold values from -0.09375 to 0.09375
Outputs:
- mixed_out: float32 [16, 1024, 2048], P('dp', 'tensor')
- grad_hidden: float32 [16, 1024, 2048], P('dp', 'tensor')
- grad_norm_gain: float32 [2, 2048], P(None, 'dp')
- grad_in_weights: float32 [2, 2, 2048, 4096], P(None, None, 'dp', 'tensor')
- grad_state_weight: float32 [2, 2048, 256], P(None, 'dp')
- grad_step_weight: float32 [2, 2048, 64], P(None, 'dp', 'tensor')
- grad_channel_taps: float32 [2, 5, 4096], P(None, None, 'tensor')
- grad_state_taps: float32 [2, 5, 256], replicated
- grad_step_bias: float32 [2, 64], P(None, 'tensor')
- grad_decay_log: float32 [2, 64], P(None, 'tensor')
- grad_skip_gain: float32 [2, 64], P(None, 'tensor')
- grad_inner_gain: float32 [2, 4096], P(None, 'tensor')
- grad_out_weight: float32 [2, 4096, 2048], P(None, 'tensor', 'dp')
The draws below stay inside these ranges and needn't reach their ends.
All inputs are finite; a program needn't handle non-finite values.
Results may differ from the reference program's by a relative error of at most 0.025.
Values may be sent and summed in bfloat16 or wider, within the bound.
A program may use at most 384 MiB of HBM per device.

```python
import jax
import jax.numpy as jnp
from jax import lax

D = 2048
HEADS = 64
STATE = 128
CONV = 4
GROUP = 256
LAYERS = 2
SEQ_LEN = 1024
INNER = 4096
SEQS = 16


def block_scale(rng, extent, split, smallest, top_value):
    level = 1.0
    for axis_at, parts in split:
        heights = jax.random.uniform(jax.random.fold_in(jax.random.fold_in(rng, 6), axis_at), (parts,), jnp.float32, smallest / len(split), top_value / len(split))
        level = level * jnp.repeat(jnp.exp(heights), extent[axis_at] // parts).reshape((-1,) + (1,) * (len(extent) - 1 - axis_at))
    return level


def scatter_about(rng, shape, scale, limit, cuts=(), held_as=jnp.bfloat16):
    drawn = scale * jax.random.normal(rng, shape, jnp.float32)
    if cuts:
        drawn = drawn * block_scale(rng, shape, cuts, -0.22, 0.18)
    return jnp.clip(drawn, -limit, limit).astype(held_as)


def setup_inputs(seed: int = 0) -> dict:
    keys = jax.random.split(jax.random.key(seed), 14)
    return {
        "hidden": scatter_about(keys[0], (SEQS, SEQ_LEN, D), 1.0, 6.0, ((0, 8), (1, 4))),
        "cotangent": scatter_about(keys[1], (SEQS, SEQ_LEN, D), 1.0, 6.0, ((0, 8), (1, 4))),
        "norm_gain": jnp.clip(1.0 + 0.1 * jax.random.normal(keys[2], (LAYERS, D), jnp.float32), 0.5, 1.5).astype(jnp.bfloat16),
        "in_weights": scatter_about(keys[3], (LAYERS, 2, D, INNER), D ** -0.5, 0.125, ((2, 8), (3, 4))),
        "state_weight": scatter_about(keys[4], (LAYERS, D, 2 * STATE), D ** -0.5, 0.125, ((1, 8),)),
        "step_weight": scatter_about(keys[5], (LAYERS, D, HEADS), (4 * D) ** -0.5, 0.0625, ((1, 8), (2, 4))),
        "channel_taps": scatter_about(keys[6], (LAYERS, CONV + 1, INNER), CONV ** -0.5, 3.0, ((2, 4),), jnp.float32),
        "state_taps": scatter_about(keys[7], (LAYERS, CONV + 1, 2 * STATE), CONV ** -0.5, 3.0, (), jnp.float32),
        "step_bias": jnp.clip(-6.0 + 4.0 * jax.random.uniform(keys[8], (LAYERS, HEADS), jnp.float32) ** block_scale(keys[8], (LAYERS, HEADS), ((1, 4),), -0.2, 0.2), -6.0, -2.0),
        "decay_log": jnp.clip(-1.0 + 3.0 * jax.random.uniform(keys[9], (LAYERS, HEADS), jnp.float32) ** block_scale(keys[9], (LAYERS, HEADS), ((1, 4),), -0.2, 0.2), -1.0, 2.0),
        "skip_gain": jnp.clip(0.5 + 1.0 * jax.random.uniform(keys[10], (LAYERS, HEADS), jnp.float32) ** block_scale(keys[10], (LAYERS, HEADS), ((1, 4),), -0.2, 0.2), 0.5, 1.5),
        "inner_gain": jnp.clip(1.0 + 0.1 * jax.random.normal(keys[11], (LAYERS, INNER), jnp.float32), 0.5, 1.5),
        "out_weight": scatter_about(keys[12], (LAYERS, INNER, D), INNER ** -0.5, 0.09375, ((1, 4), (2, 8))),
    }


EPSILON = 1e-05
HIGHEST = lax.Precision.HIGHEST

@jax.custom_vjp
def low(v):
    return lax.optimization_barrier(v.astype(jnp.bfloat16)).astype(jnp.float32)

@jax.custom_vjp
def low_back(v):
    return v

def low_keep(v):
    return (low(v), None)

def low_pass(kept, grad):
    return (grad,)

def back_keep(v):
    return (v, None)

def back_low(kept, grad):
    return (low(grad),)
low.defvjp(low_keep, low_pass)
low_back.defvjp(back_keep, back_low)

def causal_conv(signal, taps_table):
    tap_count = taps_table.shape[0] - 1
    length = signal.shape[0]
    padded = jnp.pad(signal, ((tap_count - 1, 0), (0, 0)))
    summed = jnp.broadcast_to(taps_table[tap_count], signal.shape)
    for offset in range(tap_count):
        summed = summed + taps_table[offset] * padded[offset:offset + length]
    return summed

def scan_block(state, segment):
    rates, inputs, key_rows, query_rows = segment
    length = rates.shape[0]
    running = jnp.cumsum(rates, axis=0)
    causal = jnp.tril(jnp.ones((length, length), jnp.float32))
    spread = running[:, None, :] - running[None, :, :]
    decay = jnp.exp(jnp.where(causal[:, :, None] > 0, spread, 0.0)) * causal[:, :, None]
    scores = jnp.dot(query_rows, key_rows.T, precision=HIGHEST)
    inside = jnp.einsum('tsh,shp->thp', scores[:, :, None] * decay, inputs, precision=HIGHEST)
    carried = jnp.einsum('tn,hnp->thp', query_rows, state, precision=HIGHEST) * jnp.exp(running)[:, :, None]
    remain = jnp.exp(running[-1][None, :] - running)
    fresh = jnp.einsum('sn,shp->hnp', key_rows, inputs * remain[:, :, None], precision=HIGHEST)
    return (state * jnp.exp(running[-1])[:, None, None] + fresh, inside + carried)

def state_scan(inputs, rates, key_rows, query_rows):
    length, head_count, head_width = inputs.shape
    blocks = length // GROUP
    segments = (rates.reshape(blocks, GROUP, head_count), inputs.reshape(blocks, GROUP, head_count, head_width), key_rows.reshape(blocks, GROUP, -1), query_rows.reshape(blocks, GROUP, -1))
    initial = jnp.zeros((head_count, key_rows.shape[1], head_width), jnp.float32)
    _, pieces = lax.scan(jax.checkpoint(scan_block), initial, segments)
    return pieces.reshape(length, head_count, head_width)

def mixer(gate_in, conv_in, step_in, shared_in, channel_taps, state_taps, step_bias, decay_log, skip_gain):
    length = gate_in.shape[0]
    head_count = step_in.shape[1]
    conv_out = jax.nn.silu(causal_conv(conv_in, channel_taps))
    shared = jax.nn.silu(causal_conv(shared_in, state_taps))
    half_width = shared.shape[1] // 2
    step_size = jax.nn.softplus(step_in + step_bias)
    values = conv_out.reshape(length, head_count, -1)
    rates = step_size * -jnp.exp(decay_log)
    scanned = state_scan(values * step_size[:, :, None], rates, shared[:, :half_width], shared[:, half_width:])
    scanned = scanned + skip_gain[:, None] * values
    return scanned.reshape(length, -1) * jax.nn.silu(gate_in)

def mamba_layer(stream, params):
    norm_gain, in_weights, state_weight, step_weight, channel_taps, state_taps, step_bias, decay_log, skip_gain, inner_gain, out_weight = params
    row_scale = lax.rsqrt(lax.optimization_barrier(jnp.mean(stream * stream, axis=-1, keepdims=True)) + EPSILON)
    normed = low(stream * row_scale * norm_gain)
    gate_in = low_back(jnp.dot(normed, in_weights[0], precision=HIGHEST))
    conv_in = low_back(jnp.dot(normed, in_weights[1], precision=HIGHEST))
    step_in = low_back(jnp.dot(normed, step_weight, precision=HIGHEST))
    shared_in = jnp.dot(normed, state_weight, precision=HIGHEST)
    gated = mixer(gate_in, conv_in, step_in, shared_in, channel_taps, state_taps, step_bias, decay_log, skip_gain)
    inner_scale = lax.rsqrt(lax.optimization_barrier(jnp.mean(gated * gated, axis=-1, keepdims=True)) + EPSILON)
    mixed = low(gated * inner_scale * inner_gain)
    return stream + low_back(jnp.dot(mixed, out_weight, precision=HIGHEST))

def reference(hidden, cotangent, norm_gain, in_weights, state_weight, step_weight, channel_taps, state_taps, step_bias, decay_log, skip_gain, inner_gain, out_weight):
    params = tuple((member.astype(jnp.float32) for member in (norm_gain, in_weights, state_weight, step_weight, channel_taps, state_taps, step_bias, decay_log, skip_gain, inner_gain, out_weight)))

    def forward(inputs, weights):

        def one_sequence(sequence):
            stream = sequence
            for layer_at in range(LAYERS):
                stream = mamba_layer(stream, tuple((member[layer_at] for member in weights)))
            return stream
        return lax.map(jax.checkpoint(one_sequence), inputs)
    output, pullback = jax.vjp(forward, hidden.astype(jnp.float32), params)
    grad_input, weight_grads = pullback(cotangent.astype(jnp.float32))
    return (output, grad_input, weight_grads[0], weight_grads[1], weight_grads[2], weight_grads[3], weight_grads[4], weight_grads[5], weight_grads[6], weight_grads[7], weight_grads[8], weight_grads[9], weight_grads[10])
```

```python
import functools

import jax
import jax.numpy as jnp
from jax import lax
from jax.experimental import pallas as pl
from jax.experimental.pallas import tpu as pltpu
from jax.sharding import PartitionSpec as P

EPSILON = 1e-05
CHUNK = 128
GROUP_LANES = 256
LOG2E = 1.4426950408889634
F32 = jnp.float32
BF16 = jnp.bfloat16
NN = (((1,), (0,)), ((), ()))
NT = (((1,), (1,)), ((), ()))
TN = (((0,), (0,)), ((), ()))


def mm(a, b, dims=NN):
    return lax.dot_general(a, b, dims, preferred_element_type=F32)


def sigmoid(v):
    return 0.5 * jnp.tanh(0.5 * v) + 0.5


def softplus(v):
    return jnp.maximum(v, 0.0) + jnp.log(1.0 + jnp.exp(-jnp.abs(v)))


def split3(v):
    high = v.astype(BF16)
    rest = v - high.astype(F32)
    mid = rest.astype(BF16)
    return high, mid, (rest - mid.astype(F32)).astype(BF16)


def spread(v, expand, heads):
    high = v.astype(BF16)
    low = (v - high.astype(F32)).astype(BF16)
    lane = lax.broadcasted_iota(jnp.int32, v.shape, 1)
    parts = jnp.where(lane < heads, high, jnp.where(lane < 2 * heads, low, jnp.zeros_like(low)))
    return mm(parts, expand)


def conv_rows(window, table, length):
    total = table[4:5] + table[3:4] * window[8 : 8 + length]
    for back in range(1, 4):
        total = total + table[3 - back : 4 - back] * pltpu.roll(window, back, 0)[8 : 8 + length]
    return total


def causal(length, flip):
    row = lax.broadcasted_iota(jnp.int32, (length, length), 0)
    col = lax.broadcasted_iota(jnp.int32, (length, length), 1)
    return (row <= col) if flip else (row >= col)


def head_masks(lanes, width):
    lane = lax.broadcasted_iota(jnp.int32, (1, lanes), 1)
    return [(lane >= j * width) & (lane < (j + 1) * width) for j in range(lanes // width)]


def gate_lanes(start, part):
    at = start // part * 2 * part + start % part
    return slice(at, at + GROUP_LANES), slice(at + part, at + part + GROUP_LANES)


def forward_kernel(heads, part, columns_ref, small_ref, chan_ref, taps_ref, head_ref, expand_ref, tri_ref,
                   mixed_ref, square_ref, y_ref, saved_ref, state, xbuf, sbuf):
    length, channels = y_ref.shape
    width = channels // heads
    shared = taps_ref.shape[1]
    half = shared // 2

    @pl.when(pl.program_id(0) == 0)
    def _():
        state[...] = jnp.zeros_like(state)
        xbuf[0:8] = jnp.zeros((8, channels), F32)
        sbuf[0:8] = jnp.zeros((8, shared), F32)

    sbuf[8:] = small_ref[:, :shared]
    tri = tri_ref[...]
    expand = expand_ref[...]
    dt = softplus(small_ref[:, shared:] + head_ref[0:1])
    running = sum(mm(tri, piece) for piece in split3(dt * (head_ref[1:2] * LOG2E)))
    running_t = running.T
    decay_in = jnp.exp2(running)
    decay_out = jnp.exp2(running[length - 1 :] - running)
    dt_wide = spread(dt, expand, heads)
    in_wide = spread(decay_in, expand, heads)
    out_wide = spread(dt * decay_out, expand, heads)

    taps = taps_ref[...]
    bc = conv_rows(sbuf[...], taps, length)
    bc = (bc * sigmoid(bc)).astype(BF16)
    keys, queries = bc[:, :half], bc[:, half:]
    scores = jnp.where(causal(length, False), mm(queries, keys, NT), 0.0)
    squares = jnp.zeros((length, 128), F32)
    masks = head_masks(GROUP_LANES, width)
    for start in range(0, channels, GROUP_LANES):
        lanes = slice(start, start + GROUP_LANES)
        gate_at, conv_at = gate_lanes(start, part)
        table = chan_ref[:, lanes]
        xbuf[8:, lanes] = columns_ref[:, conv_at].astype(F32)
        c = conv_rows(xbuf[:, lanes], table, length)
        xbuf[0:8, lanes] = xbuf[length:, lanes]
        xs = c * sigmoid(c)
        values = (xs * dt_wide[:, lanes]).astype(BF16)
        weights, parts = [], []
        for j in range(GROUP_LANES // width):
            h = start // width + j
            gap = jnp.minimum(running[:, h : h + 1] - running_t[h : h + 1, :], 0.0)
            weights.append((scores * jnp.exp2(gap)).astype(BF16))
            parts.append(jnp.where(masks[j], values, jnp.zeros_like(values)))
        before = state[:, lanes]
        before_low = before.astype(BF16)
        saved_ref[0, :, lanes] = before_low
        y = mm(jnp.concatenate(weights, axis=1), jnp.concatenate(parts, axis=0))
        y = y + mm(queries, before_low) * in_wide[:, lanes]
        y_ref[:, lanes] = y
        z = columns_ref[:, gate_at].astype(F32)
        gated = (y + table[5:6] * xs) * (z * sigmoid(z))
        mixed_ref[:, lanes] = (gated * table[6:7]).astype(BF16)
        power = gated * gated
        for at in range(0, GROUP_LANES, 128):
            squares = squares + power[:, at : at + 128]
        fresh = mm(keys, (xs * out_wide[:, lanes]).astype(BF16), TN)
        state[:, lanes] = before * in_wide[length - 1 :, lanes] + fresh
    square_ref[...] = jnp.sum(squares, axis=1, keepdims=True)
    sbuf[0:8] = sbuf[length:]


def backward_kernel(heads, part, columns_ref, halo_ref, small_ref, shalo_ref, y_ref, saved_ref, up_ref, pull_ref,
                    chan_ref, taps_ref, head_ref, expand_ref, tri_ref,
                    dcolumns_ref, dsmall_ref, gchan_ref, gtaps_ref, ghead_ref,
                    dstate, xbuf, sbuf, dxbuf, dsbuf):
    length, channels = y_ref.shape
    width = channels // heads
    shared = taps_ref.shape[1]
    half = shared // 2
    step_no = pl.program_id(0)
    first_block = step_no == pl.num_programs(0) - 1

    @pl.when(step_no == 0)
    def _():
        dstate[...] = jnp.zeros_like(dstate)
        dxbuf[length:] = jnp.zeros((8, channels), F32)
        dsbuf[length:] = jnp.zeros((8, shared), F32)
        gchan_ref[...] = jnp.zeros_like(gchan_ref)
        gtaps_ref[...] = jnp.zeros_like(gtaps_ref)
        ghead_ref[...] = jnp.zeros_like(ghead_ref)

    sbuf[8:] = small_ref[:, :shared]
    sbuf[0:8] = jnp.where(first_block, 0.0, shalo_ref[:, :shared])
    tri = tri_ref[...]
    expand = expand_ref[...]
    step = small_ref[:, shared:] + head_ref[0:1]
    dt = softplus(step)
    rate = dt * head_ref[1:2]
    running = sum(mm(tri, piece) for piece in split3(rate * LOG2E))
    running_t = running.T
    decay_in = jnp.exp2(running)
    decay_out = jnp.exp2(running[length - 1 :] - running)
    dt_wide = spread(dt, expand, heads)
    in_wide = spread(decay_in, expand, heads)
    out_wide = spread(decay_out, expand, heads)

    taps = taps_ref[...]
    bc_in = conv_rows(sbuf[...], taps, length)
    bc_sig = sigmoid(bc_in)
    bc = (bc_in * bc_sig).astype(BF16)
    keys, queries = bc[:, :half], bc[:, half:]
    keep = causal(length, True)
    scores = jnp.where(keep, mm(keys, queries, NT), 0.0)
    pull = pull_ref[...]
    masks = head_masks(GROUP_LANES, width)
    dscores = jnp.zeros((length, length), F32)
    dkeys = jnp.zeros((length, half), F32)
    dqueries = jnp.zeros((length, half), F32)
    drun = jnp.zeros((length, 128), F32)
    ddt = jnp.zeros((length, 128), F32)
    last_row = lax.broadcasted_iota(jnp.int32, (length, 1), 0) == length - 1
    per_group = GROUP_LANES // width
    for start in range(0, channels, GROUP_LANES):
        lanes = slice(start, start + GROUP_LANES)
        gate_at, conv_at = gate_lanes(start, part)
        table = chan_ref[:, lanes]
        xbuf[8:, lanes] = columns_ref[:, conv_at].astype(F32)
        xbuf[0:8, lanes] = jnp.where(first_block, 0.0, halo_ref[:, conv_at].astype(F32)[-8:])
        c = conv_rows(xbuf[:, lanes], table, length)
        c_sig = sigmoid(c)
        xs = c * c_sig
        z = columns_ref[:, gate_at].astype(F32)
        z_sig = sigmoid(z)
        z_silu = z * z_sig
        y = y_ref[:, lanes]
        total = y + table[5:6] * xs
        gated = total * z_silu
        up = up_ref[:, lanes].astype(F32)
        gchan_ref[6:7, lanes] += jnp.sum(up * gated, axis=0, keepdims=True)
        dgated = table[6:7] * up - gated * pull
        dcolumns_ref[:, gate_at] = (dgated * total * (z_sig + z_silu * (1.0 - z_sig))).astype(BF16)
        dy = dgated * z_silu
        gchan_ref[5:6, lanes] += jnp.sum(dy * xs, axis=0, keepdims=True)
        dy_low = dy.astype(BF16)
        dt_lanes = dt_wide[:, lanes]
        values = (xs * dt_lanes).astype(BF16)
        weights, dparts, vparts, decays = [], [], [], []
        for j in range(per_group):
            h = start // width + j
            decay = jnp.exp2(jnp.minimum(running_t[h : h + 1, :] - running[:, h : h + 1], 0.0))
            decays.append(decay)
            weights.append((scores * decay).astype(BF16))
            dparts.append(jnp.where(masks[j], dy_low, jnp.zeros_like(dy_low)))
            vparts.append(jnp.where(masks[j], values, jnp.zeros_like(values)))
        outer = mm(jnp.concatenate(vparts, axis=0), dy_low, NT)
        for j in range(per_group):
            dscores = dscores + outer[j * length : (j + 1) * length] * decays[j]
        dvalues = mm(jnp.concatenate(weights, axis=1), jnp.concatenate(dparts, axis=0))
        before = saved_ref[0, :, lanes]
        dafter = dstate[:, lanes]
        dafter_low = dafter.astype(BF16)
        out_lanes = out_wide[:, lanes]
        carried = mm(keys, dafter_low) * out_lanes
        dvalues = dvalues + carried
        values_f = values.astype(F32)
        dkeys = dkeys + mm((values_f * out_lanes).astype(BF16), dafter_low, NT)
        in_lanes = in_wide[:, lanes]
        dy_in = (dy * in_lanes).astype(BF16)
        dqueries = dqueries + mm(dy_in, before, NT)
        end_decay = in_lanes[length - 1 :]
        at_end = jnp.sum(values_f * carried, axis=0, keepdims=True) + end_decay * jnp.sum(
            before.astype(F32) * dafter, axis=0, keepdims=True
        )
        dstate[:, lanes] = end_decay * dafter + mm(queries, dy_in, TN)
        turn = dy_low.astype(F32) * y - values_f * dvalues + jnp.where(last_row, at_end, 0.0)
        turn_high = turn.astype(BF16)
        turn_low = (turn - turn_high.astype(F32)).astype(BF16)
        group_expand = expand[:, lanes]
        drun = drun + mm(turn_high, group_expand, NT) + mm(turn_low, group_expand, NT)
        ddt = ddt + mm((dvalues * xs).astype(BF16), group_expand, NT)
        dxs = dvalues * dt_lanes + table[5:6] * dy
        dc = dxs * (c_sig + xs * (1.0 - c_sig))
        dxbuf[0:length, lanes] = dc
        window = dxbuf[:, lanes]
        here = xbuf[8:, lanes]
        gchan_ref[4:5, lanes] += jnp.sum(dc, axis=0, keepdims=True)
        gchan_ref[3:4, lanes] += jnp.sum(dc * here, axis=0, keepdims=True)
        dconv = table[3:4] * dc
        for ahead in range(1, 4):
            moved = pltpu.roll(window, length + 8 - ahead, 0)[:length]
            gchan_ref[3 - ahead : 4 - ahead, lanes] += jnp.sum(moved * here, axis=0, keepdims=True)
            dconv = dconv + table[3 - ahead : 4 - ahead] * moved
        dcolumns_ref[:, conv_at] = dconv.astype(BF16)
        dxbuf[length:, lanes] = dxbuf[0:8, lanes]

    dscores_low = jnp.where(keep, dscores, 0.0).astype(BF16)
    dkeys = dkeys + mm(dscores_low, queries)
    dqueries = dqueries + mm(dscores_low, keys, TN)
    dbc = jnp.concatenate([dkeys, dqueries], axis=1) * (bc_sig + bc_in * bc_sig * (1.0 - bc_sig))
    dsbuf[0:length] = dbc
    window = dsbuf[...]
    here = sbuf[8:]
    gtaps_ref[4:5] += jnp.sum(dbc, axis=0, keepdims=True)
    gtaps_ref[3:4] += jnp.sum(dbc * here, axis=0, keepdims=True)
    dshared = taps[3:4] * dbc
    for ahead in range(1, 4):
        moved = pltpu.roll(window, length + 8 - ahead, 0)[:length]
        gtaps_ref[3 - ahead : 4 - ahead] += jnp.sum(moved * here, axis=0, keepdims=True)
        dshared = dshared + taps[3 - ahead : 4 - ahead] * moved
    dsmall_ref[:, :shared] = dshared.astype(dsmall_ref.dtype)
    dsbuf[length:] = dsbuf[0:8]

    high, mid, low = split3(drun)
    drate = mm(tri, high, TN) + mm(tri, mid, TN) + mm(tri, low, TN)
    dstep = (ddt + drate * head_ref[1:2]) * sigmoid(step)
    ghead_ref[0:1] += jnp.sum(dstep, axis=0, keepdims=True)
    ghead_ref[1:2] += jnp.sum(drate * rate, axis=0, keepdims=True)
    lane = lax.broadcasted_iota(jnp.int32, dstep.shape, 1)
    dsmall_ref[:, shared:] = jnp.where(lane < heads, dstep, 0.0).astype(dsmall_ref.dtype)


def scan_tables(heads, channels):
    row = lax.broadcasted_iota(jnp.int32, (128, channels), 0) % heads
    col = lax.broadcasted_iota(jnp.int32, (128, channels), 1) // (channels // heads)
    return (row == col).astype(BF16), jnp.tril(jnp.ones((CHUNK, CHUNK), BF16))


def whole(array):
    return pl.BlockSpec(array.shape, lambda i: (0,) * array.ndim)


def mixer_forward(columns, small, tables, heads):
    tokens, channels = columns.shape[0], columns.shape[1] // 2
    shared = tables[1].shape[1]
    blocks = tokens // CHUNK

    def rows(cols):
        return pl.BlockSpec((CHUNK, cols), lambda i: (i, 0))

    return pl.pallas_call(
        functools.partial(forward_kernel, heads, channels // 2),
        grid=(blocks,),
        in_specs=[rows(2 * channels), rows(small.shape[1])] + [whole(table) for table in tables],
        out_specs=[
            rows(channels),
            rows(1),
            rows(channels),
            pl.BlockSpec((1, shared // 2, channels), lambda i: (i, 0, 0)),
        ],
        out_shape=[
            jax.ShapeDtypeStruct((tokens, channels), BF16),
            jax.ShapeDtypeStruct((tokens, 1), F32),
            jax.ShapeDtypeStruct((tokens, channels), F32),
            jax.ShapeDtypeStruct((blocks, shared // 2, channels), BF16),
        ],
        scratch_shapes=[
            pltpu.VMEM((shared // 2, channels), F32),
            pltpu.VMEM((CHUNK + 8, channels), F32),
            pltpu.VMEM((CHUNK + 8, shared), F32),
        ],
        compiler_params=pltpu.CompilerParams(vmem_limit_bytes=48 * 1024 * 1024),
        cost_estimate=pl.CostEstimate(
            flops=tokens * channels * 6000, bytes_accessed=tokens * channels * 14, transcendentals=tokens * channels * 6
        ),
        name="mixer_forward",
    )(columns, small, *tables)


def mixer_backward(columns, small, y, saved, up, pull, tables, heads):
    tokens, channels = columns.shape[0], columns.shape[1] // 2
    shared = tables[1].shape[1]
    blocks = tokens // CHUNK

    def rows(cols):
        return pl.BlockSpec((CHUNK, cols), lambda i: (blocks - 1 - i, 0))

    def earlier(count, cols):
        per_block = CHUNK // count
        return pl.BlockSpec((count, cols), lambda i: (jnp.maximum((blocks - 1 - i) * per_block - 1, 0), 0))

    def fixed(r, c):
        return pl.BlockSpec((r, c), lambda i: (0, 0))

    return pl.pallas_call(
        functools.partial(backward_kernel, heads, channels // 2),
        grid=(blocks,),
        in_specs=[
            rows(2 * channels),
            earlier(8 if columns.dtype == F32 else 16, 2 * channels),
            rows(small.shape[1]),
            earlier(8, small.shape[1]),
            rows(channels),
            pl.BlockSpec((1, shared // 2, channels), lambda i: (blocks - 1 - i, 0, 0)),
            rows(channels),
            rows(1),
        ]
        + [whole(table) for table in tables],
        out_specs=[rows(2 * channels), rows(small.shape[1]), fixed(8, channels), fixed(8, shared), fixed(8, 128)],
        out_shape=[
            jax.ShapeDtypeStruct((tokens, 2 * channels), BF16),
            jax.ShapeDtypeStruct((tokens, small.shape[1]), BF16),
            jax.ShapeDtypeStruct((8, channels), F32),
            jax.ShapeDtypeStruct((8, shared), F32),
            jax.ShapeDtypeStruct((8, 128), F32),
        ],
        scratch_shapes=[
            pltpu.VMEM((shared // 2, channels), F32),
            pltpu.VMEM((CHUNK + 8, channels), F32),
            pltpu.VMEM((CHUNK + 8, shared), F32),
            pltpu.VMEM((CHUNK + 8, channels), F32),
            pltpu.VMEM((CHUNK + 8, shared), F32),
        ],
        compiler_params=pltpu.CompilerParams(vmem_limit_bytes=56 * 1024 * 1024),
        cost_estimate=pl.CostEstimate(
            flops=tokens * channels * 14000, bytes_accessed=tokens * channels * 20, transcendentals=tokens * channels * 6
        ),
        name="mixer_backward",
    )(columns, columns, small, small, y, saved, up, pull, *tables)


class Place:
    def __init__(self):
        self.members = lax.axis_size("tensor")
        self.groups = self.members // 2
        self.at = lax.axis_index("tensor")
        self.sequence = self.at % 2
        self.group = self.at // 2
        self.core = lax.axis_index("dp") % 2

    def to_pair(self, v):
        return lax.ppermute(v, "tensor", [(t, t ^ 1) for t in range(self.members)])

    def to_core(self, v):
        return lax.ppermute(v, "dp", [(t, t ^ 1) for t in range(lax.axis_size("dp"))])

    def to_group(self, v, hop):
        return lax.ppermute(
            v, "tensor", [(t, (t + 2 * hop) % self.members) for t in range(self.members)]
        )

    def rows_of(self, v, hop):
        count = v.shape[0] // self.groups
        return lax.dynamic_slice_in_dim(v, (self.group + hop) % self.groups * count, count, 0)

    def gather_rows(self, v):
        count = v.shape[0]
        total = jnp.zeros((count * self.groups,) + v.shape[1:], v.dtype)
        total = lax.dynamic_update_slice_in_dim(total, v, self.group * count, 0)
        for hop in range(1, self.groups):
            start = (self.group - hop) % self.groups * count
            total = lax.dynamic_update_slice_in_dim(total, self.to_group(v, hop), start, 0)
        return total

    def add_groups(self, v):
        return v + sum(self.to_group(v, hop) for hop in range(1, self.groups))

    def scatter_rows(self, product):
        arrived = [
            self.to_group(product(hop).astype(BF16), hop) for hop in range(1, self.groups)
        ]
        return product(0) + sum(piece.astype(F32) for piece in arrived)

    def in_order(self, mine, other, first):
        return jnp.where(first == 0, jnp.concatenate([mine, other]), jnp.concatenate([other, mine]))

    def take_sequence(self, v):
        mine = jnp.where(self.sequence == 0, v[0], v[1])
        other = self.to_pair(jnp.where(self.sequence == 0, v[1], v[0]))
        return self.in_order(mine, other, self.sequence)

    def give_sequence(self, v):
        count = v.shape[0] // 2
        mine = lax.dynamic_slice_in_dim(v, self.sequence * count, count, 0)
        other = self.to_pair(lax.dynamic_slice_in_dim(v, (1 - self.sequence) * count, count, 0))
        return jnp.where(
            self.sequence == 0, jnp.stack([mine, other]), jnp.stack([other, mine])
        )

    def other_shard(self, v):
        fetched = self.to_pair(lax.dynamic_index_in_dim(v, self.core, 0, keepdims=False))
        swapped = self.to_core(fetched)
        first = jnp.where(self.core == 0, fetched, swapped)
        return first, jnp.where(self.core == 0, swapped, fetched)

    def fold_other(self, own, other):
        arrived = self.to_core(lax.dynamic_index_in_dim(other, 1 - self.core, 0, keepdims=False))
        kept = lax.dynamic_index_in_dim(other, self.core, 0, keepdims=False)
        summed = (kept.astype(F32) + arrived.astype(F32)).astype(BF16)
        landed = self.to_pair(summed)
        lane = lax.broadcasted_iota(jnp.int32, own.shape, 0)
        return own + jnp.where(lane == self.core, landed[None], jnp.zeros_like(own))


def norm_scale(stream):
    return lax.rsqrt(jnp.mean(stream * stream, axis=-1, keepdims=True) + EPSILON)


def block_forward(place, stream, weights, tables, heads, inner):
    big, small_cols, out_cols, gain = weights
    row_scale = norm_scale(stream)
    normed = place.gather_rows((stream * row_scale * gain).astype(BF16))
    columns = mm(normed, big).astype(BF16)
    small = mm(normed, small_cols)
    mixed, square, y, saved = mixer_forward(columns, small, tables, heads)
    scale = lax.rsqrt(place.add_groups(square) / inner + EPSILON)
    update = place.scatter_rows(lambda hop: mm(place.rows_of(mixed, hop), out_cols))
    after = stream + update * place.rows_of(scale, 0)
    return after, (stream, normed, columns, small, mixed, y, saved, scale, update)


def block_backward(place, grad, last_up, weights, tables, heads, inner, kept):
    big, small_cols, out_cols, gain = weights
    stream, normed, columns, small, mixed, y, saved, scale, update = kept
    if last_up is None:
        own_scale = place.rows_of(scale, 0)
        own_up = (grad * own_scale).astype(BF16)
        own_pull = jnp.sum(own_up.astype(F32) * update, axis=-1, keepdims=True) * (own_scale * own_scale / inner)
        up = place.gather_rows(own_up)
        pull = place.gather_rows(own_pull)
        grad_mixed = mm(up, out_cols, NT)
    else:
        up = (last_up.astype(F32) * scale).astype(BF16)
        grad_mixed = mm(up, out_cols, NT)
        product = jnp.sum(grad_mixed * mixed.astype(F32), axis=-1, keepdims=True)
        pull = place.add_groups(product) * (scale * scale / inner)
    grad_out = mm(mixed, up, TN).astype(BF16)
    dcolumns, dsmall, gchan, gtaps, ghead = mixer_backward(
        columns, small, y, saved, grad_mixed, pull, tables, heads
    )
    grad_normed = place.scatter_rows(
        lambda hop: mm(place.rows_of(dcolumns, hop), big, NT) + mm(place.rows_of(dsmall, hop), small_cols, NT)
    )
    own_cols = dcolumns.shape[1] // 4

    def grad_part(at):
        return mm(normed, dcolumns[:, at * own_cols : (at + 1) * own_cols], TN).astype(BF16)

    grad_other = jnp.stack([grad_part(2), grad_part(3)])
    grad_own = jnp.stack([grad_part(0), grad_part(1)])
    grad_small = mm(normed, dsmall, TN)
    row_scale = norm_scale(stream)
    unit = stream * row_scale
    grad_gain = jnp.sum(grad_normed * unit, axis=0)
    lifted = grad_normed * gain
    grad = grad + row_scale * (lifted - unit * jnp.mean(lifted * unit, axis=-1, keepdims=True))
    return grad, (grad_own, grad_other, grad_small, grad_out, grad_gain, gchan, gtaps, ghead)


def local(
    hidden,
    cotangent,
    norm_gain,
    in_weights,
    state_weight,
    step_weight,
    channel_taps,
    state_taps,
    step_bias,
    decay_log,
    skip_gain,
    inner_gain,
    out_weight,
):
    place = Place()
    layers = in_weights.shape[0]
    own_heads = step_bias.shape[1]
    heads = 2 * own_heads
    own_cols = in_weights.shape[3]
    channels = 2 * own_cols
    width = own_cols // own_heads
    inner = own_cols * place.members
    shared = state_weight.shape[2]
    copies = 128 // heads
    expand, tri = scan_tables(heads, channels)

    stream = place.take_sequence(hidden).astype(F32)
    last_up = place.gather_rows(place.take_sequence(cotangent))

    per_channel = jnp.concatenate([channel_taps, inner_gain[:, None]], axis=1)
    per_head = jnp.stack([step_bias, decay_log, skip_gain], axis=1)
    packed = jnp.concatenate([per_channel.reshape(layers, -1), per_head.reshape(layers, -1)], axis=1)
    arrived = place.to_pair(packed)
    split_at = per_channel[0].size
    per_channel = jnp.concatenate([per_channel, arrived[:, :split_at].reshape(per_channel.shape)], axis=2)
    per_head = jnp.concatenate([per_head, arrived[:, split_at:].reshape(per_head.shape)], axis=2)

    thin = jnp.concatenate([state_weight, step_weight, norm_gain[:, :, None]], axis=2)
    thin = lax.all_gather(thin, "dp", axis=1, tiled=True)
    state_cols = thin[:, :, :shared]
    step_cols = thin[:, :, shared : shared + own_heads]
    step_cols = jnp.concatenate([step_cols, place.to_pair(step_cols)], axis=2)
    gains = thin[:, :, -1].astype(F32)

    weights, tables = [], []
    for layer in range(layers):
        pair = lax.all_gather(in_weights[layer], "dp", axis=1, tiled=True)
        other = place.other_shard(pair)
        big = jnp.concatenate([pair[0], pair[1], other[0], other[1]], axis=1)
        out_own = lax.all_gather(out_weight[layer], "dp", axis=1, tiled=True)
        halves = out_own.reshape(2, out_own.shape[0] // 2, out_own.shape[1])
        out_cols = jnp.concatenate([out_own, *place.other_shard(halves)], axis=0)
        small_cols = jnp.concatenate([state_cols[layer]] + [step_cols[layer]] * copies, axis=1)
        weights.append((big, small_cols, out_cols, gains[layer]))
        wide_skip = jnp.repeat(per_head[layer, 2], width)[None]
        blank = jnp.zeros((1, channels), F32)
        chan = jnp.concatenate([per_channel[layer, :5], wide_skip, per_channel[layer, 5:6], blank], axis=0)
        taps = jnp.concatenate([state_taps[layer], jnp.zeros((3, shared), F32)], axis=0)
        head = jnp.stack([per_head[layer, 0], -jnp.exp(per_head[layer, 1])])
        head = jnp.concatenate([jnp.tile(head, (1, copies)), jnp.zeros((6, 128), F32)], axis=0)
        tables.append((chan, taps, head, expand, tri))

    kept = []
    for layer in range(layers):
        stream, saved = block_forward(place, stream, weights[layer], tables[layer], heads, inner)
        kept.append(saved)
    mixed_out = place.give_sequence(stream)

    grad = lax.dynamic_slice_in_dim(last_up, place.group * stream.shape[0], stream.shape[0], 0).astype(F32)
    grads = [None] * layers
    for layer in reversed(range(layers)):
        grad, grads[layer] = block_backward(
            place,
            grad,
            last_up if layer == layers - 1 else None,
            weights[layer],
            tables[layer],
            heads,
            inner,
            kept[layer],
        )
    grad_hidden = place.give_sequence(grad.astype(BF16)).astype(F32)

    big_grads, out_grads, thin_grads, channel_grads, taps_grads = [], [], [], [], []
    for layer in range(layers):
        grad_own, grad_other, grad_small, grad_out, grad_gain, gchan, gtaps, ghead = grads[layer]
        folded = place.fold_other(grad_own, grad_other)
        big_grads.append(lax.psum_scatter(folded, "dp", scatter_dimension=1, tiled=True).astype(F32))
        quarters = grad_out.reshape(2, 2, own_cols // 2, grad_out.shape[1])
        folded = place.fold_other(quarters[0], quarters[1]).reshape(own_cols, -1)
        out_grads.append(lax.psum_scatter(folded, "dp", scatter_dimension=1, tiled=True).astype(F32))
        step_own = grad_small[:, shared : shared + own_heads]
        step_own = step_own + place.to_pair(grad_small[:, shared + own_heads : shared + heads])
        thin_grads.append(jnp.concatenate([grad_small[:, :shared], step_own, grad_gain[:, None]], axis=1).astype(BF16))
        skips = gchan[5].reshape(heads, width).sum(axis=1)
        per_channel_grad = jnp.concatenate([gchan[:5], gchan[6:7]], axis=0)
        per_head_grad = jnp.stack([ghead[0, :heads], ghead[1, :heads], skips])

        def half_of(at):
            return jnp.concatenate(
                [
                    per_channel_grad[:, at * own_cols : (at + 1) * own_cols].reshape(-1),
                    per_head_grad[:, at * own_heads : (at + 1) * own_heads].reshape(-1),
                ]
            )

        channel_grads.append(half_of(0) + place.to_pair(half_of(1)))
        taps_grads.append(gtaps[:5])

    thin_total = lax.psum_scatter(jnp.stack(thin_grads), "dp", scatter_dimension=1, tiled=True)
    step_total = thin_total[:, :, shared : shared + own_heads].astype(F32)
    joint = jnp.concatenate([thin_total[:, :, :shared], thin_total[:, :, -1:]], axis=2)
    joint = lax.psum(joint, "tensor").astype(F32)
    channel_total = lax.psum(jnp.stack(channel_grads), "dp")
    taps_total = lax.psum(jnp.stack(taps_grads), ("dp", "tensor"))
    channel_part = channel_total[:, :split_at].reshape(layers, 6, own_cols)
    head_part = channel_total[:, split_at:].reshape(layers, 3, own_heads)
    return (
        mixed_out,
        grad_hidden,
        joint[:, :, shared],
        jnp.stack(big_grads),
        joint[:, :, :shared],
        step_total,
        channel_part[:, :5],
        taps_total,
        head_part[:, 0],
        head_part[:, 1],
        head_part[:, 2],
        channel_part[:, 5],
        jnp.stack(out_grads),
    )


def solution(mesh):
    placed = (
        P("dp", "tensor", None),
        P("dp", "tensor", None),
        P(None, "dp"),
        P(None, None, "dp", "tensor"),
        P(None, "dp", None),
        P(None, "dp", "tensor"),
        P(None, None, "tensor"),
        P(),
        P(None, "tensor"),
        P(None, "tensor"),
        P(None, "tensor"),
        P(None, "tensor"),
        P(None, "tensor", "dp"),
    )
    return jax.shard_map(
        local,
        mesh=mesh,
        in_specs=placed,
        out_specs=(
            P("dp", "tensor", None),
            P("dp", "tensor", None),
            P(None, "dp"),
            P(None, None, "dp", "tensor"),
            P(None, "dp", None),
            P(None, "dp", "tensor"),
            P(None, None, "tensor"),
            P(),
            P(None, "tensor"),
            P(None, "tensor"),
            P(None, "tensor"),
            P(None, "tensor"),
            P(None, "tensor", "dp"),
        ),
        check_vma=False,
    )
```

```python
import functools

import jax
import jax.numpy as jnp
from jax import lax
from jax.experimental import pallas as pl
from jax.experimental.pallas import tpu as pltpu
from jax.sharding import PartitionSpec as P

EPSILON = 1e-05
CHUNK = 128
PIECES = 2
GROUP_LANES = 256
LOG2E = 1.4426950408889634
F32 = jnp.float32
BF16 = jnp.bfloat16
NN = (((1,), (0,)), ((), ()))
NT = (((1,), (1,)), ((), ()))
TN = (((0,), (0,)), ((), ()))


def mm(a, b, dims=NN):
    return lax.dot_general(a, b, dims, preferred_element_type=F32)


def sigmoid(v):
    return 0.5 * jnp.tanh(0.5 * v) + 0.5


def softplus(v):
    return jnp.maximum(v, 0.0) + jnp.log(1.0 + jnp.exp(-jnp.abs(v)))


def split3(v):
    high = v.astype(BF16)
    rest = v - high.astype(F32)
    mid = rest.astype(BF16)
    return high, mid, (rest - mid.astype(F32)).astype(BF16)


def spread(v, expand, heads):
    high = v.astype(BF16)
    low = (v - high.astype(F32)).astype(BF16)
    lane = lax.broadcasted_iota(jnp.int32, v.shape, 1)
    parts = jnp.where(lane < heads, high, jnp.where(lane < 2 * heads, low, jnp.zeros_like(low)))
    return mm(parts, expand)


def conv_rows(window, table, length):
    total = table[4:5] + table[3:4] * window[8 : 8 + length]
    for back in range(1, 4):
        total = total + table[3 - back : 4 - back] * pltpu.roll(window, back, 0)[8 : 8 + length]
    return total


def causal(length, flip):
    row = lax.broadcasted_iota(jnp.int32, (length, length), 0)
    col = lax.broadcasted_iota(jnp.int32, (length, length), 1)
    return (row <= col) if flip else (row >= col)


def head_masks(lanes, width):
    lane = lax.broadcasted_iota(jnp.int32, (1, lanes), 1)
    return [(lane >= j * width) & (lane < (j + 1) * width) for j in range(lanes // width)]


def forward_kernel(first, heads, half_no, *refs):
    columns_ref, small_ref, chan_ref, taps_ref, head_ref, expand_ref, tri_ref = refs[:7]
    refs = refs[7:]
    if not first:
        start_ref, tail_ref, stail_ref = refs[:3]
        refs = refs[3:]
    mixed_ref, square_ref, y_ref, saved_ref, state, xbuf, sbuf = refs[-7:]
    length, channels = y_ref.shape
    width = channels // heads
    shared = taps_ref.shape[1]
    half = shared // 2
    step_lanes = slice(half_no * (half + 128) + half, (half_no + 1) * (half + 128))

    def shared_of(ref):
        return jnp.concatenate([ref[:, :half], ref[:, half + 128 : shared + 128]], axis=1)

    @pl.when(pl.program_id(0) == 0)
    def _():
        if first:
            state[...] = jnp.zeros_like(state)
            xbuf[0:8] = jnp.zeros((8, channels), F32)
            sbuf[0:8] = jnp.zeros((8, shared), F32)
        else:
            state[...] = start_ref[...]
            xbuf[0:8] = tail_ref[:, channels:].astype(F32)[-8:]
            sbuf[0:8] = shared_of(stail_ref)

    sbuf[8:] = shared_of(small_ref)
    tri = tri_ref[...]
    expand = expand_ref[...]
    head = head_ref[8 * half_no : 8 * half_no + 8]
    dt = softplus(small_ref[:, step_lanes] + head[0:1])
    running = sum(mm(tri, piece) for piece in split3(dt * (head[1:2] * LOG2E)))
    running_t = running.T
    decay_in = jnp.exp2(running)
    decay_out = jnp.exp2(running[length - 1 :] - running)
    dt_wide = spread(dt, expand, heads)
    in_wide = spread(decay_in, expand, heads)
    out_wide = spread(dt * decay_out, expand, heads)

    taps = taps_ref[...]
    bc = conv_rows(sbuf[...], taps, length)
    bc = (bc * sigmoid(bc)).astype(BF16)
    keys, queries = bc[:, :half], bc[:, half:]
    scores = jnp.where(causal(length, False), mm(queries, keys, NT), 0.0)
    squares = jnp.zeros((length, 128), F32)
    masks = head_masks(GROUP_LANES, width)
    for start in range(0, channels, GROUP_LANES):
        lanes = slice(start, start + GROUP_LANES)
        conv_at = slice(channels + start, channels + start + GROUP_LANES)
        table = chan_ref[:, half_no * channels + start : half_no * channels + start + GROUP_LANES]
        xbuf[8:, lanes] = columns_ref[:, conv_at].astype(F32)
        c = conv_rows(xbuf[:, lanes], table, length)
        xbuf[0:8, lanes] = xbuf[length:, lanes]
        xs = c * sigmoid(c)
        values = (xs * dt_wide[:, lanes]).astype(BF16)
        weights, parts = [], []
        for j in range(GROUP_LANES // width):
            h = start // width + j
            gap = jnp.minimum(running[:, h : h + 1] - running_t[h : h + 1, :], 0.0)
            weights.append((scores * jnp.exp2(gap)).astype(BF16))
            parts.append(jnp.where(masks[j], values, jnp.zeros_like(values)))
        before = state[:, lanes]
        before_low = before.astype(BF16)
        saved_ref[0, :, lanes] = before_low
        y = mm(jnp.concatenate(weights, axis=1), jnp.concatenate(parts, axis=0))
        y = y + mm(queries, before_low) * in_wide[:, lanes]
        y_ref[:, lanes] = y
        z = columns_ref[:, lanes].astype(F32)
        gated = (y + table[5:6] * xs) * (z * sigmoid(z))
        mixed_ref[:, lanes] = (gated * table[6:7]).astype(BF16)
        power = gated * gated
        for at in range(0, GROUP_LANES, 128):
            squares = squares + power[:, at : at + 128]
        fresh = mm(keys, (xs * out_wide[:, lanes]).astype(BF16), TN)
        state[:, lanes] = before * in_wide[length - 1 :, lanes] + fresh
    square_ref[...] = jnp.sum(squares, axis=1, keepdims=True)
    sbuf[0:8] = sbuf[length:]


def backward_kernel(first, last, heads, *refs):
    columns_refs, small_ref, y_refs, saved_refs, up_refs = refs[:2], refs[2], refs[3:5], refs[5:7], refs[7:9]
    pull_ref, chan_ref, taps_ref, head_ref, expand_ref, tri_ref, halo0, halo1, shalo_ref, early0, early1, searly_ref = refs[9:21]
    halo_refs, early_refs = (halo0, halo1), (early0, early1)
    refs = refs[21:]
    if not last:
        carried_refs = refs[:6]
    dcolumns_ref, dstate, dtail_ref, dstail_ref, gchan_ref, gtaps_ref, ghead_ref, xbuf, sbuf, dxbuf, dsbuf = refs[-11:]
    length, channels = y_refs[0].shape
    width = channels // heads
    shared = taps_ref.shape[1]
    half = shared // 2
    step_no = pl.program_id(0)
    first_block = step_no == pl.num_programs(0) - 1

    @pl.when(step_no == 0)
    def _():
        if last:
            dstate[...] = jnp.zeros_like(dstate)
            dxbuf[length:] = jnp.zeros((8, 2 * channels), F32)
            dsbuf[length:] = jnp.zeros((8, shared), F32)
            gchan_ref[...] = jnp.zeros_like(gchan_ref)
            gtaps_ref[...] = jnp.zeros_like(gtaps_ref)
            ghead_ref[...] = jnp.zeros_like(ghead_ref)
        else:
            dstate[...] = carried_refs[0][...]
            dxbuf[length:] = carried_refs[1][...]
            dsbuf[length:] = carried_refs[2][...]
            gchan_ref[...] = carried_refs[3][...]
            gtaps_ref[...] = carried_refs[4][...]
            ghead_ref[...] = carried_refs[5][...]

    def outside(rows):
        return jnp.zeros_like(rows) if first else rows

    def shared_of(ref):
        return jnp.concatenate([ref[:, :half], ref[:, half + 128 : shared + 128]], axis=1)

    sbuf[8:] = shared_of(small_ref)
    sbuf[0:8] = jnp.where(first_block, outside(shared_of(searly_ref)), shared_of(shalo_ref))
    tri = tri_ref[...]
    expand = expand_ref[...]
    taps = taps_ref[...]
    bc_in = conv_rows(sbuf[...], taps, length)
    bc_sig = sigmoid(bc_in)
    bc = (bc_in * bc_sig).astype(BF16)
    keys, queries = bc[:, :half], bc[:, half:]
    keep = causal(length, True)
    scores = jnp.where(keep, mm(keys, queries, NT), 0.0)
    pull = pull_ref[...]
    masks = head_masks(GROUP_LANES, width)
    dscores = jnp.zeros((length, length), F32)
    dkeys = jnp.zeros((length, half), F32)
    dqueries = jnp.zeros((length, half), F32)
    last_row = lax.broadcasted_iota(jnp.int32, (length, 1), 0) == length - 1
    lane = lax.broadcasted_iota(jnp.int32, (length, 128), 1)
    per_group = GROUP_LANES // width
    for half_no in range(2):
        columns_ref, halo_ref, early_ref = columns_refs[half_no], halo_refs[half_no], early_refs[half_no]
        y_ref, saved_ref, up_ref = y_refs[half_no], saved_refs[half_no], up_refs[half_no]
        step_lanes = slice(half_no * (half + 128) + half, (half_no + 1) * (half + 128))
        head = head_ref[8 * half_no : 8 * half_no + 8]
        step = small_ref[:, step_lanes] + head[0:1]
        dt = softplus(step)
        rate = dt * head[1:2]
        running = sum(mm(tri, piece) for piece in split3(rate * LOG2E))
        running_t = running.T
        decay_in = jnp.exp2(running)
        decay_out = jnp.exp2(running[length - 1 :] - running)
        dt_wide = spread(dt, expand, heads)
        in_wide = spread(decay_in, expand, heads)
        out_wide = spread(decay_out, expand, heads)
        drun = jnp.zeros((length, 128), F32)
        ddt = jnp.zeros((length, 128), F32)
        for start in range(0, channels, GROUP_LANES):
            lanes = slice(start, start + GROUP_LANES)
            conv_at = slice(channels + start, channels + start + GROUP_LANES)
            at = half_no * channels + start
            wide = slice(at, at + GROUP_LANES)
            table = chan_ref[:, wide]
            xbuf[8:, lanes] = columns_ref[:, conv_at].astype(F32)
            xbuf[0:8, lanes] = jnp.where(first_block, outside(early_ref[:, conv_at].astype(F32)[-8:]), halo_ref[:, conv_at].astype(F32)[-8:])
            c = conv_rows(xbuf[:, lanes], table, length)
            c_sig = sigmoid(c)
            xs = c * c_sig
            z = columns_ref[:, lanes].astype(F32)
            z_sig = sigmoid(z)
            z_silu = z * z_sig
            y = y_ref[:, lanes]
            total = y + table[5:6] * xs
            gated = total * z_silu
            up = up_ref[:, lanes].astype(F32)
            gchan_ref[6:7, wide] += jnp.sum(up * gated, axis=0, keepdims=True)
            dgated = table[6:7] * up - gated * pull
            out_at = half_no * (2 * channels + half + 128) + start
            dcolumns_ref[:, out_at : out_at + GROUP_LANES] = (
                dgated * total * (z_sig + z_silu * (1.0 - z_sig))
            ).astype(BF16)
            dy = dgated * z_silu
            gchan_ref[5:6, wide] += jnp.sum(dy * xs, axis=0, keepdims=True)
            dy_low = dy.astype(BF16)
            dt_lanes = dt_wide[:, lanes]
            values = (xs * dt_lanes).astype(BF16)
            weights, dparts, vparts, decays = [], [], [], []
            for j in range(per_group):
                h = start // width + j
                decay = jnp.exp2(jnp.minimum(running_t[h : h + 1, :] - running[:, h : h + 1], 0.0))
                decays.append(decay)
                weights.append((scores * decay).astype(BF16))
                dparts.append(jnp.where(masks[j], dy_low, jnp.zeros_like(dy_low)))
                vparts.append(jnp.where(masks[j], values, jnp.zeros_like(values)))
            outer = mm(jnp.concatenate(vparts, axis=0), dy_low, NT)
            for j in range(per_group):
                dscores = dscores + outer[j * length : (j + 1) * length] * decays[j]
            dvalues = mm(jnp.concatenate(weights, axis=1), jnp.concatenate(dparts, axis=0))
            before = saved_ref[0, :, lanes]
            dafter = dstate[:, wide]
            dafter_low = dafter.astype(BF16)
            out_lanes = out_wide[:, lanes]
            carried = mm(keys, dafter_low) * out_lanes
            dvalues = dvalues + carried
            values_f = values.astype(F32)
            dkeys = dkeys + mm((values_f * out_lanes).astype(BF16), dafter_low, NT)
            in_lanes = in_wide[:, lanes]
            dy_in = (dy * in_lanes).astype(BF16)
            dqueries = dqueries + mm(dy_in, before, NT)
            end_decay = in_lanes[length - 1 :]
            at_end = jnp.sum(values_f * carried, axis=0, keepdims=True) + end_decay * jnp.sum(
                before.astype(F32) * dafter, axis=0, keepdims=True
            )
            dstate[:, wide] = end_decay * dafter + mm(queries, dy_in, TN)
            turn = dy_low.astype(F32) * y - values_f * dvalues + jnp.where(last_row, at_end, 0.0)
            turn_high = turn.astype(BF16)
            turn_low = (turn - turn_high.astype(F32)).astype(BF16)
            group_expand = expand[:, lanes]
            drun = drun + mm(turn_high, group_expand, NT) + mm(turn_low, group_expand, NT)
            ddt = ddt + mm((dvalues * xs).astype(BF16), group_expand, NT)
            dxs = dvalues * dt_lanes + table[5:6] * dy
            dc = dxs * (c_sig + xs * (1.0 - c_sig))
            dxbuf[0:length, wide] = dc
            window = dxbuf[:, wide]
            here = xbuf[8:, lanes]
            gchan_ref[4:5, wide] += jnp.sum(dc, axis=0, keepdims=True)
            gchan_ref[3:4, wide] += jnp.sum(dc * here, axis=0, keepdims=True)
            dconv = table[3:4] * dc
            for ahead in range(1, 4):
                moved = pltpu.roll(window, length + 8 - ahead, 0)[:length]
                gchan_ref[3 - ahead : 4 - ahead, wide] += jnp.sum(moved * here, axis=0, keepdims=True)
                dconv = dconv + table[3 - ahead : 4 - ahead] * moved
            out_at = out_at + channels
            dcolumns_ref[:, out_at : out_at + GROUP_LANES] = dconv.astype(BF16)
            dxbuf[length:, wide] = dxbuf[0:8, wide]

        drate = sum(mm(tri, piece, TN) for piece in split3(drun))
        dstep = (ddt + drate * head[1:2]) * sigmoid(step)
        ghead_ref[8 * half_no : 8 * half_no + 1] += jnp.sum(dstep, axis=0, keepdims=True)
        ghead_ref[8 * half_no + 1 : 8 * half_no + 2] += jnp.sum(drate * rate, axis=0, keepdims=True)
        out_at = half_no * (2 * channels + half + 128) + 2 * channels + half
        dcolumns_ref[:, out_at : out_at + 128] = jnp.where(lane < heads, dstep, 0.0).astype(BF16)

    dscores_low = jnp.where(keep, dscores, 0.0).astype(BF16)
    dkeys = dkeys + mm(dscores_low, queries)
    dqueries = dqueries + mm(dscores_low, keys, TN)
    dbc = jnp.concatenate([dkeys, dqueries], axis=1) * (bc_sig + bc_in * bc_sig * (1.0 - bc_sig))
    dsbuf[0:length] = dbc
    window = dsbuf[...]
    here = sbuf[8:]
    gtaps_ref[4:5] += jnp.sum(dbc, axis=0, keepdims=True)
    gtaps_ref[3:4] += jnp.sum(dbc * here, axis=0, keepdims=True)
    dshared = taps[3:4] * dbc
    for ahead in range(1, 4):
        moved = pltpu.roll(window, length + 8 - ahead, 0)[:length]
        gtaps_ref[3 - ahead : 4 - ahead] += jnp.sum(moved * here, axis=0, keepdims=True)
        dshared = dshared + taps[3 - ahead : 4 - ahead] * moved
    for half_no in range(2):
        out_at = half_no * (2 * channels + half + 128) + 2 * channels
        dcolumns_ref[:, out_at : out_at + half] = dshared[:, half_no * half : (half_no + 1) * half].astype(BF16)
    dsbuf[length:] = dsbuf[0:8]
    dtail_ref[...] = dxbuf[0:8]
    dstail_ref[...] = dsbuf[0:8]


def scan_tables(heads, channels):
    row = lax.broadcasted_iota(jnp.int32, (128, channels), 0) % heads
    col = lax.broadcasted_iota(jnp.int32, (128, channels), 1) // (channels // heads)
    return (row == col).astype(BF16), jnp.tril(jnp.ones((CHUNK, CHUNK), BF16))


def whole(array):
    return pl.BlockSpec(array.shape, lambda i: (0,) * array.ndim)


def last_rows(array, count):
    at = array.shape[0] // count - 1
    return pl.BlockSpec((count,) + array.shape[1:], lambda i: (at, 0))


def unread(arrays):
    return [pl.BlockSpec(memory_space=pl.ANY) for _ in arrays]


def mixer_forward(columns, small, tables, heads, half_no, earlier=None, after=()):
    tokens, channels = columns.shape[0], columns.shape[1] // 2
    shared = tables[1].shape[1]
    blocks = tokens // CHUNK

    def rows(cols):
        return pl.BlockSpec((CHUNK, cols), lambda i: (i, 0))

    operands = [columns, small, *tables]
    specs = [rows(2 * channels), rows(small.shape[1])] + [whole(table) for table in tables]
    if earlier is not None:
        operands += list(earlier)
        specs += [whole(earlier[0]), last_rows(earlier[1], 16), last_rows(earlier[2], 8)]
    operands += list(after)
    specs += unread(after)
    return pl.pallas_call(
        functools.partial(forward_kernel, earlier is None, heads, half_no),
        grid=(blocks,),
        in_specs=specs,
        out_specs=[
            rows(channels),
            rows(1),
            rows(channels),
            pl.BlockSpec((1, shared // 2, channels), lambda i: (i, 0, 0)),
            pl.BlockSpec((shared // 2, channels), lambda i: (0, 0)),
        ],
        out_shape=[
            jax.ShapeDtypeStruct((tokens, channels), BF16),
            jax.ShapeDtypeStruct((tokens, 1), F32),
            jax.ShapeDtypeStruct((tokens, channels), F32),
            jax.ShapeDtypeStruct((blocks, shared // 2, channels), BF16),
            jax.ShapeDtypeStruct((shared // 2, channels), F32),
        ],
        scratch_shapes=[
            pltpu.VMEM((CHUNK + 8, channels), F32),
            pltpu.VMEM((CHUNK + 8, shared), F32),
        ],
        compiler_params=pltpu.CompilerParams(vmem_limit_bytes=48 * 1024 * 1024),
        cost_estimate=pl.CostEstimate(
            flops=tokens * channels * 6000, bytes_accessed=tokens * channels * 14, transcendentals=tokens * channels * 6
        ),
        name="mixer_forward",
    )(*operands)


def mixer_backward(columns, small, y, saved, up, pull, tables, heads, early, carried, after=()):
    tokens, channels = y[0].shape
    shared = tables[1].shape[1]
    blocks = tokens // CHUNK
    small_width = small.shape[1]

    def rows(cols):
        return pl.BlockSpec((CHUNK, cols), lambda i: (blocks - 1 - i, 0))

    def halo(count, cols):
        per_block = CHUNK // count
        return pl.BlockSpec((count, cols), lambda i: (jnp.maximum((blocks - 1 - i) * per_block - 1, 0), 0))

    def fixed(r, c):
        return pl.BlockSpec((r, c), lambda i: (0, 0))

    saved_spec = pl.BlockSpec((1, shared // 2, channels), lambda i: (blocks - 1 - i, 0, 0))
    before = (columns[0], columns[1], small) if early is None else early
    operands = [*columns, small, *y, *saved, *up, pull, *tables, *columns, small, *before]
    specs = [rows(2 * channels)] * 2 + [rows(small_width)] + [rows(channels)] * 2 + [saved_spec] * 2 + [rows(channels)] * 2
    specs += [rows(1)] + [whole(table) for table in tables]
    specs += [halo(16, 2 * channels)] * 2 + [halo(8, small_width)]
    specs += [last_rows(before[0], 16), last_rows(before[1], 16), last_rows(before[2], 8)]
    if carried is not None:
        operands += list(carried)
        specs += [whole(array) for array in carried]
    operands += list(after)
    specs += unread(after)
    fixed_shapes = [(shared // 2, 2 * channels), (8, 2 * channels), (8, shared), (8, 2 * channels), (8, shared), (16, 128)]
    return pl.pallas_call(
        functools.partial(backward_kernel, early is None, carried is None, heads),
        grid=(blocks,),
        in_specs=specs,
        out_specs=[rows(4 * channels + shared + 256)] + [fixed(*shape) for shape in fixed_shapes],
        out_shape=[
            jax.ShapeDtypeStruct((tokens, 4 * channels + shared + 256), BF16),
        ]
        + [jax.ShapeDtypeStruct(shape, F32) for shape in fixed_shapes],
        scratch_shapes=[
            pltpu.VMEM((CHUNK + 8, channels), F32),
            pltpu.VMEM((CHUNK + 8, shared), F32),
            pltpu.VMEM((CHUNK + 8, 2 * channels), F32),
            pltpu.VMEM((CHUNK + 8, shared), F32),
        ],
        compiler_params=pltpu.CompilerParams(vmem_limit_bytes=56 * 1024 * 1024),
        cost_estimate=pl.CostEstimate(
            flops=tokens * channels * 28000, bytes_accessed=tokens * channels * 40, transcendentals=tokens * channels * 12
        ),
        name="mixer_backward",
    )(*operands)


class Place:
    def __init__(self):
        self.members = lax.axis_size("tensor")
        self.groups = self.members // 2
        self.sequence = lax.axis_index("tensor") % 2
        self.group = lax.axis_index("tensor") // 2
        copies = lax.axis_size("dp")
        self.owners = [
            [d * self.members + 2 * g + s for s in range(2) for d in range(copies)] for g in range(self.groups)
        ]

    def to_pair(self, v):
        return lax.ppermute(v, "tensor", [(t, t ^ 1) for t in range(self.members)])

    def to_group(self, v, hop):
        return lax.ppermute(v, "tensor", [(t, (t + 2 * hop) % self.members) for t in range(self.members)])

    def gather_owners(self, v):
        return lax.all_gather(v, ("dp", "tensor"), axis=0, axis_index_groups=self.owners, tiled=True)

    def scatter_owners(self, v):
        return lax.psum_scatter(v, ("dp", "tensor"), scatter_dimension=0, axis_index_groups=self.owners, tiled=True)

    def add_groups(self, v):
        return v + sum(self.to_group(v, hop) for hop in range(1, self.groups))

    def sum_groups(self, v):
        return v.astype(F32) + sum(self.to_group(v, hop).astype(F32) for hop in range(1, self.groups))

    def both(self, v, axis):
        other = self.to_pair(v)
        return jnp.where(
            self.sequence == 0, jnp.concatenate([v, other], axis=axis), jnp.concatenate([other, v], axis=axis)
        )

    def rows_of(self, chunks, hop):
        at = (self.group + hop) % self.groups
        if len(chunks) == self.groups == 2:
            return jnp.where(at == 0, chunks[0], chunks[1])
        total = jnp.concatenate(chunks)
        count = total.shape[0] // self.groups
        return lax.dynamic_slice_in_dim(total, at * count, count, 0)

    def gather_chunks(self, v, chunks):
        if chunks == self.groups == 2:
            other = self.to_group(v, 1)
            return [jnp.where(self.group == at, v, other) for at in range(2)]
        count = v.shape[0]
        total = jnp.zeros((count * self.groups,) + v.shape[1:], v.dtype)
        total = lax.dynamic_update_slice_in_dim(total, v, self.group * count, 0)
        for hop in range(1, self.groups):
            start = (self.group - hop) % self.groups * count
            total = lax.dynamic_update_slice_in_dim(total, self.to_group(v, hop), start, 0)
        return jnp.split(total, chunks)

    def scatter_rows(self, chunks):
        arrived = [self.to_group(self.rows_of(chunks, hop), hop) for hop in range(1, self.groups)]
        return self.rows_of(chunks, 0).astype(F32) + sum(piece.astype(F32) for piece in arrived)

    def take_sequence(self, v):
        mine = jnp.where(self.sequence == 0, v[0], v[1])
        other = self.to_pair(jnp.where(self.sequence == 0, v[1], v[0]))
        return jnp.where(self.sequence == 0, jnp.concatenate([mine, other]), jnp.concatenate([other, mine]))

    def give_sequence(self, v):
        first, second = jnp.split(v, 2)
        mine = jnp.where(self.sequence == 0, first, second)
        other = self.to_pair(jnp.where(self.sequence == 0, second, first))
        return jnp.where(self.sequence == 0, jnp.stack([mine, other]), jnp.stack([other, mine]))


def norm_scale(stream):
    return lax.rsqrt(jnp.mean(stream * stream, axis=-1, keepdims=True) + EPSILON)


def block_forward(place, streams, weights, tables, heads, inner, final):
    in_cols, small_cols, out_rows, gain = weights
    main = small_cols[0].shape[1]
    kept = {"stream": streams, "columns": [], "y": [], "saved": [], "mixed": [], "scale": [], "update": []}
    normed = [(stream * norm_scale(stream) * gain).astype(BF16) for stream in streams]
    small = [mm(part, jnp.concatenate(small_cols, axis=1)) for part in normed]
    halves = []
    for half_no, cols in enumerate(in_cols):
        results, earlier = [], None
        for at, part in enumerate(normed):
            columns = mm(part, cols[:, :-main]).astype(BF16)
            mixed, square, y, saved, state = mixer_forward(columns, small[at], tables, heads, half_no, earlier)
            earlier = (state, columns, small[at])
            results.append((columns, mixed, square, y, saved))
        halves.append(results)
    shares, scales = [], []
    for at in range(len(streams)):
        first, second = halves[0][at], halves[1][at]
        shares.append((mm(first[1], out_rows[0], NT) + mm(second[1], out_rows[1], NT)).astype(BF16))
        scales.append(lax.rsqrt(place.add_groups(first[2] + second[2]) / inner + EPSILON))
        for key, position in (("columns", 0), ("mixed", 1), ("y", 3), ("saved", 4)):
            kept[key].append((first[position], second[position]))
    kept.update(normed=normed, small=small, scale=scales)
    if final:
        after = place.rows_of(streams, 0) + place.scatter_rows(shares) * place.rows_of(scales, 0)
    else:
        kept["update"] = [place.sum_groups(share) for share in shares]
        after = [stream + update * scale for stream, update, scale in zip(streams, kept["update"], scales)]
    return after, kept


def block_backward(place, grads, weights, tables, heads, inner, kept, final, first, after):
    in_cols, small_cols, out_rows, gain = weights
    chunks = len(grads)
    scales = kept["scale"]
    ups = [(grad * scale).astype(BF16) for grad, scale in zip(grads, scales)]
    grad_mixed = [[mm(up, rows) for rows in out_rows] for up in ups]
    if final:
        pulls = [
            sum(jnp.sum(g * m.astype(F32), axis=-1, keepdims=True) for g, m in zip(*pairs))
            for pairs in zip(grad_mixed, kept["mixed"])
        ]
        pulls = [place.add_groups(pull) for pull in pulls]
    else:
        pulls = [jnp.sum(up.astype(F32) * u, axis=-1, keepdims=True) for up, u in zip(ups, kept["update"])]
    pulls = [pull * (scale * scale / inner) for pull, scale in zip(pulls, scales)]
    up = jnp.concatenate(ups)
    mixed = [jnp.concatenate([part[half_no] for part in kept["mixed"]]) for half_no in range(2)]
    grad_out = jnp.concatenate([mm(up, part, TN).astype(BF16) for part in mixed])
    out_owned = place.scatter_owners(grad_out)

    dcolumns, shares = [None] * chunks, [None] * chunks
    carried = None
    for at in reversed(range(chunks)):
        early = (*kept["columns"][at - 1], kept["small"][at - 1]) if at else None
        result = mixer_backward(
            kept["columns"][at],
            kept["small"][at],
            kept["y"][at],
            kept["saved"][at],
            grad_mixed[at],
            pulls[at],
            tables,
            heads,
            early,
            carried,
            after[at],
        )
        dcolumns[at], carried = jnp.split(result[0], 2, axis=1), result[1:]
        shares[at] = sum(mm(part, cols, NT) for part, cols in zip(dcolumns[at], in_cols)).astype(BF16)
    normed = jnp.concatenate(kept["normed"])
    joined = [jnp.concatenate([part[half_no] for part in dcolumns]) for half_no in range(2)]
    grad_in = jnp.concatenate([mm(normed, part, TN).astype(BF16) for part in joined])
    in_owned = place.scatter_owners(grad_in)

    streams = kept["stream"]
    if first:
        streams, grads = [place.rows_of(streams, 0)], [place.rows_of(grads, 0)]
        sums = [place.scatter_rows(shares)]
    else:
        sums = [place.sum_groups(share) for share in shares]
    grad_gain, results = 0.0, []
    for stream, grad, grad_normed in zip(streams, grads, sums):
        row_scale = norm_scale(stream)
        unit = stream * row_scale
        grad_gain = grad_gain + jnp.sum(grad_normed * unit, axis=0)
        lifted = grad_normed * gain
        results.append(grad + row_scale * (lifted - unit * jnp.mean(lifted * unit, axis=-1, keepdims=True)))
    if not first:
        grad_gain = jnp.where(place.group == 0, grad_gain, 0.0)
    return results, (in_owned, out_owned, grad_gain, carried[3:], grad_in)


def local(
    hidden,
    cotangent,
    norm_gain,
    in_weights,
    state_weight,
    step_weight,
    channel_taps,
    state_taps,
    step_bias,
    decay_log,
    skip_gain,
    inner_gain,
    out_weight,
):
    place = Place()
    layers = in_weights.shape[0]
    rows = in_weights.shape[2]
    heads = step_bias.shape[1]
    own_cols = in_weights.shape[3]
    width = own_cols // heads
    inner = own_cols * place.members
    shared = state_weight.shape[2]
    half = shared // 2
    copies = 128 // heads
    main = 2 * own_cols
    expand, tri = scan_tables(heads, own_cols)

    weights = []
    for layer in range(layers):
        state_half = lax.dynamic_slice_in_dim(state_weight[layer], place.sequence * half, half, 1)
        thin = [step_weight[layer]] * 2
        blank = jnp.zeros((rows, 127 - 2 * heads), BF16)
        block = [in_weights[layer, 0], in_weights[layer, 1], state_half, *thin, blank, norm_gain[layer][:, None]]
        block = jnp.concatenate(block + [out_weight[layer].T], axis=1)
        both = place.gather_owners(block)
        shards = jnp.split(both, 2)
        thin_end = main + half + 128
        in_cols = [shard[:, :thin_end] for shard in shards]
        small_cols = [shard[:, main:thin_end] for shard in shards]
        out_rows = [shard[:, thin_end:] for shard in shards]
        gain = shards[0][:, thin_end - 1].astype(F32)
        weights.append((in_cols, small_cols, out_rows, gain))

    streams = place.gather_chunks(place.take_sequence(hidden), PIECES)
    streams = [stream.astype(F32) for stream in streams]
    per_channel = place.both(jnp.concatenate([channel_taps, inner_gain[:, None]], axis=1), 2)
    per_head = jnp.stack([step_bias, decay_log, skip_gain], axis=1)
    per_head = place.both(per_head[:, None], 1)
    tables = []
    for layer in range(layers):
        wide_skip = jnp.repeat(per_head[layer, :, 2].reshape(-1), width)[None]
        blank = jnp.zeros((1, main), F32)
        chan = jnp.concatenate([per_channel[layer, :5], wide_skip, per_channel[layer, 5:6], blank], axis=0)
        taps = jnp.concatenate([state_taps[layer], jnp.zeros((3, shared), F32)], axis=0)
        head = []
        for part in range(2):
            pair = jnp.stack([per_head[layer, part, 0], -jnp.exp(per_head[layer, part, 1])])
            pair = jnp.concatenate([pair, pair, jnp.zeros((2, 128 - 2 * heads), F32)], axis=1)
            head += [pair, jnp.zeros((6, 128), F32)]
        tables.append((chan, taps, jnp.concatenate(head), expand, tri))

    last_up = place.gather_chunks(place.take_sequence(cotangent), PIECES)
    kept = []
    for layer in range(layers):
        streams, saved = block_forward(
            place, streams, weights[layer], tables[layer], heads, inner, layer == layers - 1
        )
        kept.append(saved)
    mixed_out = place.give_sequence(streams)

    grads = [part.astype(F32) for part in last_up]
    taken = [None] * layers
    after = [()] * PIECES
    for layer in reversed(range(layers)):
        grads, taken[layer] = block_backward(
            place,
            grads,
            weights[layer],
            tables[layer],
            heads,
            inner,
            kept[layer],
            layer == layers - 1,
            layer == 0,
            after,
        )
        after = [()] * (PIECES - 1) + [(taken[layer][-1],)]
    grad_hidden = place.give_sequence(grads[0].astype(BF16)).astype(F32)

    slots, sizes = [], []
    for layer in range(layers):
        gchan, gtaps, ghead = taken[layer][3]
        skips = gchan[5].reshape(2, heads, width).sum(axis=2)
        mine = jnp.stack([ghead[0, :heads], ghead[8, :heads], ghead[1, :heads], ghead[9, :heads], skips[0], skips[1]])
        channels = jnp.concatenate([gchan[:5].reshape(-1), gchan[6], mine.reshape(-1)])
        slot = lax.broadcasted_iota(jnp.int32, (place.groups, 1), 0) == place.group
        slotted = jnp.where(slot, channels[None], 0.0).reshape(-1)
        slots.append(jnp.concatenate([slotted, gtaps[:5].reshape(-1), taken[layer][2]]))
        sizes = [channels.size, gtaps[:5].size]
    totals = [lax.psum(slot, ("dp", "tensor")) for slot in slots]

    outs = []
    for layer in range(layers):
        total = totals[layer]
        count = sizes[0] * place.groups
        channels = lax.dynamic_slice_in_dim(total, place.group * sizes[0], sizes[0], 0)
        taps_part = total[count : count + sizes[1]].reshape(5, shared)
        gain_part = lax.dynamic_slice_in_dim(total, count + sizes[1] + lax.axis_index("dp") * rows, rows, 0)
        per_channel_part = channels[: 6 * main].reshape(6, 2, own_cols)
        per_channel_part = lax.dynamic_index_in_dim(per_channel_part, place.sequence, 1, keepdims=False)
        per_head_part = channels[6 * main :].reshape(3, 2, heads)
        per_head_part = lax.dynamic_index_in_dim(per_head_part, place.sequence, 1, keepdims=False)
        in_owned, out_owned = taken[layer][:2]
        in_owned = in_owned.astype(F32)
        state_part = place.both(place.add_groups(in_owned[:, main : main + half]), 1)
        outs.append(
            (
                gain_part,
                jnp.stack([in_owned[:, :own_cols], in_owned[:, own_cols:main]]),
                state_part,
                in_owned[:, main + half : main + half + heads],
                per_channel_part[:5],
                taps_part,
                per_head_part[0],
                per_head_part[1],
                per_head_part[2],
                per_channel_part[5],
                out_owned.astype(F32).T,
            )
        )
    return (mixed_out, grad_hidden) + tuple(jnp.stack(parts) for parts in zip(*outs))


def solution(mesh):
    placed = (
        P("dp", "tensor", None),
        P("dp", "tensor", None),
        P(None, "dp"),
        P(None, None, "dp", "tensor"),
        P(None, "dp", None),
        P(None, "dp", "tensor"),
        P(None, None, "tensor"),
        P(),
        P(None, "tensor"),
        P(None, "tensor"),
        P(None, "tensor"),
        P(None, "tensor"),
        P(None, "tensor", "dp"),
    )
    return jax.shard_map(
        local,
        mesh=mesh,
        in_specs=placed,
        out_specs=(
            P("dp", "tensor", None),
            P("dp", "tensor", None),
            P(None, "dp"),
            P(None, None, "dp", "tensor"),
            P(None, "dp", None),
            P(None, "dp", "tensor"),
            P(None, None, "tensor"),
            P(),
            P(None, "tensor"),
            P(None, "tensor"),
            P(None, "tensor"),
            P(None, "tensor"),
            P(None, "tensor", "dp"),
        ),
        check_vma=False,
    )
```

```python
import functools

import jax
import jax.numpy as jnp
from jax import lax
from jax.experimental import pallas as pl
from jax.experimental.pallas import tpu as pltpu
from jax.sharding import PartitionSpec as P

EPSILON = 1e-05
CHUNK = 128
PIECES = 2
GROUP_LANES = 256
LOG2E = 1.4426950408889634
F32 = jnp.float32
BF16 = jnp.bfloat16
NN = (((1,), (0,)), ((), ()))
NT = (((1,), (1,)), ((), ()))
MESH = pl.DeviceIdType.MESH
TN = (((0,), (0,)), ((), ()))


def mm(a, b, dims=NN):
    return lax.dot_general(a, b, dims, preferred_element_type=F32)


def sigmoid(v):
    return 0.5 * jnp.tanh(0.5 * v) + 0.5


def softplus(v):
    return jnp.maximum(v, 0.0) + jnp.log(1.0 + jnp.exp(-jnp.abs(v)))


def split3(v):
    high = v.astype(BF16)
    rest = v - high.astype(F32)
    mid = rest.astype(BF16)
    return high, mid, (rest - mid.astype(F32)).astype(BF16)


def spread(v, expand, heads):
    high = v.astype(BF16)
    low = (v - high.astype(F32)).astype(BF16)
    lane = lax.broadcasted_iota(jnp.int32, v.shape, 1)
    parts = jnp.where(lane < heads, high, jnp.where(lane < 2 * heads, low, jnp.zeros_like(low)))
    return mm(parts, expand)


def conv_rows(window, table, length):
    total = table[4:5] + table[3:4] * window[8 : 8 + length]
    for back in range(1, 4):
        total = total + table[3 - back : 4 - back] * pltpu.roll(window, back, 0)[8 : 8 + length]
    return total


def causal(length, flip):
    row = lax.broadcasted_iota(jnp.int32, (length, length), 0)
    col = lax.broadcasted_iota(jnp.int32, (length, length), 1)
    return (row <= col) if flip else (row >= col)


def head_masks(lanes, width):
    lane = lax.broadcasted_iota(jnp.int32, (1, lanes), 1)
    return [(lane >= j * width) & (lane < (j + 1) * width) for j in range(lanes // width)]


def forward_kernel(first, heads, half_no, *refs):
    columns_ref, small_ref, chan_ref, taps_ref, head_ref, expand_ref, tri_ref = refs[:7]
    refs = refs[7:]
    if not first:
        start_ref, tail_ref, stail_ref = refs[:3]
        refs = refs[3:]
    mixed_ref, square_ref, y_ref, saved_ref, state, xbuf, sbuf = refs[-7:]
    length, channels = y_ref.shape
    width = channels // heads
    shared = taps_ref.shape[1]
    half = shared // 2
    step_lanes = slice(half_no * (half + 128) + half, (half_no + 1) * (half + 128))

    def shared_of(ref):
        return jnp.concatenate([ref[:, :half], ref[:, half + 128 : shared + 128]], axis=1)

    @pl.when(pl.program_id(0) == 0)
    def _():
        if first:
            state[...] = jnp.zeros_like(state)
            xbuf[0:8] = jnp.zeros((8, channels), F32)
            sbuf[0:8] = jnp.zeros((8, shared), F32)
        else:
            state[...] = start_ref[...]
            xbuf[0:8] = tail_ref[:, channels:].astype(F32)[-8:]
            sbuf[0:8] = shared_of(stail_ref)

    sbuf[8:] = shared_of(small_ref)
    tri = tri_ref[...]
    expand = expand_ref[...]
    head = head_ref[8 * half_no : 8 * half_no + 8]
    dt = softplus(small_ref[:, step_lanes] + head[0:1])
    running = sum(mm(tri, piece) for piece in split3(dt * (head[1:2] * LOG2E)))
    running_t = running.T
    decay_in = jnp.exp2(running)
    decay_out = jnp.exp2(running[length - 1 :] - running)
    dt_wide = spread(dt, expand, heads)
    in_wide = spread(decay_in, expand, heads)
    out_wide = spread(dt * decay_out, expand, heads)

    taps = taps_ref[...]
    bc = conv_rows(sbuf[...], taps, length)
    bc = (bc * sigmoid(bc)).astype(BF16)
    keys, queries = bc[:, :half], bc[:, half:]
    scores = jnp.where(causal(length, False), mm(queries, keys, NT), 0.0)
    squares = jnp.zeros((length, 128), F32)
    masks = head_masks(GROUP_LANES, width)
    for start in range(0, channels, GROUP_LANES):
        lanes = slice(start, start + GROUP_LANES)
        conv_at = slice(channels + start, channels + start + GROUP_LANES)
        table = chan_ref[:, half_no * channels + start : half_no * channels + start + GROUP_LANES]
        xbuf[8:, lanes] = columns_ref[:, conv_at].astype(F32)
        c = conv_rows(xbuf[:, lanes], table, length)
        xbuf[0:8, lanes] = xbuf[length:, lanes]
        xs = c * sigmoid(c)
        values = (xs * dt_wide[:, lanes]).astype(BF16)
        weights, parts = [], []
        for j in range(GROUP_LANES // width):
            h = start // width + j
            gap = jnp.minimum(running[:, h : h + 1] - running_t[h : h + 1, :], 0.0)
            weights.append((scores * jnp.exp2(gap)).astype(BF16))
            parts.append(jnp.where(masks[j], values, jnp.zeros_like(values)))
        before = state[:, lanes]
        before_low = before.astype(BF16)
        saved_ref[0, :, lanes] = before_low
        y = mm(jnp.concatenate(weights, axis=1), jnp.concatenate(parts, axis=0))
        y = y + mm(queries, before_low) * in_wide[:, lanes]
        y_ref[:, lanes] = y
        z = columns_ref[:, lanes].astype(F32)
        gated = (y + table[5:6] * xs) * (z * sigmoid(z))
        mixed_ref[:, lanes] = (gated * table[6:7]).astype(BF16)
        power = gated * gated
        for at in range(0, GROUP_LANES, 128):
            squares = squares + power[:, at : at + 128]
        fresh = mm(keys, (xs * out_wide[:, lanes]).astype(BF16), TN)
        state[:, lanes] = before * in_wide[length - 1 :, lanes] + fresh
    square_ref[...] = jnp.sum(squares, axis=1, keepdims=True)
    sbuf[0:8] = sbuf[length:]


def backward_kernel(first, last, heads, *refs):
    columns_refs, small_ref, y_refs, saved_refs, up_refs = refs[:2], refs[2], refs[3:5], refs[5:7], refs[7:9]
    pull_ref, chan_ref, taps_ref, head_ref, expand_ref, tri_ref, halo0, halo1, shalo_ref, early0, early1, searly_ref = refs[9:21]
    halo_refs, early_refs = (halo0, halo1), (early0, early1)
    refs = refs[21:]
    if not last:
        carried_refs = refs[:6]
    dcolumns_ref, dstate, dtail_ref, dstail_ref, gchan_ref, gtaps_ref, ghead_ref, xbuf, sbuf, dxbuf, dsbuf = refs[-11:]
    length, channels = y_refs[0].shape
    width = channels // heads
    shared = taps_ref.shape[1]
    half = shared // 2
    step_no = pl.program_id(0)
    first_block = step_no == pl.num_programs(0) - 1

    @pl.when(step_no == 0)
    def _():
        if last:
            dstate[...] = jnp.zeros_like(dstate)
            dxbuf[length:] = jnp.zeros((8, 2 * channels), F32)
            dsbuf[length:] = jnp.zeros((8, shared), F32)
            gchan_ref[...] = jnp.zeros_like(gchan_ref)
            gtaps_ref[...] = jnp.zeros_like(gtaps_ref)
            ghead_ref[...] = jnp.zeros_like(ghead_ref)
        else:
            dstate[...] = carried_refs[0][...]
            dxbuf[length:] = carried_refs[1][...]
            dsbuf[length:] = carried_refs[2][...]
            gchan_ref[...] = carried_refs[3][...]
            gtaps_ref[...] = carried_refs[4][...]
            ghead_ref[...] = carried_refs[5][...]

    def outside(rows):
        return jnp.zeros_like(rows) if first else rows

    def shared_of(ref):
        return jnp.concatenate([ref[:, :half], ref[:, half + 128 : shared + 128]], axis=1)

    sbuf[8:] = shared_of(small_ref)
    sbuf[0:8] = jnp.where(first_block, outside(shared_of(searly_ref)), shared_of(shalo_ref))
    tri = tri_ref[...]
    expand = expand_ref[...]
    taps = taps_ref[...]
    bc_in = conv_rows(sbuf[...], taps, length)
    bc_sig = sigmoid(bc_in)
    bc = (bc_in * bc_sig).astype(BF16)
    keys, queries = bc[:, :half], bc[:, half:]
    keep = causal(length, True)
    scores = jnp.where(keep, mm(keys, queries, NT), 0.0)
    pull = pull_ref[...]
    masks = head_masks(GROUP_LANES, width)
    dscores = jnp.zeros((length, length), F32)
    dkeys = jnp.zeros((length, half), F32)
    dqueries = jnp.zeros((length, half), F32)
    last_row = lax.broadcasted_iota(jnp.int32, (length, 1), 0) == length - 1
    lane = lax.broadcasted_iota(jnp.int32, (length, 128), 1)
    per_group = GROUP_LANES // width
    for half_no in range(2):
        columns_ref, halo_ref, early_ref = columns_refs[half_no], halo_refs[half_no], early_refs[half_no]
        y_ref, saved_ref, up_ref = y_refs[half_no], saved_refs[half_no], up_refs[half_no]
        step_lanes = slice(half_no * (half + 128) + half, (half_no + 1) * (half + 128))
        head = head_ref[8 * half_no : 8 * half_no + 8]
        step = small_ref[:, step_lanes] + head[0:1]
        dt = softplus(step)
        rate = dt * head[1:2]
        running = sum(mm(tri, piece) for piece in split3(rate * LOG2E))
        running_t = running.T
        decay_in = jnp.exp2(running)
        decay_out = jnp.exp2(running[length - 1 :] - running)
        dt_wide = spread(dt, expand, heads)
        in_wide = spread(decay_in, expand, heads)
        out_wide = spread(decay_out, expand, heads)
        drun = jnp.zeros((length, 128), F32)
        ddt = jnp.zeros((length, 128), F32)
        for start in range(0, channels, GROUP_LANES):
            lanes = slice(start, start + GROUP_LANES)
            conv_at = slice(channels + start, channels + start + GROUP_LANES)
            at = half_no * channels + start
            wide = slice(at, at + GROUP_LANES)
            table = chan_ref[:, wide]
            xbuf[8:, lanes] = columns_ref[:, conv_at].astype(F32)
            xbuf[0:8, lanes] = jnp.where(first_block, outside(early_ref[:, conv_at].astype(F32)[-8:]), halo_ref[:, conv_at].astype(F32)[-8:])
            c = conv_rows(xbuf[:, lanes], table, length)
            c_sig = sigmoid(c)
            xs = c * c_sig
            z = columns_ref[:, lanes].astype(F32)
            z_sig = sigmoid(z)
            z_silu = z * z_sig
            y = y_ref[:, lanes]
            total = y + table[5:6] * xs
            gated = total * z_silu
            up = up_ref[:, lanes].astype(F32)
            gchan_ref[6:7, wide] += jnp.sum(up * gated, axis=0, keepdims=True)
            dgated = table[6:7] * up - gated * pull
            out_at = half_no * (2 * channels + half + 128) + start
            dcolumns_ref[:, out_at : out_at + GROUP_LANES] = (
                dgated * total * (z_sig + z_silu * (1.0 - z_sig))
            ).astype(BF16)
            dy = dgated * z_silu
            gchan_ref[5:6, wide] += jnp.sum(dy * xs, axis=0, keepdims=True)
            dy_low = dy.astype(BF16)
            dt_lanes = dt_wide[:, lanes]
            values = (xs * dt_lanes).astype(BF16)
            weights, dparts, vparts, decays = [], [], [], []
            for j in range(per_group):
                h = start // width + j
                decay = jnp.exp2(jnp.minimum(running_t[h : h + 1, :] - running[:, h : h + 1], 0.0))
                decays.append(decay)
                weights.append((scores * decay).astype(BF16))
                dparts.append(jnp.where(masks[j], dy_low, jnp.zeros_like(dy_low)))
                vparts.append(jnp.where(masks[j], values, jnp.zeros_like(values)))
            outer = mm(jnp.concatenate(vparts, axis=0), dy_low, NT)
            for j in range(per_group):
                dscores = dscores + outer[j * length : (j + 1) * length] * decays[j]
            dvalues = mm(jnp.concatenate(weights, axis=1), jnp.concatenate(dparts, axis=0))
            before = saved_ref[0, :, lanes]
            dafter = dstate[:, wide]
            dafter_low = dafter.astype(BF16)
            out_lanes = out_wide[:, lanes]
            carried = mm(keys, dafter_low) * out_lanes
            dvalues = dvalues + carried
            values_f = values.astype(F32)
            dkeys = dkeys + mm((values_f * out_lanes).astype(BF16), dafter_low, NT)
            in_lanes = in_wide[:, lanes]
            dy_in = (dy * in_lanes).astype(BF16)
            dqueries = dqueries + mm(dy_in, before, NT)
            end_decay = in_lanes[length - 1 :]
            at_end = jnp.sum(values_f * carried, axis=0, keepdims=True) + end_decay * jnp.sum(
                before.astype(F32) * dafter, axis=0, keepdims=True
            )
            dstate[:, wide] = end_decay * dafter + mm(queries, dy_in, TN)
            turn = dy_low.astype(F32) * y - values_f * dvalues + jnp.where(last_row, at_end, 0.0)
            turn_high = turn.astype(BF16)
            turn_low = (turn - turn_high.astype(F32)).astype(BF16)
            group_expand = expand[:, lanes]
            drun = drun + mm(turn_high, group_expand, NT) + mm(turn_low, group_expand, NT)
            ddt = ddt + mm((dvalues * xs).astype(BF16), group_expand, NT)
            dxs = dvalues * dt_lanes + table[5:6] * dy
            dc = dxs * (c_sig + xs * (1.0 - c_sig))
            dxbuf[0:length, wide] = dc
            window = dxbuf[:, wide]
            here = xbuf[8:, lanes]
            gchan_ref[4:5, wide] += jnp.sum(dc, axis=0, keepdims=True)
            gchan_ref[3:4, wide] += jnp.sum(dc * here, axis=0, keepdims=True)
            dconv = table[3:4] * dc
            for ahead in range(1, 4):
                moved = pltpu.roll(window, length + 8 - ahead, 0)[:length]
                gchan_ref[3 - ahead : 4 - ahead, wide] += jnp.sum(moved * here, axis=0, keepdims=True)
                dconv = dconv + table[3 - ahead : 4 - ahead] * moved
            out_at = out_at + channels
            dcolumns_ref[:, out_at : out_at + GROUP_LANES] = dconv.astype(BF16)
            dxbuf[length:, wide] = dxbuf[0:8, wide]

        drate = sum(mm(tri, piece, TN) for piece in split3(drun))
        dstep = (ddt + drate * head[1:2]) * sigmoid(step)
        ghead_ref[8 * half_no : 8 * half_no + 1] += jnp.sum(dstep, axis=0, keepdims=True)
        ghead_ref[8 * half_no + 1 : 8 * half_no + 2] += jnp.sum(drate * rate, axis=0, keepdims=True)
        out_at = half_no * (2 * channels + half + 128) + 2 * channels + half
        dcolumns_ref[:, out_at : out_at + 128] = jnp.where(lane < heads, dstep, 0.0).astype(BF16)

    dscores_low = jnp.where(keep, dscores, 0.0).astype(BF16)
    dkeys = dkeys + mm(dscores_low, queries)
    dqueries = dqueries + mm(dscores_low, keys, TN)
    dbc = jnp.concatenate([dkeys, dqueries], axis=1) * (bc_sig + bc_in * bc_sig * (1.0 - bc_sig))
    dsbuf[0:length] = dbc
    window = dsbuf[...]
    here = sbuf[8:]
    gtaps_ref[4:5] += jnp.sum(dbc, axis=0, keepdims=True)
    gtaps_ref[3:4] += jnp.sum(dbc * here, axis=0, keepdims=True)
    dshared = taps[3:4] * dbc
    for ahead in range(1, 4):
        moved = pltpu.roll(window, length + 8 - ahead, 0)[:length]
        gtaps_ref[3 - ahead : 4 - ahead] += jnp.sum(moved * here, axis=0, keepdims=True)
        dshared = dshared + taps[3 - ahead : 4 - ahead] * moved
    for half_no in range(2):
        out_at = half_no * (2 * channels + half + 128) + 2 * channels
        dcolumns_ref[:, out_at : out_at + half] = dshared[:, half_no * half : (half_no + 1) * half].astype(BF16)
    dsbuf[length:] = dsbuf[0:8]
    dtail_ref[...] = dxbuf[0:8]
    dstail_ref[...] = dsbuf[0:8]


def scan_tables(heads, channels):
    row = lax.broadcasted_iota(jnp.int32, (128, channels), 0) % heads
    col = lax.broadcasted_iota(jnp.int32, (128, channels), 1) // (channels // heads)
    return (row == col).astype(BF16), jnp.tril(jnp.ones((CHUNK, CHUNK), BF16))


def whole(array):
    return pl.BlockSpec(array.shape, lambda i: (0,) * array.ndim)


def last_rows(array, count):
    at = array.shape[0] // count - 1
    return pl.BlockSpec((count,) + array.shape[1:], lambda i: (at, 0))


def unread(arrays):
    return [pl.BlockSpec(memory_space=pl.ANY) for _ in arrays]


def mixer_forward(columns, small, tables, heads, half_no, earlier=None, after=()):
    tokens, channels = columns.shape[0], columns.shape[1] // 2
    shared = tables[1].shape[1]
    blocks = tokens // CHUNK

    def rows(cols):
        return pl.BlockSpec((CHUNK, cols), lambda i: (i, 0))

    operands = [columns, small, *tables]
    specs = [rows(2 * channels), rows(small.shape[1])] + [whole(table) for table in tables]
    if earlier is not None:
        operands += list(earlier)
        specs += [whole(earlier[0]), last_rows(earlier[1], 16), last_rows(earlier[2], 8)]
    operands += list(after)
    specs += unread(after)
    return pl.pallas_call(
        functools.partial(forward_kernel, earlier is None, heads, half_no),
        grid=(blocks,),
        in_specs=specs,
        out_specs=[
            rows(channels),
            rows(1),
            rows(channels),
            pl.BlockSpec((1, shared // 2, channels), lambda i: (i, 0, 0)),
            pl.BlockSpec((shared // 2, channels), lambda i: (0, 0)),
        ],
        out_shape=[
            jax.ShapeDtypeStruct((tokens, channels), BF16),
            jax.ShapeDtypeStruct((tokens, 1), F32),
            jax.ShapeDtypeStruct((tokens, channels), F32),
            jax.ShapeDtypeStruct((blocks, shared // 2, channels), BF16),
            jax.ShapeDtypeStruct((shared // 2, channels), F32),
        ],
        scratch_shapes=[
            pltpu.VMEM((CHUNK + 8, channels), F32),
            pltpu.VMEM((CHUNK + 8, shared), F32),
        ],
        compiler_params=pltpu.CompilerParams(vmem_limit_bytes=48 * 1024 * 1024),
        cost_estimate=pl.CostEstimate(
            flops=tokens * channels * 6000, bytes_accessed=tokens * channels * 14, transcendentals=tokens * channels * 6
        ),
        name="mixer_forward",
    )(*operands)


def mixer_backward(columns, small, y, saved, up, pull, tables, heads, early, carried, after=()):
    tokens, channels = y[0].shape
    shared = tables[1].shape[1]
    blocks = tokens // CHUNK
    small_width = small.shape[1]

    def rows(cols):
        return pl.BlockSpec((CHUNK, cols), lambda i: (blocks - 1 - i, 0))

    def halo(count, cols):
        per_block = CHUNK // count
        return pl.BlockSpec((count, cols), lambda i: (jnp.maximum((blocks - 1 - i) * per_block - 1, 0), 0))

    def fixed(r, c):
        return pl.BlockSpec((r, c), lambda i: (0, 0))

    saved_spec = pl.BlockSpec((1, shared // 2, channels), lambda i: (blocks - 1 - i, 0, 0))
    before = (columns[0], columns[1], small) if early is None else early
    operands = [*columns, small, *y, *saved, *up, pull, *tables, *columns, small, *before]
    specs = [rows(2 * channels)] * 2 + [rows(small_width)] + [rows(channels)] * 2 + [saved_spec] * 2 + [rows(channels)] * 2
    specs += [rows(1)] + [whole(table) for table in tables]
    specs += [halo(16, 2 * channels)] * 2 + [halo(8, small_width)]
    specs += [last_rows(before[0], 16), last_rows(before[1], 16), last_rows(before[2], 8)]
    if carried is not None:
        operands += list(carried)
        specs += [whole(array) for array in carried]
    operands += list(after)
    specs += unread(after)
    fixed_shapes = [(shared // 2, 2 * channels), (8, 2 * channels), (8, shared), (8, 2 * channels), (8, shared), (16, 128)]
    return pl.pallas_call(
        functools.partial(backward_kernel, early is None, carried is None, heads),
        grid=(blocks,),
        in_specs=specs,
        out_specs=[rows(4 * channels + shared + 256)] + [fixed(*shape) for shape in fixed_shapes],
        out_shape=[
            jax.ShapeDtypeStruct((tokens, 4 * channels + shared + 256), BF16),
        ]
        + [jax.ShapeDtypeStruct(shape, F32) for shape in fixed_shapes],
        scratch_shapes=[
            pltpu.VMEM((CHUNK + 8, channels), F32),
            pltpu.VMEM((CHUNK + 8, shared), F32),
            pltpu.VMEM((CHUNK + 8, 2 * channels), F32),
            pltpu.VMEM((CHUNK + 8, shared), F32),
        ],
        compiler_params=pltpu.CompilerParams(vmem_limit_bytes=56 * 1024 * 1024),
        cost_estimate=pl.CostEstimate(
            flops=tokens * channels * 28000, bytes_accessed=tokens * channels * 40, transcendentals=tokens * channels * 12
        ),
        name="mixer_backward",
    )(*operands)


def stacked_product(lhs, rhs, shards):
    features, tokens = lhs[0].shape
    columns = sum(part.shape[1] for part in rhs[0]) // shards
    whole_rows = len(rhs[0]) == 1
    row_tile = min(512, features)
    tile = columns // 2 if columns % 256 == 0 else columns
    tiles = columns // tile
    chunks = len(lhs)

    def kernel(*refs):
        out_ref = refs[-1]
        shard = pl.program_id(0)
        total = 0.0
        for at in range(chunks):
            rows = refs[at][...]
            if whole_rows:
                total = total + mm(rows, refs[chunks + at][...])
            else:
                pair = refs[chunks + 2 * at : chunks + 2 * at + 2]
                total = total + mm(rows, jnp.where(shard == 0, pair[0][...], pair[1][...]))
        out_ref[0] = total.astype(BF16)

    lhs_spec = pl.BlockSpec((row_tile, tokens), lambda s, n, m: (m, 0))
    if whole_rows:
        rhs_spec = pl.BlockSpec((tokens, tile), lambda s, n, m: (0, s * tiles + n))
    else:
        rhs_spec = pl.BlockSpec((tokens, tile), lambda s, n, m: (0, n))
    parts = [part for chunk in rhs for part in chunk]
    return pl.pallas_call(
        kernel,
        grid=(shards, tiles, features // row_tile),
        in_specs=[lhs_spec] * chunks + [rhs_spec] * len(parts),
        out_specs=pl.BlockSpec((1, row_tile, tile), lambda s, n, m: (s, m, n)),
        out_shape=jax.ShapeDtypeStruct((shards, features, columns), BF16),
        compiler_params=pltpu.CompilerParams(vmem_limit_bytes=48 * 1024 * 1024),
        cost_estimate=pl.CostEstimate(
            flops=2 * shards * features * columns * tokens * chunks,
            bytes_accessed=2 * shards * (features * columns + chunks * tokens * columns + chunks * features * tokens),
            transcendentals=0,
        ),
        name="stacked_product",
    )(*lhs, *parts)


def reduce_kernel(chips, groups, hops, parts, *refs):
    lhs, rhs, vec_ref = refs[:parts], refs[parts : 2 * parts], refs[2 * parts]
    (out_ref, vec_out, pair_out, pair_in, own, chip_out, chip_in, vec_send, vec_recv,
     pair_send_sem, pair_recv_sem, chip_send_sem, chip_recv_sem, vec_send_sem, vec_recv_sem) = refs[2 * parts + 1 :]
    rows, columns = out_ref.shape
    dp, tensor = lax.axis_index("dp"), lax.axis_index("tensor")
    chip, core = dp // 2, dp % 2
    shard, group = tensor % 2, tensor // 2
    tile = columns // 3 if columns % 384 == 0 else columns

    def core_device():
        return (dp + 1 - 2 * core, tensor)

    def pair_device():
        return (dp, tensor + 1 - 2 * shard)

    def chip_device(hop):
        return ((chip + hop) % chips * 2 + core, tensor)

    def group_device(hop):
        return (dp, (group + hop) % groups * 2 + shard)

    partners = [core_device(), pair_device()]
    partners += [chip_device(hop) for hop in range(1, chips)] + [group_device(hop) for hop in range(1, groups)]
    barrier = pltpu.get_barrier_semaphore()
    for partner in partners:
        pl.semaphore_signal(barrier, inc=1, device_id=partner, device_id_type=MESH)
    pl.semaphore_wait(barrier, len(partners))

    def copy(src, dst, send_sem, recv_sem, device):
        return pltpu.make_async_remote_copy(
            src_ref=src, dst_ref=dst, send_sem=send_sem, recv_sem=recv_sem, device_id=device, device_id_type=MESH
        )

    stages = [[core_device()], [pair_device()], [chip_device(hop) for hop in range(1, chips)]]
    stages.append([group_device(hop) for hop in range(1, groups)])
    firsts = [sum(len(stage) for stage in stages[:at]) for at in range(4)]

    def vec_copies(stage):
        return [
            copy(vec_send.at[stage], vec_recv.at[firsts[stage] + at], vec_send_sem.at[firsts[stage] + at],
                 vec_recv_sem.at[firsts[stage] + at], device)
            for at, device in enumerate(stages[stage])
        ]

    def vec_start(stage):
        for each in vec_copies(stage):
            each.start()

    def vec_finish(stage):
        total = vec_send[stage]
        for at, each in enumerate(vec_copies(stage)):
            each.wait()
            total = total + vec_recv[firsts[stage] + at]
        if stage < 3:
            vec_send[stage + 1] = total
            vec_start(stage + 1)
        else:
            vec_out[...] = total

    vec_send[0] = vec_ref[...]
    vec_start(0)

    def product(piece_rows, at):
        total = 0.0
        for part in range(parts):
            total = total + mm(lhs[part][piece_rows, :], rhs[part][:, pl.ds(at, tile)])
        return total

    def pair_copy(piece):
        return copy(pair_out.at[piece % 2], pair_in.at[piece], pair_send_sem.at[piece], pair_recv_sem.at[piece], pair_device())

    def chip_copy(hop):
        return copy(chip_out.at[hop - 1], chip_in.at[hop - 1], chip_send_sem.at[hop - 1], chip_recv_sem.at[hop - 1], chip_device(hop))

    def take_pair(piece):
        pair_copy(piece).wait_recv()
        hop = hops[piece]

        @pl.loop(0, columns // tile)
        def _(step):
            at = pl.ds(pl.multiple_of(step * tile, 128), tile)
            total = own[piece % 2, :, at] + pair_in[piece, :, at].astype(F32)
            if hop:
                chip_out[hop - 1, :, at] = total.astype(BF16)
            else:
                own[piece % 2, :, at] = total

        if hop:
            chip_copy(hop).start()

    for piece, hop in enumerate(hops):
        piece_rows = pl.ds(pl.multiple_of((chip + hop) % chips * rows, rows), rows)
        if piece >= 2:
            pair_copy(piece - 2).wait_send()

        @pl.loop(0, columns // tile)
        def _(step):
            at = pl.multiple_of(step * tile, 128)
            column = pl.multiple_of((1 - shard) * columns + at, 128)
            pair_out[piece % 2, :, pl.ds(at, tile)] = product(piece_rows, column).astype(BF16)

        pair_copy(piece).start()

        @pl.loop(0, columns // tile)
        def _(step):
            at = pl.multiple_of(step * tile, 128)
            column = pl.multiple_of(shard * columns + at, 128)
            own[piece % 2, :, pl.ds(at, tile)] = product(piece_rows, column)

        if piece:
            take_pair(piece - 1)
        if piece < 4:
            vec_finish(piece)
    last = len(hops) - 1
    for stage in range(len(hops), 4):
        vec_finish(stage)
    take_pair(last)
    for hop in range(1, chips):
        chip_copy(hop).wait_recv()

    @pl.loop(0, columns // tile)
    def _(step):
        at = pl.ds(pl.multiple_of(step * tile, 128), tile)
        total = own[last % 2, :, at]
        for hop in range(1, chips):
            total = total + chip_in[hop - 1, :, at].astype(F32)
        out_ref[:, at] = total

    for piece in range(max(0, last - 1), last + 1):
        pair_copy(piece).wait_send()
    for hop in range(1, chips):
        chip_copy(hop).wait_send()


def reduced_product(place, lhs, rhs, vec):
    chips, groups = place.chips, place.groups
    rows, columns = lhs[0].shape[0] // chips, rhs[0].shape[1] // 2
    hops = sorted(range(chips), key=lambda hop: -min(hop, chips - hop))
    parts = len(lhs)
    vecs = 1 + 1 + (chips - 1) + (groups - 1)
    vmem = pl.BlockSpec(memory_space=pltpu.VMEM)
    return pl.pallas_call(
        functools.partial(reduce_kernel, chips, groups, hops, parts),
        in_specs=[vmem] * (2 * parts + 1),
        out_specs=[vmem] * 2,
        out_shape=[jax.ShapeDtypeStruct((rows, columns), F32), jax.ShapeDtypeStruct(vec.shape, F32)],
        scratch_shapes=[
            pltpu.VMEM((2, rows, columns), BF16),
            pltpu.VMEM((chips, rows, columns), BF16),
            pltpu.VMEM((2, rows, columns), F32),
            pltpu.VMEM((chips - 1, rows, columns), BF16),
            pltpu.VMEM((chips - 1, rows, columns), BF16),
            pltpu.VMEM((4,) + vec.shape, F32),
            pltpu.VMEM((vecs,) + vec.shape, F32),
            pltpu.SemaphoreType.DMA((chips,)),
            pltpu.SemaphoreType.DMA((chips,)),
            pltpu.SemaphoreType.DMA((chips - 1,)),
            pltpu.SemaphoreType.DMA((chips - 1,)),
            pltpu.SemaphoreType.DMA((vecs,)),
            pltpu.SemaphoreType.DMA((vecs,)),
        ],
        compiler_params=pltpu.CompilerParams(
            collective_id=0, has_side_effects=True, vmem_limit_bytes=58 * 1024 * 1024
        ),
        cost_estimate=pl.CostEstimate(
            flops=4 * chips * rows * columns * parts * lhs[0].shape[1], bytes_accessed=100 * 1024 * 1024, transcendentals=0
        ),
        name="reduced_product",
    )(*lhs, *rhs, vec)


class Place:
    def __init__(self):
        self.members = lax.axis_size("tensor")
        self.groups = self.members // 2
        self.sequence = lax.axis_index("tensor") % 2
        self.group = lax.axis_index("tensor") // 2
        self.chips = lax.axis_size("dp") // 2
        self.chip = lax.axis_index("dp") // 2
        self.core = lax.axis_index("dp") % 2
        copies = lax.axis_size("dp")
        self.owners = [
            [d * self.members + 2 * g + s for s in range(2) for d in range(copies)] for g in range(self.groups)
        ]

    def to_pair(self, v):
        return lax.ppermute(v, "tensor", [(t, t ^ 1) for t in range(self.members)])

    def to_group(self, v, hop):
        return lax.ppermute(v, "tensor", [(t, (t + 2 * hop) % self.members) for t in range(self.members)])

    def to_core(self, v):
        return lax.ppermute(v, "dp", [(t, t ^ 1) for t in range(2 * self.chips)])

    def to_chip(self, v, hop):
        count = 2 * self.chips
        return lax.ppermute(v, "dp", [(t, (t + 2 * hop) % count) for t in range(count)])

    def core_rows(self, v):
        parts = v.reshape(self.chips, 2, -1, v.shape[1])
        near = lax.dynamic_index_in_dim(parts, self.core, 1, keepdims=False)
        far = lax.dynamic_index_in_dim(parts, 1 - self.core, 1, keepdims=False)
        return near.reshape(-1, v.shape[1]), far.reshape(-1, v.shape[1])

    def scatter_owners(self, v):
        v = v.reshape(-1, v.shape[-1])
        return lax.psum_scatter(v, ("dp", "tensor"), scatter_dimension=0, axis_index_groups=self.owners, tiled=True)

    def gather_owners(self, v):
        return lax.all_gather(v, ("dp", "tensor"), axis=0, axis_index_groups=self.owners, tiled=True)

    def add_groups(self, v):
        return v + sum(self.to_group(v, hop) for hop in range(1, self.groups))

    def sum_groups(self, v):
        return v.astype(F32) + sum(self.to_group(v, hop).astype(F32) for hop in range(1, self.groups))

    def both(self, v, axis):
        other = self.to_pair(v)
        return jnp.where(
            self.sequence == 0, jnp.concatenate([v, other], axis=axis), jnp.concatenate([other, v], axis=axis)
        )

    def rows_of(self, chunks, hop):
        at = (self.group + hop) % self.groups
        if len(chunks) == self.groups == 2:
            return jnp.where(at == 0, chunks[0], chunks[1])
        total = jnp.concatenate(chunks)
        count = total.shape[0] // self.groups
        return lax.dynamic_slice_in_dim(total, at * count, count, 0)

    def gather_chunks(self, v, chunks):
        if chunks == self.groups == 2:
            other = self.to_group(v, 1)
            return [jnp.where(self.group == at, v, other) for at in range(2)]
        count = v.shape[0]
        total = jnp.zeros((count * self.groups,) + v.shape[1:], v.dtype)
        total = lax.dynamic_update_slice_in_dim(total, v, self.group * count, 0)
        for hop in range(1, self.groups):
            start = (self.group - hop) % self.groups * count
            total = lax.dynamic_update_slice_in_dim(total, self.to_group(v, hop), start, 0)
        return jnp.split(total, chunks)

    def scatter_rows(self, chunks):
        arrived = [self.to_group(self.rows_of(chunks, hop), hop) for hop in range(1, self.groups)]
        return self.rows_of(chunks, 0).astype(F32) + sum(piece.astype(F32) for piece in arrived)

    def take_sequence(self, v):
        mine = jnp.where(self.sequence == 0, v[0], v[1])
        other = self.to_pair(jnp.where(self.sequence == 0, v[1], v[0]))
        return jnp.where(self.sequence == 0, jnp.concatenate([mine, other]), jnp.concatenate([other, mine]))

    def give_sequence(self, v):
        first, second = jnp.split(v, 2)
        mine = jnp.where(self.sequence == 0, first, second)
        other = self.to_pair(jnp.where(self.sequence == 0, second, first))
        return jnp.where(self.sequence == 0, jnp.stack([mine, other]), jnp.stack([other, mine]))


def then(v, *earlier):
    return lax.optimization_barrier((v, earlier))[0]


class LastSum:

    def __init__(self, place, features, columns):
        self.place = place
        rows = [place.core_rows(part) for part in features]
        self.lhs = [near for near, far in rows] + [place.to_core(far) for near, far in rows]
        self.rhs = [part for part in columns] + [[place.to_core(shard) for shard in part] for part in columns]

    def by_permutes(self):
        self.stack = stacked_product(self.lhs, self.rhs, 2)
        return self.stack

    def to_pair(self):
        other = lax.dynamic_index_in_dim(self.stack, 1 - self.place.sequence, 0, keepdims=False)
        self.landed = self.place.to_pair(other)
        return other

    def to_chips(self):
        place = self.place
        own = lax.dynamic_index_in_dim(self.stack, place.sequence, 0, keepdims=False)
        total = (own.astype(F32) + self.landed.astype(F32)).astype(BF16)
        pieces = total.reshape(place.chips, -1, total.shape[1])
        self.kept = lax.dynamic_index_in_dim(pieces, place.chip, 0, keepdims=False)
        hops = range(1, place.chips)
        self.sent = [
            lax.dynamic_index_in_dim(pieces, (place.chip + hop) % place.chips, 0, keepdims=False) for hop in hops
        ]
        self.arrived = [place.to_chip(piece, hop) for piece, hop in zip(self.sent, hops)]
        return self.sent

    def total(self):
        return self.kept.astype(F32) + sum(piece.astype(F32) for piece in self.arrived)


def norm_scale(stream):
    return lax.rsqrt(jnp.mean(stream * stream, axis=-1, keepdims=True) + EPSILON)


def block_forward(place, streams, weights, tables, heads, inner, final):
    in_cols, small_cols, out_rows, gain = weights
    main = small_cols[0].shape[1]
    kept = {"stream": streams, "columns": [], "y": [], "saved": [], "mixed": [], "scale": [], "update": []}
    normed = [(stream * norm_scale(stream) * gain).astype(BF16) for stream in streams]
    small = [mm(part, jnp.concatenate(small_cols, axis=1)) for part in normed]
    halves = []
    for half_no, cols in enumerate(in_cols):
        results, earlier = [], None
        for at, part in enumerate(normed):
            columns = mm(part, cols[:, :-main]).astype(BF16)
            mixed, square, y, saved, state = mixer_forward(columns, small[at], tables, heads, half_no, earlier)
            earlier = (state, columns, small[at])
            results.append((columns, mixed, square, y, saved))
        halves.append(results)
    shares, scales = [], []
    for at in range(len(streams)):
        first, second = halves[0][at], halves[1][at]
        scales.append(lax.rsqrt(place.add_groups(first[2] + second[2]) / inner + EPSILON))
        share = (mm(first[1], out_rows[0], NT) + mm(second[1], out_rows[1], NT)).astype(BF16)
        shares.append(then(share, scales[at]))
        for key, position in (("columns", 0), ("mixed", 1), ("y", 3), ("saved", 4)):
            kept[key].append((first[position], second[position]))
    kept.update(normed=normed, small=small, scale=scales)
    if final:
        after = place.rows_of(streams, 0) + place.scatter_rows(shares) * place.rows_of(scales, 0)
    else:
        kept["update"] = [place.sum_groups(share) for share in shares]
        after = [stream + update * scale for stream, update, scale in zip(streams, kept["update"], scales)]
    return after, kept


def norm_backward(stream, grad, grad_normed, gain):
    row_scale = norm_scale(stream)
    unit = stream * row_scale
    lifted = grad_normed * gain
    back = grad + row_scale * (lifted - unit * jnp.mean(lifted * unit, axis=-1, keepdims=True))
    return back, jnp.sum(grad_normed * unit, axis=0)


class Backward:
    def __init__(self, place, weights, tables, heads, inner, kept):
        self.place, self.weights, self.tables, self.heads, self.inner, self.kept = place, weights, tables, heads, inner, kept
        chunks = len(kept["normed"])
        self.ups, self.grad_mixed, self.pulls = [None] * chunks, [None] * chunks, [None] * chunks
        self.dcolumns, self.shares = [None] * chunks, [None] * chunks
        self.carried = None

    def enter(self, at, grad):
        scale = self.kept["scale"][at]
        self.ups[at] = (grad * scale).astype(BF16)
        self.grad_mixed[at] = [mm(self.ups[at], rows) for rows in self.weights[2]]
        if self.kept["update"]:
            pull = jnp.sum(self.ups[at].astype(F32) * self.kept["update"][at], axis=-1, keepdims=True)
        else:
            pairs = zip(self.grad_mixed[at], self.kept["mixed"][at])
            pull = sum(jnp.sum(g * m.astype(F32), axis=-1, keepdims=True) for g, m in pairs)
            pull = self.place.add_groups(pull)
        self.pulls[at] = pull * (scale * scale / self.inner)

    def mix(self, at, after=()):
        kept = self.kept
        result = mixer_backward(
            kept["columns"][at],
            kept["small"][at],
            kept["y"][at],
            kept["saved"][at],
            self.grad_mixed[at],
            self.pulls[at],
            self.tables,
            self.heads,
            (*kept["columns"][at - 1], kept["small"][at - 1]) if at else None,
            self.carried,
            after,
        )
        self.dcolumns[at], self.carried = result[0], result[1:]

    def share(self, columns):
        parts = jnp.split(columns, 2, axis=1)
        return sum(mm(part, cols, NT) for part, cols in zip(parts, self.weights[0])).astype(BF16)


def local(
    hidden,
    cotangent,
    norm_gain,
    in_weights,
    state_weight,
    step_weight,
    channel_taps,
    state_taps,
    step_bias,
    decay_log,
    skip_gain,
    inner_gain,
    out_weight,
):
    place = Place()
    layers = in_weights.shape[0]
    rows = in_weights.shape[2]
    heads = step_bias.shape[1]
    own_cols = in_weights.shape[3]
    width = own_cols // heads
    inner = own_cols * place.members
    shared = state_weight.shape[2]
    half = shared // 2
    copies = 128 // heads
    main = 2 * own_cols
    expand, tri = scan_tables(heads, own_cols)

    weights = []
    for layer in range(layers):
        state_half = lax.dynamic_slice_in_dim(state_weight[layer], place.sequence * half, half, 1)
        thin = [step_weight[layer]] * 2
        blank = jnp.zeros((rows, 127 - 2 * heads), BF16)
        block = [in_weights[layer, 0], in_weights[layer, 1], state_half, *thin, blank, norm_gain[layer][:, None]]
        block = jnp.concatenate(block + [out_weight[layer].T], axis=1)
        both = place.gather_owners(block)
        shards = jnp.split(both, 2)
        thin_end = main + half + 128
        in_cols = [shard[:, :thin_end] for shard in shards]
        small_cols = [shard[:, main:thin_end] for shard in shards]
        out_rows = [shard[:, thin_end:] for shard in shards]
        gain = shards[0][:, thin_end - 1].astype(F32)
        weights.append((in_cols, small_cols, out_rows, gain))

    streams = place.gather_chunks(place.take_sequence(hidden), PIECES)
    streams = [stream.astype(F32) for stream in streams]
    per_channel = place.both(jnp.concatenate([channel_taps, inner_gain[:, None]], axis=1), 2)
    per_head = jnp.stack([step_bias, decay_log, skip_gain], axis=1)
    per_head = place.both(per_head[:, None], 1)
    tables = []
    for layer in range(layers):
        wide_skip = jnp.repeat(per_head[layer, :, 2].reshape(-1), width)[None]
        blank = jnp.zeros((1, main), F32)
        chan = jnp.concatenate([per_channel[layer, :5], wide_skip, per_channel[layer, 5:6], blank], axis=0)
        taps = jnp.concatenate([state_taps[layer], jnp.zeros((3, shared), F32)], axis=0)
        head = []
        for part in range(2):
            pair = jnp.stack([per_head[layer, part, 0], -jnp.exp(per_head[layer, part, 1])])
            pair = jnp.concatenate([pair, pair, jnp.zeros((2, 128 - 2 * heads), F32)], axis=1)
            head += [pair, jnp.zeros((6, 128), F32)]
        tables.append((chan, taps, jnp.concatenate(head), expand, tri))

    kept = []
    for layer in range(layers):
        final = layer == layers - 1
        if layer == 0:
            last_up = place.take_sequence(then(cotangent, streams))
            last_up = place.gather_chunks(last_up, PIECES)
        streams, saved = block_forward(place, streams, weights[layer], tables[layer], heads, inner, final)
        kept.append(saved)
    mixed_out = place.give_sequence(streams.astype(BF16)).astype(F32)

    grads = [part.astype(F32) for part in last_up]
    in_grads, out_grads, gain_grads, carried = [None] * layers, [None] * layers, [None] * layers, [None] * layers
    for layer in reversed(range(layers)):
        back = Backward(place, weights[layer], tables[layer], heads, inner, kept[layer])
        for at in reversed(range(PIECES)):
            back.enter(at, grads[at])
        streams, gain, mixed = kept[layer]["stream"], weights[layer][3], kept[layer]["mixed"]
        turned = [part.T for part in kept[layer]["normed"]]
        ups = [part.T for part in back.ups]
        if layer:
            out_stack = stacked_product(ups, mixed, 2)
            out_grads[layer] = place.scatter_owners(out_stack)
            held = (out_stack,)
            for at in reversed(range(PIECES)):
                back.mix(at, held)
                back.shares[at] = back.share(back.dcolumns[at])
                held = (back.shares[at],)
            in_stack = stacked_product(then(tuple(turned), *back.shares), [[part] for part in back.dcolumns], 2)
            in_grads[layer] = place.scatter_owners(in_stack)
            sums = then(tuple(place.sum_groups(share) for share in back.shares), in_stack)
            results = [norm_backward(*parts, gain) for parts in zip(streams, grads, sums)]
            grads = [result[0] for result in results]
            gain_grads[layer] = jnp.where(place.group == 0, sum(result[1] for result in results), 0.0)
        else:
            out_sum = LastSum(place, ups, mixed)
            held = (out_sum.by_permutes(), out_sum.to_pair())
            for at in reversed(range(PIECES)):
                back.mix(at, held)
                held = ()
            if len(back.dcolumns) == place.groups:
                sent = [back.share(place.rows_of(back.dcolumns, hop)) for hop in range(1, place.groups)]
                own = back.share(then(place.rows_of(back.dcolumns, 0), *sent))
            else:
                shares = [back.share(columns) for columns in back.dcolumns]
                sent = [place.rows_of(shares, hop) for hop in range(1, place.groups)]
                own = place.rows_of(shares, 0)
            arrived = [place.to_group(piece, hop) for hop, piece in enumerate(sent, 1)]
            in_sum = LastSum(place, turned, [[part] for part in back.dcolumns])
            out_sent = out_sum.to_chips()
            grad_normed = own.astype(F32) + sum(piece.astype(F32) for piece in arrived)
            grad, gain_grads[layer] = norm_backward(
                place.rows_of(streams, 0), place.rows_of(grads, 0), grad_normed, gain
            )
        carried[layer] = back.carried[3:]
    grad_hidden = place.give_sequence(grad.astype(BF16)).astype(F32)

    slots, sizes = [], []
    for layer in range(layers):
        gchan, gtaps, ghead = carried[layer]
        skips = gchan[5].reshape(2, heads, width).sum(axis=2)
        mine = jnp.stack([ghead[0, :heads], ghead[8, :heads], ghead[1, :heads], ghead[9, :heads], skips[0], skips[1]])
        channels = jnp.concatenate([gchan[:5].reshape(-1), gchan[6], mine.reshape(-1)])
        slot = lax.broadcasted_iota(jnp.int32, (place.groups, 1), 0) == place.group
        slotted = jnp.where(slot, channels[None], 0.0).reshape(-1)
        slots.append(jnp.concatenate([slotted, gtaps[:5].reshape(-1), gain_grads[layer]]))
        sizes = [channels.size, gtaps[:5].size]
    vec = jnp.concatenate(slots)
    count = -(-vec.size // 1024) * 1024
    vec = jnp.concatenate([vec, jnp.zeros((count - vec.size,), F32)]).reshape(-1, 128)
    vec = then(vec, *out_sent)
    in_grads[0], vec = reduced_product(place, in_sum.lhs, [part for (part,) in in_sum.rhs], vec)
    out_grads[0] = out_sum.total()
    totals = jnp.split(vec.reshape(-1)[: layers * slots[0].size], layers)

    outs = []
    for layer in range(layers):
        total = totals[layer]
        count = sizes[0] * place.groups
        channels = lax.dynamic_slice_in_dim(total, place.group * sizes[0], sizes[0], 0)
        taps_part = total[count : count + sizes[1]].reshape(5, shared)
        gain_part = lax.dynamic_slice_in_dim(total, count + sizes[1] + lax.axis_index("dp") * rows, rows, 0)
        per_channel_part = channels[: 6 * main].reshape(6, 2, own_cols)
        per_channel_part = lax.dynamic_index_in_dim(per_channel_part, place.sequence, 1, keepdims=False)
        per_head_part = channels[6 * main :].reshape(3, 2, heads)
        per_head_part = lax.dynamic_index_in_dim(per_head_part, place.sequence, 1, keepdims=False)
        in_owned, out_owned = in_grads[layer].astype(F32), out_grads[layer].astype(F32)
        state_part = place.both(place.add_groups(in_owned[:, main : main + half]), 1)
        outs.append(
            (
                gain_part,
                jnp.stack([in_owned[:, :own_cols], in_owned[:, own_cols:main]]),
                state_part,
                in_owned[:, main + half : main + half + heads],
                per_channel_part[:5],
                taps_part,
                per_head_part[0],
                per_head_part[1],
                per_head_part[2],
                per_channel_part[5],
                out_owned.T,
            )
        )
    return (mixed_out, grad_hidden) + tuple(jnp.stack(parts) for parts in zip(*outs))


def solution(mesh):
    placed = (
        P("dp", "tensor", None),
        P("dp", "tensor", None),
        P(None, "dp"),
        P(None, None, "dp", "tensor"),
        P(None, "dp", None),
        P(None, "dp", "tensor"),
        P(None, None, "tensor"),
        P(),
        P(None, "tensor"),
        P(None, "tensor"),
        P(None, "tensor"),
        P(None, "tensor"),
        P(None, "tensor", "dp"),
    )
    return jax.shard_map(
        local,
        mesh=mesh,
        in_specs=placed,
        out_specs=(
            P("dp", "tensor", None),
            P("dp", "tensor", None),
            P(None, "dp"),
            P(None, None, "dp", "tensor"),
            P(None, "dp", None),
            P(None, "dp", "tensor"),
            P(None, None, "tensor"),
            P(),
            P(None, "tensor"),
            P(None, "tensor"),
            P(None, "tensor"),
            P(None, "tensor"),
            P(None, "tensor", "dp"),
        ),
        check_vma=False,
    )
```

```python
import functools

import jax
import jax.numpy as jnp
from jax import lax
from jax.experimental import pallas as pl
from jax.experimental.pallas import tpu as pltpu
from jax.sharding import PartitionSpec as P

EPSILON = 1e-05
CHUNK = 128
PIECES = 2
GROUP_LANES = 256
LOG2E = 1.4426950408889634
F32 = jnp.float32
BF16 = jnp.bfloat16
NN = (((1,), (0,)), ((), ()))
NT = (((1,), (1,)), ((), ()))
MESH = pl.DeviceIdType.MESH
TN = (((0,), (0,)), ((), ()))


def mm(a, b, dims=NN):
    return lax.dot_general(a, b, dims, preferred_element_type=F32)


def sigmoid(v):
    return 0.5 * jnp.tanh(0.5 * v) + 0.5


def softplus(v):
    return jnp.maximum(v, 0.0) + jnp.log(1.0 + jnp.exp(-jnp.abs(v)))


def split3(v):
    high = v.astype(BF16)
    rest = v - high.astype(F32)
    mid = rest.astype(BF16)
    return high, mid, (rest - mid.astype(F32)).astype(BF16)


def spread(v, expand, heads):
    high = v.astype(BF16)
    low = (v - high.astype(F32)).astype(BF16)
    lane = lax.broadcasted_iota(jnp.int32, v.shape, 1)
    parts = jnp.where(lane < heads, high, jnp.where(lane < 2 * heads, low, jnp.zeros_like(low)))
    return mm(parts, expand)


def conv_rows(window, table, length):
    total = table[4:5] + table[3:4] * window[8 : 8 + length]
    for back in range(1, 4):
        total = total + table[3 - back : 4 - back] * pltpu.roll(window, back, 0)[8 : 8 + length]
    return total


def causal(length, flip):
    row = lax.broadcasted_iota(jnp.int32, (length, length), 0)
    col = lax.broadcasted_iota(jnp.int32, (length, length), 1)
    return (row <= col) if flip else (row >= col)


def head_masks(lanes, width):
    lane = lax.broadcasted_iota(jnp.int32, (1, lanes), 1)
    return [(lane >= j * width) & (lane < (j + 1) * width) for j in range(lanes // width)]


def both_halves(ref):
    half = ref.shape[2] - 128
    return jnp.concatenate([ref[0, :, :half], ref[1, :, :half]], axis=1)


def forward_kernel(first, heads, *refs):
    columns_ref, small_ref, chan_ref, taps_ref, head_ref, expand_ref, tri_ref = refs[:7]
    refs = refs[7:]
    if not first:
        start_ref, tail_ref, stail_ref = refs[:3]
    mixed_ref, square_ref, y_ref, saved_ref, state, xbuf, sbuf = refs[-7:]
    length, channels = y_ref.shape[1:]
    width = channels // heads
    shared = taps_ref.shape[1]
    half = shared // 2

    @pl.when(pl.program_id(0) == 0)
    def _():
        if first:
            state[...] = jnp.zeros_like(state)
            xbuf[0:8] = jnp.zeros((8, 2 * channels), F32)
            sbuf[0:8] = jnp.zeros((8, shared), F32)
        else:
            state[...] = start_ref[...]
            for half_no in range(2):
                xbuf[0:8, half_no * channels : (half_no + 1) * channels] = tail_ref[half_no, :, channels:].astype(F32)[-8:]
            sbuf[0:8] = both_halves(stail_ref)

    sbuf[8:] = both_halves(small_ref)
    tri = tri_ref[...]
    expand = expand_ref[...]
    taps = taps_ref[...]
    bc = conv_rows(sbuf[...], taps, length)
    bc = (bc * sigmoid(bc)).astype(BF16)
    keys, queries = bc[:, :half], bc[:, half:]
    scores = jnp.where(causal(length, False), mm(queries, keys, NT), 0.0)
    squares = jnp.zeros((length, 128), F32)
    masks = head_masks(GROUP_LANES, width)
    for half_no in range(2):
        head = head_ref[8 * half_no : 8 * half_no + 8]
        dt = softplus(small_ref[half_no, :, half:] + head[0:1])
        running = sum(mm(tri, piece) for piece in split3(dt * (head[1:2] * LOG2E)))
        running_t = running.T
        decay_in = jnp.exp2(running)
        decay_out = jnp.exp2(running[length - 1 :] - running)
        dt_wide = spread(dt, expand, heads)
        in_wide = spread(decay_in, expand, heads)
        out_wide = spread(dt * decay_out, expand, heads)
        for start in range(0, channels, GROUP_LANES):
            lanes = slice(start, start + GROUP_LANES)
            conv_at = slice(channels + start, channels + start + GROUP_LANES)
            wide = slice(half_no * channels + start, half_no * channels + start + GROUP_LANES)
            table = chan_ref[:, wide]
            xbuf[8:, wide] = columns_ref[half_no, :, conv_at].astype(F32)
            c = conv_rows(xbuf[:, wide], table, length)
            xbuf[0:8, wide] = xbuf[length:, wide]
            xs = c * sigmoid(c)
            values = (xs * dt_wide[:, lanes]).astype(BF16)
            weights, parts = [], []
            for j in range(GROUP_LANES // width):
                h = start // width + j
                gap = jnp.minimum(running[:, h : h + 1] - running_t[h : h + 1, :], 0.0)
                weights.append((scores * jnp.exp2(gap)).astype(BF16))
                parts.append(jnp.where(masks[j], values, jnp.zeros_like(values)))
            before = state[:, wide]
            before_low = before.astype(BF16)
            saved_ref[half_no, 0, :, lanes] = before_low
            y = mm(jnp.concatenate(weights, axis=1), jnp.concatenate(parts, axis=0))
            y = y + mm(queries, before_low) * in_wide[:, lanes]
            y_ref[half_no, :, lanes] = y
            z = columns_ref[half_no, :, lanes].astype(F32)
            gated = (y + table[5:6] * xs) * (z * sigmoid(z))
            mixed_ref[half_no, :, lanes] = (gated * table[6:7]).astype(BF16)
            power = gated * gated
            for at in range(0, GROUP_LANES, 128):
                squares = squares + power[:, at : at + 128]
            fresh = mm(keys, (xs * out_wide[:, lanes]).astype(BF16), TN)
            state[:, wide] = before * in_wide[length - 1 :, lanes] + fresh
    square_ref[...] = jnp.sum(squares, axis=1, keepdims=True)
    sbuf[0:8] = sbuf[length:]


def backward_kernel(first, last, heads, *refs):
    columns_ref, small_ref, y_ref, saved_ref, up_ref, pull_ref = refs[:6]
    chan_ref, taps_ref, head_ref, expand_ref, tri_ref, halo_ref, shalo_ref, early_ref, searly_ref = refs[6:15]
    refs = refs[15:]
    if not last:
        carried_refs = refs[:6]
    dcolumns_ref, dstate, dtail_ref, dstail_ref, gchan_ref, gtaps_ref, ghead_ref, xbuf, sbuf, dxbuf, dsbuf = refs[-11:]
    length, channels = y_ref.shape[1:]
    width = channels // heads
    shared = taps_ref.shape[1]
    half = shared // 2
    step_no = pl.program_id(0)
    first_block = step_no == pl.num_programs(0) - 1

    @pl.when(step_no == 0)
    def _():
        if last:
            dstate[...] = jnp.zeros_like(dstate)
            dxbuf[length:] = jnp.zeros((8, 2 * channels), F32)
            dsbuf[length:] = jnp.zeros((8, shared), F32)
            gchan_ref[...] = jnp.zeros_like(gchan_ref)
            gtaps_ref[...] = jnp.zeros_like(gtaps_ref)
            ghead_ref[...] = jnp.zeros_like(ghead_ref)
        else:
            dstate[...] = carried_refs[0][...]
            dxbuf[length:] = carried_refs[1][...]
            dsbuf[length:] = carried_refs[2][...]
            gchan_ref[...] = carried_refs[3][...]
            gtaps_ref[...] = carried_refs[4][...]
            ghead_ref[...] = carried_refs[5][...]

    def outside(rows):
        return jnp.zeros_like(rows) if first else rows

    sbuf[8:] = both_halves(small_ref)
    sbuf[0:8] = jnp.where(first_block, outside(both_halves(searly_ref)), both_halves(shalo_ref))
    tri = tri_ref[...]
    expand = expand_ref[...]
    taps = taps_ref[...]
    bc_in = conv_rows(sbuf[...], taps, length)
    bc_sig = sigmoid(bc_in)
    bc = (bc_in * bc_sig).astype(BF16)
    keys, queries = bc[:, :half], bc[:, half:]
    keep = causal(length, True)
    scores = jnp.where(keep, mm(keys, queries, NT), 0.0)
    pull = pull_ref[...]
    masks = head_masks(GROUP_LANES, width)
    dscores = jnp.zeros((length, length), F32)
    dkeys = jnp.zeros((length, half), F32)
    dqueries = jnp.zeros((length, half), F32)
    last_row = lax.broadcasted_iota(jnp.int32, (length, 1), 0) == length - 1
    lane = lax.broadcasted_iota(jnp.int32, (length, 128), 1)
    per_group = GROUP_LANES // width
    for half_no in range(2):
        head = head_ref[8 * half_no : 8 * half_no + 8]
        step = small_ref[half_no, :, half:] + head[0:1]
        dt = softplus(step)
        rate = dt * head[1:2]
        running = sum(mm(tri, piece) for piece in split3(rate * LOG2E))
        running_t = running.T
        decay_in = jnp.exp2(running)
        decay_out = jnp.exp2(running[length - 1 :] - running)
        dt_wide = spread(dt, expand, heads)
        in_wide = spread(decay_in, expand, heads)
        out_wide = spread(decay_out, expand, heads)
        drun = jnp.zeros((length, 128), F32)
        ddt = jnp.zeros((length, 128), F32)
        for start in range(0, channels, GROUP_LANES):
            lanes = slice(start, start + GROUP_LANES)
            conv_at = slice(channels + start, channels + start + GROUP_LANES)
            at = half_no * channels + start
            wide = slice(at, at + GROUP_LANES)
            table = chan_ref[:, wide]
            xbuf[8:, lanes] = columns_ref[half_no, :, conv_at].astype(F32)
            xbuf[0:8, lanes] = jnp.where(first_block, outside(early_ref[half_no, :, conv_at].astype(F32)[-8:]), halo_ref[half_no, :, conv_at].astype(F32)[-8:])
            c = conv_rows(xbuf[:, lanes], table, length)
            c_sig = sigmoid(c)
            xs = c * c_sig
            z = columns_ref[half_no, :, lanes].astype(F32)
            z_sig = sigmoid(z)
            z_silu = z * z_sig
            y = y_ref[half_no, :, lanes]
            total = y + table[5:6] * xs
            gated = total * z_silu
            up = up_ref[half_no, :, lanes].astype(F32)
            gchan_ref[6:7, wide] += jnp.sum(up * gated, axis=0, keepdims=True)
            dgated = table[6:7] * up - gated * pull
            out_at = half_no * (2 * channels + half + 128) + start
            dcolumns_ref[:, out_at : out_at + GROUP_LANES] = (
                dgated * total * (z_sig + z_silu * (1.0 - z_sig))
            ).astype(BF16)
            dy = dgated * z_silu
            gchan_ref[5:6, wide] += jnp.sum(dy * xs, axis=0, keepdims=True)
            dy_low = dy.astype(BF16)
            dt_lanes = dt_wide[:, lanes]
            values = (xs * dt_lanes).astype(BF16)
            weights, dparts, vparts, decays = [], [], [], []
            for j in range(per_group):
                h = start // width + j
                decay = jnp.exp2(jnp.minimum(running_t[h : h + 1, :] - running[:, h : h + 1], 0.0))
                decays.append(decay)
                weights.append((scores * decay).astype(BF16))
                dparts.append(jnp.where(masks[j], dy_low, jnp.zeros_like(dy_low)))
                vparts.append(jnp.where(masks[j], values, jnp.zeros_like(values)))
            outer = mm(jnp.concatenate(vparts, axis=0), dy_low, NT)
            for j in range(per_group):
                dscores = dscores + outer[j * length : (j + 1) * length] * decays[j]
            dvalues = mm(jnp.concatenate(weights, axis=1), jnp.concatenate(dparts, axis=0))
            before = saved_ref[half_no, 0, :, lanes]
            dafter = dstate[:, wide]
            dafter_low = dafter.astype(BF16)
            out_lanes = out_wide[:, lanes]
            carried = mm(keys, dafter_low) * out_lanes
            dvalues = dvalues + carried
            values_f = values.astype(F32)
            dkeys = dkeys + mm((values_f * out_lanes).astype(BF16), dafter_low, NT)
            in_lanes = in_wide[:, lanes]
            dy_in = (dy * in_lanes).astype(BF16)
            dqueries = dqueries + mm(dy_in, before, NT)
            end_decay = in_lanes[length - 1 :]
            at_end = jnp.sum(values_f * carried, axis=0, keepdims=True) + end_decay * jnp.sum(
                before.astype(F32) * dafter, axis=0, keepdims=True
            )
            dstate[:, wide] = end_decay * dafter + mm(queries, dy_in, TN)
            turn = dy_low.astype(F32) * y - values_f * dvalues + jnp.where(last_row, at_end, 0.0)
            turn_high = turn.astype(BF16)
            turn_low = (turn - turn_high.astype(F32)).astype(BF16)
            group_expand = expand[:, lanes]
            drun = drun + mm(turn_high, group_expand, NT) + mm(turn_low, group_expand, NT)
            ddt = ddt + mm((dvalues * xs).astype(BF16), group_expand, NT)
            dxs = dvalues * dt_lanes + table[5:6] * dy
            dc = dxs * (c_sig + xs * (1.0 - c_sig))
            dxbuf[0:length, wide] = dc
            window = dxbuf[:, wide]
            here = xbuf[8:, lanes]
            gchan_ref[4:5, wide] += jnp.sum(dc, axis=0, keepdims=True)
            gchan_ref[3:4, wide] += jnp.sum(dc * here, axis=0, keepdims=True)
            dconv = table[3:4] * dc
            for ahead in range(1, 4):
                moved = pltpu.roll(window, length + 8 - ahead, 0)[:length]
                gchan_ref[3 - ahead : 4 - ahead, wide] += jnp.sum(moved * here, axis=0, keepdims=True)
                dconv = dconv + table[3 - ahead : 4 - ahead] * moved
            out_at = out_at + channels
            dcolumns_ref[:, out_at : out_at + GROUP_LANES] = dconv.astype(BF16)
            dxbuf[length:, wide] = dxbuf[0:8, wide]

        drate = sum(mm(tri, piece, TN) for piece in split3(drun))
        dstep = (ddt + drate * head[1:2]) * sigmoid(step)
        ghead_ref[8 * half_no : 8 * half_no + 1] += jnp.sum(dstep, axis=0, keepdims=True)
        ghead_ref[8 * half_no + 1 : 8 * half_no + 2] += jnp.sum(drate * rate, axis=0, keepdims=True)
        out_at = half_no * (2 * channels + half + 128) + 2 * channels + half
        dcolumns_ref[:, out_at : out_at + 128] = jnp.where(lane < heads, dstep, 0.0).astype(BF16)

    dscores_low = jnp.where(keep, dscores, 0.0).astype(BF16)
    dkeys = dkeys + mm(dscores_low, queries)
    dqueries = dqueries + mm(dscores_low, keys, TN)
    dbc = jnp.concatenate([dkeys, dqueries], axis=1) * (bc_sig + bc_in * bc_sig * (1.0 - bc_sig))
    dsbuf[0:length] = dbc
    window = dsbuf[...]
    here = sbuf[8:]
    gtaps_ref[4:5] += jnp.sum(dbc, axis=0, keepdims=True)
    gtaps_ref[3:4] += jnp.sum(dbc * here, axis=0, keepdims=True)
    dshared = taps[3:4] * dbc
    for ahead in range(1, 4):
        moved = pltpu.roll(window, length + 8 - ahead, 0)[:length]
        gtaps_ref[3 - ahead : 4 - ahead] += jnp.sum(moved * here, axis=0, keepdims=True)
        dshared = dshared + taps[3 - ahead : 4 - ahead] * moved
    for half_no in range(2):
        out_at = half_no * (2 * channels + half + 128) + 2 * channels
        dcolumns_ref[:, out_at : out_at + half] = dshared[:, half_no * half : (half_no + 1) * half].astype(BF16)
    dsbuf[length:] = dsbuf[0:8]
    dtail_ref[...] = dxbuf[0:8]
    dstail_ref[...] = dsbuf[0:8]


def scan_tables(heads, channels):
    row = lax.broadcasted_iota(jnp.int32, (128, channels), 0) % heads
    col = lax.broadcasted_iota(jnp.int32, (128, channels), 1) // (channels // heads)
    return (row == col).astype(BF16), jnp.tril(jnp.ones((CHUNK, CHUNK), BF16))


def whole(array):
    return pl.BlockSpec(array.shape, lambda i: (0,) * array.ndim)


def last_rows(array, count):
    at = array.shape[1] // count - 1
    return pl.BlockSpec((2, count, array.shape[2]), lambda i: (0, at, 0))


def unread(arrays):
    return [pl.BlockSpec(memory_space=pl.ANY) for _ in arrays]


def mixer_forward(columns, small, tables, heads, earlier=None):
    _, tokens, channels = columns.shape
    channels = channels // 2
    shared = tables[1].shape[1]
    blocks = tokens // CHUNK

    def rows(cols):
        return pl.BlockSpec((2, CHUNK, cols), lambda i: (0, i, 0))

    operands = [columns, small, *tables]
    specs = [rows(2 * channels), rows(small.shape[2])] + [whole(table) for table in tables]
    if earlier is not None:
        operands += list(earlier)
        specs += [whole(earlier[0]), last_rows(earlier[1], 16), last_rows(earlier[2], 8)]
    return pl.pallas_call(
        functools.partial(forward_kernel, earlier is None, heads),
        grid=(blocks,),
        in_specs=specs,
        out_specs=[
            rows(channels),
            pl.BlockSpec((CHUNK, 1), lambda i: (i, 0)),
            rows(channels),
            pl.BlockSpec((2, 1, shared // 2, channels), lambda i: (0, i, 0, 0)),
            pl.BlockSpec((shared // 2, 2 * channels), lambda i: (0, 0)),
        ],
        out_shape=[
            jax.ShapeDtypeStruct((2, tokens, channels), BF16),
            jax.ShapeDtypeStruct((tokens, 1), F32),
            jax.ShapeDtypeStruct((2, tokens, channels), F32),
            jax.ShapeDtypeStruct((2, blocks, shared // 2, channels), BF16),
            jax.ShapeDtypeStruct((shared // 2, 2 * channels), F32),
        ],
        scratch_shapes=[
            pltpu.VMEM((CHUNK + 8, 2 * channels), F32),
            pltpu.VMEM((CHUNK + 8, shared), F32),
        ],
        compiler_params=pltpu.CompilerParams(vmem_limit_bytes=48 * 1024 * 1024),
        cost_estimate=pl.CostEstimate(
            flops=tokens * channels * 12000, bytes_accessed=tokens * channels * 28, transcendentals=tokens * channels * 12
        ),
        name="mixer_forward",
    )(*operands)


def mixer_backward(columns, small, y, saved, up, pull, tables, heads, early, carried, after=()):
    _, tokens, channels = y.shape
    shared = tables[1].shape[1]
    blocks = tokens // CHUNK
    thin = small.shape[2]

    def rows(cols):
        return pl.BlockSpec((2, CHUNK, cols), lambda i: (0, blocks - 1 - i, 0))

    def flat_rows(cols):
        return pl.BlockSpec((CHUNK, cols), lambda i: (blocks - 1 - i, 0))

    def halo(count, cols):
        per_block = CHUNK // count
        return pl.BlockSpec((2, count, cols), lambda i: (0, jnp.maximum((blocks - 1 - i) * per_block - 1, 0), 0))

    def fixed(r, c):
        return pl.BlockSpec((r, c), lambda i: (0, 0))

    saved_spec = pl.BlockSpec((2, 1, shared // 2, channels), lambda i: (0, blocks - 1 - i, 0, 0))
    before = (columns, small) if early is None else early
    operands = [columns, small, y, saved, up, pull, *tables, columns, small, *before]
    specs = [rows(2 * channels), rows(thin), rows(channels), saved_spec, rows(channels), flat_rows(1)]
    specs += [whole(table) for table in tables] + [halo(16, 2 * channels), halo(8, thin)]
    specs += [last_rows(before[0], 16), last_rows(before[1], 8)]
    if carried is not None:
        operands += list(carried)
        specs += [whole(array) for array in carried]
    operands += list(after)
    specs += unread(after)
    fixed_shapes = [(shared // 2, 2 * channels), (8, 2 * channels), (8, shared), (8, 2 * channels), (8, shared), (16, 128)]
    return pl.pallas_call(
        functools.partial(backward_kernel, early is None, carried is None, heads),
        grid=(blocks,),
        in_specs=specs,
        out_specs=[flat_rows(4 * channels + 2 * thin)] + [fixed(*shape) for shape in fixed_shapes],
        out_shape=[jax.ShapeDtypeStruct((tokens, 4 * channels + 2 * thin), BF16)]
        + [jax.ShapeDtypeStruct(shape, F32) for shape in fixed_shapes],
        scratch_shapes=[
            pltpu.VMEM((CHUNK + 8, channels), F32),
            pltpu.VMEM((CHUNK + 8, shared), F32),
            pltpu.VMEM((CHUNK + 8, 2 * channels), F32),
            pltpu.VMEM((CHUNK + 8, shared), F32),
        ],
        compiler_params=pltpu.CompilerParams(vmem_limit_bytes=56 * 1024 * 1024),
        cost_estimate=pl.CostEstimate(
            flops=tokens * channels * 28000, bytes_accessed=tokens * channels * 40, transcendentals=tokens * channels * 12
        ),
        name="mixer_backward",
    )(*operands)


def product_call(kernel, grid, specs, outs, out_specs, operands, flops, name):
    moved = sum(array.size * array.dtype.itemsize for array in operands[:1]) + flops // 512
    return pl.pallas_call(
        kernel,
        grid=grid,
        in_specs=specs,
        out_specs=out_specs,
        out_shape=outs,
        compiler_params=pltpu.CompilerParams(vmem_limit_bytes=60 * 1024 * 1024),
        cost_estimate=pl.CostEstimate(flops=flops, bytes_accessed=moved, transcendentals=0),
        name=name,
    )(*operands)


def in_projection(normed, gathered, own, thin):
    tokens, features = normed.shape

    def kernel(normed_ref, main_ref, thin_ref, columns_ref, small_ref):
        rows = normed_ref[...]
        columns_ref[0] = mm(rows, main_ref[...]).astype(BF16)

        @pl.when(pl.program_id(1) == 0)
        def _():
            small_ref[0] = mm(rows, thin_ref[...])

    return product_call(
        kernel,
        (2, 2),
        [
            pl.BlockSpec((tokens, features), lambda s, n: (0, 0)),
            pl.BlockSpec((features, own), lambda s, n: (s, 1 + n)),
            pl.BlockSpec((features, thin), lambda s, n: (s, 3 * own // thin)),
        ],
        [jax.ShapeDtypeStruct((2, tokens, 2 * own), BF16), jax.ShapeDtypeStruct((2, tokens, thin), F32)],
        [
            pl.BlockSpec((1, tokens, own), lambda s, n: (s, 0, n)),
            pl.BlockSpec((1, tokens, thin), lambda s, n: (s, 0, 0)),
        ],
        (normed, gathered, gathered),
        4 * tokens * features * (2 * own + thin),
        "in_projection",
    )


def out_projection(mixed, gathered, own):
    _, tokens, _ = mixed.shape
    features = gathered.shape[0] // 2
    tile = min(512, features)
    tiles = features // tile

    def kernel(mixed_ref, first_ref, second_ref, share_ref):
        share_ref[...] = (mm(mixed_ref[0], first_ref[...], NT) + mm(mixed_ref[1], second_ref[...], NT)).astype(BF16)

    return product_call(
        kernel,
        (tiles,),
        [
            pl.BlockSpec((2, tokens, own), lambda n: (0, 0, 0)),
            pl.BlockSpec((tile, own), lambda n: (n, 0)),
            pl.BlockSpec((tile, own), lambda n: (tiles + n, 0)),
        ],
        jax.ShapeDtypeStruct((tokens, features), BF16),
        pl.BlockSpec((tokens, tile), lambda n: (0, n)),
        (mixed, gathered, gathered),
        4 * tokens * features * own,
        "out_projection",
    )


def mixed_gradient(up, gathered, own, mixed):
    tokens, features = up.shape

    def kernel(up_ref, weight_ref, mixed_ref, grad_ref, pull_ref):
        grad = mm(up_ref[...], weight_ref[...])
        grad_ref[0] = grad.astype(BF16)
        pull = jnp.sum(grad * mixed_ref[0].astype(F32), axis=1, keepdims=True)

        @pl.when(pl.program_id(0) == 0)
        def _():
            pull_ref[...] = pull

        @pl.when(pl.program_id(0) == 1)
        def _():
            pull_ref[...] += pull

    return product_call(
        kernel,
        (2,),
        [
            pl.BlockSpec((tokens, features), lambda s: (0, 0)),
            pl.BlockSpec((features, own), lambda s: (s, 0)),
            pl.BlockSpec((1, tokens, own), lambda s: (s, 0, 0)),
        ],
        [jax.ShapeDtypeStruct((2, tokens, own), BF16), jax.ShapeDtypeStruct((tokens, 1), F32)],
        [pl.BlockSpec((1, tokens, own), lambda s: (s, 0, 0)), pl.BlockSpec((tokens, 1), lambda s: (0, 0))],
        (up, gathered, mixed),
        4 * tokens * features * own,
        "mixed_gradient",
    )


def normed_gradient(dcolumns, gathered, own, thin):
    tokens, columns = dcolumns.shape
    features = gathered.shape[0] // 2
    tile = min(512, features)
    tiles = features // tile

    def kernel(dcolumns_ref, *refs):
        total, at = 0.0, 0
        for ref in refs[:-1]:
            total = total + mm(dcolumns_ref[:, at : at + ref.shape[1]], ref[...], NT)
            at += ref.shape[1]
        refs[-1][...] = total.astype(BF16)

    specs = [pl.BlockSpec((tokens, columns), lambda n: (0, 0))]
    for shard in range(2):
        specs.append(pl.BlockSpec((tile, own), lambda n, s=shard: (s * tiles + n, 1)))
        specs.append(pl.BlockSpec((tile, own), lambda n, s=shard: (s * tiles + n, 2)))
        specs.append(pl.BlockSpec((tile, thin), lambda n, s=shard: (s * tiles + n, 3 * own // thin)))
    return product_call(
        kernel,
        (tiles,),
        specs,
        jax.ShapeDtypeStruct((tokens, features), BF16),
        pl.BlockSpec((tokens, tile), lambda n: (0, n)),
        (dcolumns,) + (gathered,) * 6,
        2 * tokens * features * columns,
        "normed_gradient",
    )


def stacked_product(lhs, rhs, block=None):
    tokens, features = lhs[0].shape
    chunks = len(lhs)
    split = rhs[0].ndim == 3
    columns = rhs[0].shape[-1] if split else rhs[0].shape[1] // 2
    row_tile, core = (min(256, features), jnp.zeros((1,), jnp.int32)) if block is None else block
    stride = 1 if block is None else 2
    steps = features // (row_tile * stride)

    def kernel(core_ref, *refs):
        out_ref = refs[-1]
        for shard in range(2):
            total = 0.0
            for at in range(chunks):
                ref = refs[chunks + at]
                part = ref[shard] if split else ref[:, shard * columns : (shard + 1) * columns]
                total = total + mm(refs[at][...], part, TN)
            out_ref[shard] = total.astype(BF16)

    return pl.pallas_call(
        kernel,
        grid_spec=pltpu.PrefetchScalarGridSpec(
            num_scalar_prefetch=1,
            grid=(steps,),
            in_specs=[pl.BlockSpec((tokens, row_tile), lambda m, core_ref: (0, stride * m + core_ref[0]))] * chunks
            + [pl.BlockSpec(part.shape, lambda m, core_ref, n=part.ndim: (0,) * n) for part in rhs],
            out_specs=pl.BlockSpec((2, row_tile, columns), lambda m, core_ref: (0, m, 0)),
        ),
        out_shape=jax.ShapeDtypeStruct((2, steps * row_tile, columns), BF16),
        compiler_params=pltpu.CompilerParams(vmem_limit_bytes=60 * 1024 * 1024),
        cost_estimate=pl.CostEstimate(
            flops=4 * steps * row_tile * columns * tokens * chunks,
            bytes_accessed=4 * steps * row_tile * columns + 2 * chunks * tokens * (2 * columns + features),
            transcendentals=0,
        ),
        name="stacked_product",
    )(core, *lhs, *rhs)


class Where:
    def __init__(self, chips, groups):
        self.chips, self.groups = chips, groups
        self.dp, self.tensor = lax.axis_index("dp"), lax.axis_index("tensor")
        self.chip, self.core = self.dp // 2, self.dp % 2
        self.shard, self.group = self.tensor % 2, self.tensor // 2

    def other_core(self):
        return (self.dp + 1 - 2 * self.core, self.tensor)

    def pair(self):
        return (self.dp, self.tensor + 1 - 2 * self.shard)

    def chip_at(self, chip):
        return (chip * 2 + self.core, self.tensor)

    def chip_hop(self, hop):
        return self.chip_at((self.chip + hop) % self.chips)

    def group_hop(self, hop):
        return (self.dp, (self.group + hop) % self.groups * 2 + self.shard)

    def meet(self):
        partners = [self.other_core(), self.pair()]
        partners += [self.chip_hop(hop) for hop in range(1, self.chips)]
        partners += [self.group_hop(hop) for hop in range(1, self.groups)]
        barrier = pltpu.get_barrier_semaphore()
        for partner in partners:
            pl.semaphore_signal(barrier, inc=1, device_id=partner, device_id_type=MESH)
        pl.semaphore_wait(barrier, len(partners))


def remote(src, dst, send_sem, recv_sem, device):
    return pltpu.make_async_remote_copy(
        src_ref=src, dst_ref=dst, send_sem=send_sem, recv_sem=recv_sem, device_id=device, device_id_type=MESH
    )


def gather_kernel(chips, groups, block_ref, hidden_ref, all_ref, stream_ref, left_sem, right_sem, pair_sem, core_sem,
                  chain_recv, pair_recv, core_recv, hidden_send, hidden_recv, local_sem):
    at = Where(chips, groups)
    at.meet()
    mine = pltpu.make_async_copy(block_ref, all_ref.at[at.shard, at.dp], local_sem.at[0])
    mine.start()
    rows = pltpu.make_async_copy(hidden_ref.at[at.shard], stream_ref.at[at.tensor], local_sem.at[1])
    rows.start()

    def hidden_copies():
        slot = stream_ref.at[at.tensor]
        copies = [remote(hidden_ref.at[1 - at.shard], slot, hidden_send.at[0], hidden_recv.at[at.tensor], at.pair())]
        for hop in range(1, groups):
            copies.append(
                remote(hidden_ref.at[at.shard], slot, hidden_send.at[hop], hidden_recv.at[at.tensor], at.group_hop(hop))
            )
        return copies

    def hidden_passed():
        other = at.tensor + 1 - 2 * at.shard
        slot = stream_ref.at[other]
        return [
            remote(slot, slot, hidden_send.at[groups - 1 + hop], hidden_recv.at[other], at.group_hop(hop))
            for hop in range(1, groups)
        ]

    def source(chip):
        return chip * 2 + at.core

    def own_or(chip):
        return all_ref.at[at.shard, source(chip)]

    def to_left(chip, src):
        return remote(src, own_or(chip), left_sem.at[chip], chain_recv.at[chip], at.chip_at(jnp.maximum(at.chip - 1, 0)))

    def to_right(chip, src):
        neighbour = at.chip_at(jnp.minimum(at.chip + 1, chips - 1))
        return remote(src, own_or(chip), right_sem.at[chip], chain_recv.at[chip], neighbour)

    def to_pair(chip, src):
        return remote(src, own_or(chip), pair_sem.at[chip], pair_recv.at[chip], at.pair())

    def to_core(shard, chip, src):
        place = all_ref.at[shard, source(chip)]
        return remote(src, place, core_sem.at[shard, chip], core_recv.at[shard, chip], at.other_core())

    has_left, has_right = at.chip > 0, at.chip < chips - 1
    for copy in hidden_copies():
        copy.start()
    to_pair(at.chip, block_ref).start()

    @pl.when(has_left)
    def _():
        to_left(at.chip, block_ref).start()

    @pl.when(has_right)
    def _():
        to_right(at.chip, block_ref).start()

    to_core(at.shard, at.chip, block_ref).start()

    def from_left(step):
        chip = jnp.maximum(at.chip - step, 0)
        return at.chip >= step, chip

    def from_right(step):
        chip = jnp.minimum(at.chip + step, chips - 1)
        return at.chip + step < chips, chip

    for step in range(1, chips):
        there, chip = from_left(step)

        @pl.when(there)
        def _():
            block = own_or(chip)
            to_right(chip, block).wait_recv()

            @pl.when(has_right)
            def _():
                to_right(chip, block).start()

            to_pair(chip, block).start()
            to_core(at.shard, chip, block).start()

        there, chip = from_right(step)

        @pl.when(there)
        def _():
            block = own_or(chip)
            to_left(chip, block).wait_recv()

            @pl.when(has_left)
            def _():
                to_left(chip, block).start()

            to_pair(chip, block).start()
            to_core(at.shard, chip, block).start()

        if step == 1:
            hidden_copies()[0].wait_send()
            other = at.tensor + 1 - 2 * at.shard
            arrived = stream_ref.at[other]
            remote(arrived, arrived, hidden_send.at[0], hidden_recv.at[other], at.pair()).wait_recv()
            for copy in hidden_passed():
                copy.start()

    def pair_block(chip):
        return all_ref.at[1 - at.shard, source(chip)]

    def pass_pair(chip):
        block = pair_block(chip)
        remote(block, block, pair_sem.at[chip], pair_recv.at[chip], at.pair()).wait_recv()
        to_core(1 - at.shard, chip, block).start()

    pass_pair(at.chip)
    for step in range(1, chips):
        there, chip = from_left(step)

        @pl.when(there)
        def _():
            pass_pair(chip)

        there, chip = from_right(step)

        @pl.when(there)
        def _():
            pass_pair(chip)

    mine.wait()
    rows.wait()
    for copy in hidden_copies()[1:]:
        copy.wait_send()
    for copy in hidden_passed():
        copy.wait_send()
    for hop in range(1, groups):
        for shard in range(2):
            member = (at.group + hop) % groups * 2 + shard
            arrived = stream_ref.at[member]
            remote(arrived, arrived, hidden_send.at[0], hidden_recv.at[member], at.pair()).wait_recv()
    far_core = 1 - at.core
    for chip in range(chips):
        block = own_or(chip)
        to_pair(chip, block).wait_send()
        for shard in range(2):
            to_core(shard, chip, all_ref.at[shard, source(chip)]).wait_send()
            arrived = all_ref.at[shard, chip * 2 + far_core]
            remote(arrived, arrived, core_sem.at[shard, chip], core_recv.at[shard, chip], at.other_core()).wait_recv()

        @pl.when(has_right & (at.chip >= chip))
        def _():
            to_right(chip, block).wait_send()

        @pl.when(has_left & (at.chip <= chip))
        def _():
            to_left(chip, block).wait_send()


def gathered_first(place, block, hidden):
    chips, groups, members = place.chips, place.groups, place.members
    anywhere = pl.BlockSpec(memory_space=pl.ANY)
    dma = pltpu.SemaphoreType.DMA
    both, stream = pl.pallas_call(
        functools.partial(gather_kernel, chips, groups),
        in_specs=[anywhere] * 2,
        out_specs=[anywhere] * 2,
        out_shape=[
            jax.ShapeDtypeStruct((2, 2 * chips) + block.shape, BF16),
            jax.ShapeDtypeStruct((members,) + hidden.shape[1:], BF16),
        ],
        scratch_shapes=[
            dma((chips,)), dma((chips,)), dma((chips,)), dma((2, chips)),
            dma((chips,)), dma((chips,)), dma((2, chips)),
            dma((2 * groups,)), dma((members,)), dma((2,)),
        ],
        compiler_params=pltpu.CompilerParams(collective_id=1, has_side_effects=True),
        cost_estimate=pl.CostEstimate(flops=0, bytes_accessed=300 * 1024 * 1024, transcendentals=0),
        name="gathered_first",
    )(block, hidden)
    return both.reshape(-1, block.shape[1]), stream.reshape(-1, hidden.shape[2])


def reduce_kernel(chips, groups, orders, parts, *refs):
    lhs, rhs, halves_ref, common_ref = refs[:parts], refs[parts : 2 * parts], refs[2 * parts], refs[2 * parts + 1]
    (out_ref, half_out, common_out, pair_out, pair_in, own, chain_in, half_buf, half_in, common_buf, common_in,
     pair_send, pair_recv, chain_send, chain_recv, half_send, half_recv, common_send, common_recv) = refs[2 * parts + 2 :]
    rows, columns = out_ref.shape
    tile = columns // 2 if columns % 256 == 0 else columns
    at = Where(chips, groups)
    at.meet()

    stages = [[at.other_core()], [at.pair()], [at.chip_hop(hop) for hop in range(1, chips)]]
    stages.append([at.group_hop(hop) for hop in range(1, groups)])
    firsts = [sum(len(stage) for stage in stages[:no]) for no in range(4)]

    def small_copies(stage):
        copies = []
        for step, device in enumerate(stages[stage]):
            slot = firsts[stage] + step
            copies.append(
                remote(common_buf.at[stage], common_in.at[slot], common_send.at[slot], common_recv.at[slot], device)
            )
            if stage == 0:
                for shard in range(2):
                    copies.append(
                        remote(half_buf.at[0, shard], half_in.at[shard], half_send.at[shard], half_recv.at[shard], device)
                    )
            elif stage == 1:
                copies.append(
                    remote(half_buf.at[1, 1 - at.shard], half_in.at[2], half_send.at[2], half_recv.at[2], device)
                )
            elif stage == 2:
                copies.append(
                    remote(half_buf.at[2, 0], half_in.at[3 + step], half_send.at[3 + step], half_recv.at[3 + step], device)
                )
        return copies

    def small_start(stage):
        for copy in small_copies(stage):
            copy.start()

    def small_finish(stage):
        for copy in small_copies(stage):
            copy.wait()
        total = common_buf[stage]
        for step in range(len(stages[stage])):
            total = total + common_in[firsts[stage] + step]
        if stage < 3:
            common_buf[stage + 1] = total
        else:
            common_out[...] = total
        if stage == 0:
            for shard in range(2):
                half_buf[1, shard] = half_buf[0, shard] + half_in[shard]
        elif stage == 1:
            half_buf[2, 0] = jnp.where(at.shard == 0, half_buf[1, 0], half_buf[1, 1]) + half_in[2]
        elif stage == 2:
            total = half_buf[2, 0]
            for step in range(chips - 1):
                total = total + half_in[3 + step]
            half_out[...] = total
        if stage < 3:
            small_start(stage + 1)

    half_buf[0] = halves_ref[...]
    common_buf[0] = common_ref[...]
    small_start(0)

    def target(step):
        chip = 0
        for number, order in enumerate(orders):
            chip = chip + jnp.where(at.chip == number, order[step], 0)
        return chip

    def pair_copy(step):
        return remote(pair_out.at[step], pair_in.at[step], pair_send.at[step], pair_recv.at[step], at.pair())

    def chain_copy(step):
        chip = target(step)
        right = chip > at.chip
        neighbour = jnp.clip(jnp.where(right, at.chip + 1, at.chip - 1), 0, chips - 1)
        slot = jnp.where(right | (neighbour != chip), chip, chips)
        return remote(pair_out.at[step], chain_in.at[slot], chain_send.at[step], chain_recv.at[slot], at.chip_at(neighbour))

    def arrival(slot):
        block = chain_in.at[slot]
        return remote(block, block, chain_send.at[0], chain_recv.at[slot], at.pair())

    def multiply(step):
        chip = target(step)
        features = pl.ds(pl.multiple_of((2 * chip + at.core) * rows, 128), rows)

        def product(column):
            total = 0.0
            for part in range(parts):
                total = total + mm(lhs[part][:, features], rhs[part][:, pl.ds(column, tile)], TN)
            return total

        @pl.loop(0, columns // tile)
        def _(tile_no):
            first = pl.multiple_of(tile_no * tile, 128)
            column = pl.multiple_of((1 - at.shard) * columns + first, 128)
            pair_out[step, :, pl.ds(first, tile)] = product(column).astype(BF16)

        pair_copy(step).start()

        @pl.loop(0, columns // tile)
        def _(tile_no):
            first = pl.multiple_of(tile_no * tile, 128)
            column = pl.multiple_of(at.shard * columns + first, 128)
            own[step % 3, :, pl.ds(first, tile)] = product(column)

    def in_tiles(body):
        @pl.loop(0, columns // 128)
        def _(tile_no):
            body(pl.ds(pl.multiple_of(tile_no * 128, 128), 128))

    def add_to_own(step, block, slot):
        def body(lanes):
            own[step % 3, :, lanes] = own[step % 3, :, lanes] + block[slot, :, lanes].astype(F32)

        in_tiles(body)

    def pass_on(step):
        pair_copy(step).wait()
        add_to_own(step, pair_in, step)
        chip = target(step)
        if step < chips - 1:

            @pl.when(((chip > at.chip) & (at.chip > 0)) | ((chip < at.chip) & (at.chip < chips - 1)))
            def _():
                arrival(chip).wait_recv()
                add_to_own(step, chain_in, chip)

            def body(lanes):
                pair_out[step, :, lanes] = own[step % 3, :, lanes].astype(BF16)

            in_tiles(body)
            chain_copy(step).start()
        else:

            @pl.when(at.chip > 0)
            def _():
                arrival(at.chip).wait_recv()
                add_to_own(step, chain_in, at.chip)

            @pl.when(at.chip < chips - 1)
            def _():
                arrival(chips).wait_recv()
                add_to_own(step, chain_in, chips)

            def body(lanes):
                out_ref[:, lanes] = own[step % 3, :, lanes]

            in_tiles(body)

    for step in range(chips):
        multiply(step)
        if step >= 2:
            pass_on(step - 2)
        if step < 4:
            small_finish(step)
    for stage in range(chips, 4):
        small_finish(stage)
    for step in range(max(0, chips - 2), chips):
        pass_on(step)
    for step in range(chips - 1):
        chain_copy(step).wait_send()


def reduced_product(place, lhs, rhs, halves, common, number):
    chips, groups = place.chips, place.groups
    rows, columns = lhs[0].shape[1] // (2 * chips), rhs[0].shape[1] // 2
    orders = []
    for chip in range(chips):
        due = {to: chip + chips - 1 - to if to > chip else chips - 1 - chip + to for to in range(chips) if to != chip}
        orders.append(sorted(due, key=due.get) + [chip])
    parts = len(lhs)
    slots = 1 + 1 + (chips - 1) + (groups - 1)
    vmem = pl.BlockSpec(memory_space=pltpu.VMEM)
    dma = pltpu.SemaphoreType.DMA
    half = halves.shape[1:]
    return pl.pallas_call(
        functools.partial(reduce_kernel, chips, groups, orders, parts),
        in_specs=[vmem] * (2 * parts + 2),
        out_specs=[vmem] * 3,
        out_shape=[
            jax.ShapeDtypeStruct((rows, columns), F32),
            jax.ShapeDtypeStruct(half, F32),
            jax.ShapeDtypeStruct(common.shape, F32),
        ],
        scratch_shapes=[
            pltpu.VMEM((chips, rows, columns), BF16),
            pltpu.VMEM((chips, rows, columns), BF16),
            pltpu.VMEM((3, rows, columns), F32),
            pltpu.VMEM((chips + 1, rows, columns), BF16),
            pltpu.VMEM((3, 2) + half, F32),
            pltpu.VMEM((2 + chips,) + half, F32),
            pltpu.VMEM((4,) + common.shape, F32),
            pltpu.VMEM((slots,) + common.shape, F32),
            dma((chips,)), dma((chips,)), dma((chips,)), dma((chips + 1,)),
            dma((2 + chips,)), dma((2 + chips,)), dma((slots,)), dma((slots,)),
        ],
        compiler_params=pltpu.CompilerParams(
            collective_id=2 + number, has_side_effects=True, vmem_limit_bytes=60 * 1024 * 1024
        ),
        cost_estimate=pl.CostEstimate(
            flops=24 * chips * rows * columns * parts * lhs[0].shape[0], bytes_accessed=100 * 1024 * 1024, transcendentals=0
        ),
        name="reduced_product",
    )(*lhs, *rhs, halves, common)


class Place:
    def __init__(self):
        self.members = lax.axis_size("tensor")
        self.groups = self.members // 2
        self.sequence = lax.axis_index("tensor") % 2
        self.group = lax.axis_index("tensor") // 2
        self.chips = lax.axis_size("dp") // 2
        self.chip = lax.axis_index("dp") // 2
        self.core = lax.axis_index("dp") % 2
        copies = lax.axis_size("dp")
        self.owners = [
            [d * self.members + 2 * g + s for s in range(2) for d in range(copies)] for g in range(self.groups)
        ]

    def to_pair(self, v):
        return lax.ppermute(v, "tensor", [(t, t ^ 1) for t in range(self.members)])

    def to_group(self, v, hop):
        return lax.ppermute(v, "tensor", [(t, (t + 2 * hop) % self.members) for t in range(self.members)])

    def to_core(self, v):
        return lax.ppermute(v, "dp", [(t, t ^ 1) for t in range(2 * self.chips)])

    def to_chip(self, v, hop):
        count = 2 * self.chips
        return lax.ppermute(v, "dp", [(t, (t + 2 * hop) % count) for t in range(count)])

    def gather_owners(self, v):
        return lax.all_gather(v, ("dp", "tensor"), axis=0, axis_index_groups=self.owners, tiled=True)

    def add_groups(self, v):
        return v + sum(self.to_group(v, hop) for hop in range(1, self.groups))

    def sent_to_groups(self, v):
        return [self.to_group(v, hop) for hop in range(1, self.groups)]

    def both(self, v, axis):
        other = self.to_pair(v)
        return jnp.where(
            self.sequence == 0, jnp.concatenate([v, other], axis=axis), jnp.concatenate([other, v], axis=axis)
        )

    def rows_of(self, chunks, hop):
        at = (self.group + hop) % self.groups
        if len(chunks) == self.groups == 2:
            return jnp.where(at == 0, chunks[0], chunks[1])
        total = jnp.concatenate(chunks)
        count = total.shape[0] // self.groups
        return lax.dynamic_slice_in_dim(total, at * count, count, 0)

    def gather_chunks(self, v, chunks):
        if chunks == self.groups == 2:
            other = self.to_group(v, 1)
            return [jnp.where(self.group == at, v, other) for at in range(2)]
        count = v.shape[0]
        total = jnp.zeros((count * self.groups,) + v.shape[1:], v.dtype)
        total = lax.dynamic_update_slice_in_dim(total, v, self.group * count, 0)
        for hop in range(1, self.groups):
            start = (self.group - hop) % self.groups * count
            total = lax.dynamic_update_slice_in_dim(total, self.to_group(v, hop), start, 0)
        return jnp.split(total, chunks)

    def scatter_rows(self, chunks):
        arrived = [self.to_group(self.rows_of(chunks, hop), hop) for hop in range(1, self.groups)]
        return self.rows_of(chunks, 0).astype(F32) + sum(piece.astype(F32) for piece in arrived)

    def take_sequence(self, v):
        mine = jnp.where(self.sequence == 0, v[0], v[1])
        other = self.to_pair(jnp.where(self.sequence == 0, v[1], v[0]))
        return jnp.where(self.sequence == 0, jnp.concatenate([mine, other]), jnp.concatenate([other, mine]))

    def give_sequence(self, v):
        first, second = jnp.split(v.astype(BF16), 2)
        mine = jnp.where(self.sequence == 0, first, second)
        other = self.to_pair(jnp.where(self.sequence == 0, second, first))
        return mine, other

    def both_sequences(self, given, *earlier):
        mine, other = then(given, *earlier)
        mine, other = mine.astype(F32), other.astype(F32)
        return jnp.where(self.sequence == 0, jnp.stack([mine, other]), jnp.stack([other, mine]))


def then(v, *earlier):
    return lax.optimization_barrier((v, earlier))[0]


def added(v, arrived):
    return v.astype(F32) + sum(piece.astype(F32) for piece in arrived)


class WeightSum:

    def __init__(self, place, features, columns):
        self.place = place
        self.lhs = list(features) + [place.to_core(part) for part in features]
        self.rhs = list(columns) + [place.to_core(part) for part in columns]

    def to_pair(self, *earlier):
        place = self.place
        self.lhs = list(then(tuple(self.lhs), *earlier))
        rows = self.lhs[0].shape[1] // (2 * place.chips)
        self.stack = stacked_product(self.lhs, self.rhs, (rows, place.core.astype(jnp.int32)[None]))
        other = lax.dynamic_index_in_dim(self.stack, 1 - self.place.sequence, 0, keepdims=False)
        self.landed = self.place.to_pair(other)
        return other

    def to_chips(self):
        place = self.place
        own = lax.dynamic_index_in_dim(self.stack, place.sequence, 0, keepdims=False)
        total = (own.astype(F32) + self.landed.astype(F32)).astype(BF16)
        pieces = total.reshape(place.chips, -1, total.shape[1])
        self.kept = lax.dynamic_index_in_dim(pieces, place.chip, 0, keepdims=False)
        hops = range(1, place.chips)
        self.sent = [
            lax.dynamic_index_in_dim(pieces, (place.chip + hop) % place.chips, 0, keepdims=False) for hop in hops
        ]
        self.arrived = [place.to_chip(piece, hop) for piece, hop in zip(self.sent, hops)]
        return self.sent

    def total(self, *earlier):
        kept, arrived = then((self.kept, tuple(self.arrived)), *earlier)
        return added(kept, arrived)


def norm_scale(stream):
    return lax.rsqrt(jnp.mean(stream * stream, axis=-1, keepdims=True) + EPSILON)


def block_forward(place, incoming, weights, tables, heads, inner, final):
    gathered, gain, own, thin = weights
    kept = {"update": []}
    for key in ("stream", "normed", "columns", "small", "mixed", "y", "saved", "scale", "share"):
        kept[key] = []
    earlier = None
    for at in range(PIECES):
        stream = incoming(at, *kept["share"][-1:])
        part = (stream * norm_scale(stream) * gain).astype(BF16)
        if at:
            part = then(part, kept["share"][at - 1])
        columns, small = in_projection(part, gathered, own, thin)
        mixed, square, y, saved, state = mixer_forward(columns, small, tables, heads, earlier)
        earlier = (state, columns, small)
        scale = lax.rsqrt(place.add_groups(square) / inner + EPSILON)
        share = then(out_projection(mixed, gathered, own), scale)
        results = (stream, part, columns, small, mixed, y, saved, scale, share)
        names = ("stream", "normed", "columns", "small", "mixed", "y", "saved", "scale", "share")
        for key, value in zip(names, results):
            kept[key].append(value)
    shares, scales = kept["share"], kept["scale"]
    if final:
        after = place.rows_of(kept["stream"], 0) + place.scatter_rows(shares) * place.rows_of(scales, 0)
    else:
        arrived = [place.sent_to_groups(share) for share in shares]

        def after(at, *earlier):
            update = added(shares[at], then(tuple(arrived[at]), *earlier) if earlier else arrived[at])
            kept["update"].append(update)
            return kept["stream"][at] + update * scales[at]

    return after, kept


def norm_backward(stream, grad, grad_normed, gain):
    row_scale = norm_scale(stream)
    unit = stream * row_scale
    lifted = grad_normed * gain
    back = grad + row_scale * (lifted - unit * jnp.mean(lifted * unit, axis=-1, keepdims=True))
    return back, jnp.sum(grad_normed * unit, axis=0)


class Backward:
    def __init__(self, place, weights, tables, heads, inner, kept, final):
        self.final = final
        self.place, self.weights, self.tables, self.heads, self.inner, self.kept = place, weights, tables, heads, inner, kept
        chunks = len(kept["normed"])
        self.ups, self.grad_mixed, self.pulls = [None] * chunks, [None] * chunks, [None] * chunks
        self.dcolumns, self.shares = [None] * chunks, [None] * chunks
        self.carried = None

    def enter(self, at, grad):
        gathered, _, own, _ = self.weights
        scale = self.kept["scale"][at]
        self.ups[at] = (grad * scale).astype(BF16)
        self.grad_mixed[at], pull = mixed_gradient(self.ups[at], gathered, own, self.kept["mixed"][at])
        if not self.final:
            pull = jnp.sum(self.ups[at].astype(F32) * self.kept["update"][at], axis=-1, keepdims=True)
        else:
            pull = self.place.add_groups(pull)
        self.pulls[at] = pull * (scale * scale / self.inner)

    def mix(self, at, after=()):
        kept = self.kept
        result = mixer_backward(
            kept["columns"][at],
            kept["small"][at],
            kept["y"][at],
            kept["saved"][at],
            self.grad_mixed[at],
            self.pulls[at],
            self.tables,
            self.heads,
            (kept["columns"][at - 1], kept["small"][at - 1]) if at else None,
            self.carried,
            after,
        )
        self.dcolumns[at], self.carried = result[0], result[1:]

    def share(self, columns):
        gathered, _, own, thin = self.weights
        return normed_gradient(columns, gathered, own, thin)


def local(
    hidden,
    cotangent,
    norm_gain,
    in_weights,
    state_weight,
    step_weight,
    channel_taps,
    state_taps,
    step_bias,
    decay_log,
    skip_gain,
    inner_gain,
    out_weight,
):
    place = Place()
    layers = in_weights.shape[0]
    rows = in_weights.shape[2]
    heads = step_bias.shape[1]
    own_cols = in_weights.shape[3]
    width = own_cols // heads
    inner = own_cols * place.members
    shared = state_weight.shape[2]
    half = shared // 2
    copies = 128 // heads
    main = 2 * own_cols
    expand, tri = scan_tables(heads, own_cols)

    weights = []
    for layer in range(layers):
        if layer == 1:
            in_weights = then(in_weights, gathered)
        state_half = lax.dynamic_slice_in_dim(state_weight[layer], place.sequence * half, half, 1)
        thin = [step_weight[layer]] * 2
        blank = jnp.zeros((rows, 127 - 2 * heads), BF16)
        block = [out_weight[layer].T, in_weights[layer, 0], in_weights[layer, 1], state_half, *thin, blank]
        block = jnp.concatenate(block + [norm_gain[layer][:, None]], axis=1)
        if layer:
            gathered = place.gather_owners(block)
        else:
            gathered, sequence_rows = gathered_first(place, block, hidden)
        gain = gathered[: gathered.shape[0] // 2, -1].astype(F32)
        weights.append((gathered, gain, own_cols, half + 128))

    chunks = [stream.astype(F32) for stream in jnp.split(sequence_rows, PIECES)]

    def streams(at, *earlier):
        return chunks[at]

    per_channel = place.both(jnp.concatenate([channel_taps, inner_gain[:, None]], axis=1), 2)
    per_head = jnp.stack([step_bias, decay_log, skip_gain], axis=1)
    per_head = place.both(per_head[:, None], 1)
    tables = []
    for layer in range(layers):
        wide_skip = jnp.repeat(per_head[layer, :, 2].reshape(-1), width)[None]
        blank = jnp.zeros((1, main), F32)
        chan = jnp.concatenate([per_channel[layer, :5], wide_skip, per_channel[layer, 5:6], blank], axis=0)
        taps = jnp.concatenate([state_taps[layer], jnp.zeros((3, shared), F32)], axis=0)
        head = []
        for part in range(2):
            pair = jnp.stack([per_head[layer, part, 0], -jnp.exp(per_head[layer, part, 1])])
            pair = jnp.concatenate([pair, pair, jnp.zeros((2, 128 - 2 * heads), F32)], axis=1)
            head += [pair, jnp.zeros((6, 128), F32)]
        tables.append((chan, taps, jnp.concatenate(head), expand, tri))

    kept = []
    for layer in range(layers):
        final = layer == layers - 1
        if layer == 0:
            last_up = place.take_sequence(then(cotangent, chunks))
            last_up = place.gather_chunks(last_up, PIECES)
        streams, saved = block_forward(place, streams, weights[layer], tables[layer], heads, inner, final)
        kept.append(saved)
    mixed_out = place.give_sequence(streams)

    grads = [part.astype(F32) for part in last_up]
    in_sums, out_sums, gain_grads, carried = [None] * layers, [None] * layers, [0.0] * layers, [None] * layers
    half_totals, common_totals = [None] * layers, [None] * layers
    pending, held = None, ()

    def small_sums(layer):
        gchan, gtaps, ghead = carried[layer]
        blank = jnp.zeros((1, own_cols - 256), F32)
        parts = []
        for part in range(2):
            per_head_row = jnp.concatenate([ghead[8 * part : 8 * part + 1], ghead[8 * part + 1 : 8 * part + 2], blank], axis=1)
            parts.append(jnp.concatenate([gchan[:7, part * own_cols : (part + 1) * own_cols], per_head_row]))
        return jnp.stack(parts), gtaps

    for layer in reversed(range(layers)):
        final = layer == layers - 1
        back = Backward(place, weights[layer], tables[layer], heads, inner, kept[layer], final)
        for at in reversed(range(PIECES)):
            if not final:
                share, arrived = pending[at]
                before = (in_sums[layer + 1].owned,) if at == PIECES - 1 else (back.ups[at + 1],)
                grad_normed = added(share, then(tuple(arrived), *before))
                grads[at], gain_grad = norm_backward(
                    kept[layer + 1]["stream"][at], grads[at], grad_normed, weights[layer + 1][1]
                )
                gain_grads[layer + 1] = gain_grads[layer + 1] + jnp.where(place.group == 0, gain_grad, 0.0)
            back.enter(at, grads[at])
        normed, mixed = kept[layer]["normed"], kept[layer]["mixed"]
        out_sum = out_sums[layer] = WeightSum(place, back.ups, mixed)
        held += (out_sum.to_pair(),)
        for at in reversed(range(PIECES)):
            back.mix(at, held)
            held = ()
            if layer:
                back.shares[at] = back.share(back.dcolumns[at])
                held = (back.shares[at],)
                if at == PIECES - 1:
                    held += tuple(out_sum.to_chips())
        carried[layer] = back.carried[3:]
        in_sum = in_sums[layer] = WeightSum(place, normed, back.dcolumns)
        if layer:
            pending = [(share, place.sent_to_groups(share)) for share in back.shares]
            halves, common = small_sums(layer)
            halves = then(halves, *back.shares)
            in_sum.owned, half_totals[layer], common_totals[layer] = reduced_product(
                place, in_sum.lhs, in_sum.rhs, halves, common, layer
            )
            continue
        if PIECES == place.groups:
            sent = [back.share(place.rows_of(back.dcolumns, hop)) for hop in range(1, place.groups)]
            own = back.share(then(place.rows_of(back.dcolumns, 0), *sent))
        else:
            shares = [back.share(columns) for columns in back.dcolumns]
            sent = [place.rows_of(shares, hop) for hop in range(1, place.groups)]
            own = place.rows_of(shares, 0)
        arrived = [place.to_group(piece, hop) for hop, piece in enumerate(sent, 1)]
        out_sent = out_sum.to_chips()
        grad, gain_grads[layer] = norm_backward(
            place.rows_of(kept[layer]["stream"], 0), place.rows_of(grads, 0), added(own, arrived), weights[layer][1]
        )
    grad_hidden = place.give_sequence(grad)

    halves, common = small_sums(0)
    gains = jnp.stack(gain_grads).reshape(-1, shared)
    common = jnp.concatenate([common, gains, jnp.zeros((-gains.shape[0] % 8, shared), F32)])
    common = then(common, *out_sent)
    in_sums[0].owned, half_totals[0], common_totals[0] = reduced_product(
        place, in_sum.lhs, in_sum.rhs, halves, common, 0
    )
    gain_total = common_totals[0][8 : 8 + gains.shape[0]].reshape(layers, -1)

    outs = []
    for layer in range(layers):
        per_channel_part = half_totals[layer]
        gain_part = lax.dynamic_slice_in_dim(gain_total[layer], lax.axis_index("dp") * rows, rows, 0)
        taps_part = common_totals[layer][:5]
        in_owned, out_owned = in_sums[layer].owned, out_sums[layer].total(in_sums[layer].owned)
        state_part = place.both(place.add_groups(in_owned[:, main : main + half]), 1)
        outs.append(
            (
                gain_part,
                jnp.stack([in_owned[:, :own_cols], in_owned[:, own_cols:main]]),
                state_part,
                in_owned[:, main + half : main + half + heads],
                per_channel_part[:5],
                taps_part,
                per_channel_part[7, :heads],
                per_channel_part[7, 128 : 128 + heads],
                per_channel_part[5].reshape(heads, width).sum(axis=1),
                per_channel_part[6],
                out_owned.T,
            )
        )
    mixed_out = place.both_sequences(mixed_out, in_sums[-1].owned)
    grad_hidden = place.both_sequences(grad_hidden, in_sums[0].owned)
    return (mixed_out, grad_hidden) + tuple(jnp.stack(parts) for parts in zip(*outs))


def solution(mesh):
    placed = (
        P("dp", "tensor", None),
        P("dp", "tensor", None),
        P(None, "dp"),
        P(None, None, "dp", "tensor"),
        P(None, "dp", None),
        P(None, "dp", "tensor"),
        P(None, None, "tensor"),
        P(),
        P(None, "tensor"),
        P(None, "tensor"),
        P(None, "tensor"),
        P(None, "tensor"),
        P(None, "tensor", "dp"),
    )
    return jax.shard_map(
        local,
        mesh=mesh,
        in_specs=placed,
        out_specs=(
            P("dp", "tensor", None),
            P("dp", "tensor", None),
            P(None, "dp"),
            P(None, None, "dp", "tensor"),
            P(None, "dp", None),
            P(None, "dp", "tensor"),
            P(None, None, "tensor"),
            P(),
            P(None, "tensor"),
            P(None, "tensor"),
            P(None, "tensor"),
            P(None, "tensor"),
            P(None, "tensor", "dp"),
        ),
        check_vma=False,
    )
```

```python
import functools

import jax
import jax.numpy as jnp
from jax import lax
from jax.experimental import pallas as pl
from jax.experimental.pallas import tpu as pltpu
from jax.sharding import PartitionSpec as P

EPSILON = 1e-05
CHUNK = 128
PIECES = 2
GROUP_LANES = 256
LOG2E = 1.4426950408889634
F32 = jnp.float32
BF16 = jnp.bfloat16
NN = (((1,), (0,)), ((), ()))
NT = (((1,), (1,)), ((), ()))
MESH = pl.DeviceIdType.MESH
TN = (((0,), (0,)), ((), ()))


def mm(a, b, dims=NN):
    return lax.dot_general(a, b, dims, preferred_element_type=F32)


def sigmoid(v):
    return 0.5 * jnp.tanh(0.5 * v) + 0.5


def softplus(v):
    return jnp.maximum(v, 0.0) + jnp.log(1.0 + jnp.exp(-jnp.abs(v)))


def split3(v):
    high = v.astype(BF16)
    rest = v - high.astype(F32)
    mid = rest.astype(BF16)
    return high, mid, (rest - mid.astype(F32)).astype(BF16)


def spread(v, expand, heads):
    high = v.astype(BF16)
    low = (v - high.astype(F32)).astype(BF16)
    lane = lax.broadcasted_iota(jnp.int32, v.shape, 1)
    parts = jnp.where(lane < heads, high, jnp.where(lane < 2 * heads, low, jnp.zeros_like(low)))
    return mm(parts, expand)


def conv_rows(window, table, length):
    total = table[4:5] + table[3:4] * window[8 : 8 + length]
    for back in range(1, 4):
        total = total + table[3 - back : 4 - back] * pltpu.roll(window, back, 0)[8 : 8 + length]
    return total


def causal(length, flip):
    row = lax.broadcasted_iota(jnp.int32, (length, length), 0)
    col = lax.broadcasted_iota(jnp.int32, (length, length), 1)
    return (row <= col) if flip else (row >= col)


def head_masks(lanes, width):
    lane = lax.broadcasted_iota(jnp.int32, (1, lanes), 1)
    return [(lane >= j * width) & (lane < (j + 1) * width) for j in range(lanes // width)]


def both_halves(ref):
    half = ref.shape[2] - 128
    return jnp.concatenate([ref[0, :, :half], ref[1, :, :half]], axis=1)


def forward_kernel(first, heads, *refs):
    columns_ref, small_ref, chan_ref, taps_ref, head_ref, expand_ref, tri_ref = refs[:7]
    refs = refs[7:]
    if not first:
        start_ref, tail_ref, stail_ref = refs[:3]
    mixed_ref, square_ref, y_ref, saved_ref, state, xbuf, sbuf = refs[-7:]
    length, channels = y_ref.shape[1:]
    width = channels // heads
    shared = taps_ref.shape[1]
    half = shared // 2

    @pl.when(pl.program_id(0) == 0)
    def _():
        if first:
            state[...] = jnp.zeros_like(state)
            xbuf[0:8] = jnp.zeros((8, 2 * channels), F32)
            sbuf[0:8] = jnp.zeros((8, shared), F32)
        else:
            state[...] = start_ref[...]
            for half_no in range(2):
                xbuf[0:8, half_no * channels : (half_no + 1) * channels] = tail_ref[half_no, :, channels:].astype(F32)[-8:]
            sbuf[0:8] = both_halves(stail_ref)

    sbuf[8:] = both_halves(small_ref)
    tri = tri_ref[...]
    expand = expand_ref[...]
    taps = taps_ref[...]
    bc = conv_rows(sbuf[...], taps, length)
    bc = (bc * sigmoid(bc)).astype(BF16)
    keys, queries = bc[:, :half], bc[:, half:]
    scores = jnp.where(causal(length, False), mm(queries, keys, NT), 0.0)
    squares = jnp.zeros((length, 128), F32)
    masks = head_masks(GROUP_LANES, width)
    for half_no in range(2):
        head = head_ref[8 * half_no : 8 * half_no + 8]
        dt = softplus(small_ref[half_no, :, half:] + head[0:1])
        running = sum(mm(tri, piece) for piece in split3(dt * (head[1:2] * LOG2E)))
        running_t = running.T
        decay_in = jnp.exp2(running)
        decay_out = jnp.exp2(running[length - 1 :] - running)
        dt_wide = spread(dt, expand, heads)
        in_wide = spread(decay_in, expand, heads)
        out_wide = spread(dt * decay_out, expand, heads)
        for start in range(0, channels, GROUP_LANES):
            lanes = slice(start, start + GROUP_LANES)
            conv_at = slice(channels + start, channels + start + GROUP_LANES)
            wide = slice(half_no * channels + start, half_no * channels + start + GROUP_LANES)
            table = chan_ref[:, wide]
            xbuf[8:, wide] = columns_ref[half_no, :, conv_at].astype(F32)
            c = conv_rows(xbuf[:, wide], table, length)
            xbuf[0:8, wide] = xbuf[length:, wide]
            xs = c * sigmoid(c)
            values = (xs * dt_wide[:, lanes]).astype(BF16)
            weights, parts = [], []
            for j in range(GROUP_LANES // width):
                h = start // width + j
                gap = jnp.minimum(running[:, h : h + 1] - running_t[h : h + 1, :], 0.0)
                weights.append((scores * jnp.exp2(gap)).astype(BF16))
                parts.append(jnp.where(masks[j], values, jnp.zeros_like(values)))
            before = state[:, wide]
            before_low = before.astype(BF16)
            saved_ref[half_no, 0, :, lanes] = before_low
            y = mm(jnp.concatenate(weights, axis=1), jnp.concatenate(parts, axis=0))
            y = y + mm(queries, before_low) * in_wide[:, lanes]
            y_ref[half_no, :, lanes] = y
            z = columns_ref[half_no, :, lanes].astype(F32)
            gated = (y + table[5:6] * xs) * (z * sigmoid(z))
            mixed_ref[half_no, :, lanes] = (gated * table[6:7]).astype(BF16)
            power = gated * gated
            for at in range(0, GROUP_LANES, 128):
                squares = squares + power[:, at : at + 128]
            fresh = mm(keys, (xs * out_wide[:, lanes]).astype(BF16), TN)
            state[:, wide] = before * in_wide[length - 1 :, lanes] + fresh
    square_ref[...] = jnp.sum(squares, axis=1, keepdims=True)
    sbuf[0:8] = sbuf[length:]


def backward_kernel(first, last, heads, *refs):
    columns_ref, small_ref, y_ref, saved_ref, up_ref, pull_ref = refs[:6]
    chan_ref, taps_ref, head_ref, expand_ref, tri_ref, halo_ref, shalo_ref, early_ref, searly_ref = refs[6:15]
    refs = refs[15:]
    if not last:
        carried_refs = refs[:6]
    dcolumns_ref, dstate, dtail_ref, dstail_ref, gchan_ref, gtaps_ref, ghead_ref, xbuf, sbuf, dxbuf, dsbuf = refs[-11:]
    length, channels = y_ref.shape[1:]
    width = channels // heads
    shared = taps_ref.shape[1]
    half = shared // 2
    step_no = pl.program_id(0)
    first_block = step_no == pl.num_programs(0) - 1

    @pl.when(step_no == 0)
    def _():
        if last:
            dstate[...] = jnp.zeros_like(dstate)
            dxbuf[length:] = jnp.zeros((8, 2 * channels), F32)
            dsbuf[length:] = jnp.zeros((8, shared), F32)
            gchan_ref[...] = jnp.zeros_like(gchan_ref)
            gtaps_ref[...] = jnp.zeros_like(gtaps_ref)
            ghead_ref[...] = jnp.zeros_like(ghead_ref)
        else:
            dstate[...] = carried_refs[0][...]
            dxbuf[length:] = carried_refs[1][...]
            dsbuf[length:] = carried_refs[2][...]
            gchan_ref[...] = carried_refs[3][...]
            gtaps_ref[...] = carried_refs[4][...]
            ghead_ref[...] = carried_refs[5][...]

    def outside(rows):
        return jnp.zeros_like(rows) if first else rows

    sbuf[8:] = both_halves(small_ref)
    sbuf[0:8] = jnp.where(first_block, outside(both_halves(searly_ref)), both_halves(shalo_ref))
    tri = tri_ref[...]
    expand = expand_ref[...]
    taps = taps_ref[...]
    bc_in = conv_rows(sbuf[...], taps, length)
    bc_sig = sigmoid(bc_in)
    bc = (bc_in * bc_sig).astype(BF16)
    keys, queries = bc[:, :half], bc[:, half:]
    keep = causal(length, True)
    scores = jnp.where(keep, mm(keys, queries, NT), 0.0)
    pull = pull_ref[...]
    masks = head_masks(GROUP_LANES, width)
    dscores = jnp.zeros((length, length), F32)
    dkeys = jnp.zeros((length, half), F32)
    dqueries = jnp.zeros((length, half), F32)
    last_row = lax.broadcasted_iota(jnp.int32, (length, 1), 0) == length - 1
    lane = lax.broadcasted_iota(jnp.int32, (length, 128), 1)
    per_group = GROUP_LANES // width
    for half_no in range(2):
        head = head_ref[8 * half_no : 8 * half_no + 8]
        step = small_ref[half_no, :, half:] + head[0:1]
        dt = softplus(step)
        rate = dt * head[1:2]
        running = sum(mm(tri, piece) for piece in split3(rate * LOG2E))
        running_t = running.T
        decay_in = jnp.exp2(running)
        decay_out = jnp.exp2(running[length - 1 :] - running)
        dt_wide = spread(dt, expand, heads)
        in_wide = spread(decay_in, expand, heads)
        out_wide = spread(decay_out, expand, heads)
        drun = jnp.zeros((length, 128), F32)
        ddt = jnp.zeros((length, 128), F32)
        for start in range(0, channels, GROUP_LANES):
            lanes = slice(start, start + GROUP_LANES)
            conv_at = slice(channels + start, channels + start + GROUP_LANES)
            at = half_no * channels + start
            wide = slice(at, at + GROUP_LANES)
            table = chan_ref[:, wide]
            xbuf[8:, lanes] = columns_ref[half_no, :, conv_at].astype(F32)
            xbuf[0:8, lanes] = jnp.where(first_block, outside(early_ref[half_no, :, conv_at].astype(F32)[-8:]), halo_ref[half_no, :, conv_at].astype(F32)[-8:])
            c = conv_rows(xbuf[:, lanes], table, length)
            c_sig = sigmoid(c)
            xs = c * c_sig
            z = columns_ref[half_no, :, lanes].astype(F32)
            z_sig = sigmoid(z)
            z_silu = z * z_sig
            y = y_ref[half_no, :, lanes]
            total = y + table[5:6] * xs
            gated = total * z_silu
            up = up_ref[half_no, :, lanes].astype(F32)
            gchan_ref[6:7, wide] += jnp.sum(up * gated, axis=0, keepdims=True)
            dgated = table[6:7] * up - gated * pull
            out_at = half_no * (2 * channels + half + 128) + start
            dcolumns_ref[:, out_at : out_at + GROUP_LANES] = (
                dgated * total * (z_sig + z_silu * (1.0 - z_sig))
            ).astype(BF16)
            dy = dgated * z_silu
            gchan_ref[5:6, wide] += jnp.sum(dy * xs, axis=0, keepdims=True)
            dy_low = dy.astype(BF16)
            dt_lanes = dt_wide[:, lanes]
            values = (xs * dt_lanes).astype(BF16)
            weights, dparts, vparts, decays = [], [], [], []
            for j in range(per_group):
                h = start // width + j
                decay = jnp.exp2(jnp.minimum(running_t[h : h + 1, :] - running[:, h : h + 1], 0.0))
                decays.append(decay)
                weights.append((scores * decay).astype(BF16))
                dparts.append(jnp.where(masks[j], dy_low, jnp.zeros_like(dy_low)))
                vparts.append(jnp.where(masks[j], values, jnp.zeros_like(values)))
            outer = mm(jnp.concatenate(vparts, axis=0), dy_low, NT)
            for j in range(per_group):
                dscores = dscores + outer[j * length : (j + 1) * length] * decays[j]
            dvalues = mm(jnp.concatenate(weights, axis=1), jnp.concatenate(dparts, axis=0))
            before = saved_ref[half_no, 0, :, lanes]
            dafter = dstate[:, wide]
            dafter_low = dafter.astype(BF16)
            out_lanes = out_wide[:, lanes]
            carried = mm(keys, dafter_low) * out_lanes
            dvalues = dvalues + carried
            values_f = values.astype(F32)
            dkeys = dkeys + mm((values_f * out_lanes).astype(BF16), dafter_low, NT)
            in_lanes = in_wide[:, lanes]
            dy_in = (dy * in_lanes).astype(BF16)
            dqueries = dqueries + mm(dy_in, before, NT)
            end_decay = in_lanes[length - 1 :]
            at_end = jnp.sum(values_f * carried, axis=0, keepdims=True) + end_decay * jnp.sum(
                before.astype(F32) * dafter, axis=0, keepdims=True
            )
            dstate[:, wide] = end_decay * dafter + mm(queries, dy_in, TN)
            turn = dy_low.astype(F32) * y - values_f * dvalues + jnp.where(last_row, at_end, 0.0)
            turn_high = turn.astype(BF16)
            turn_low = (turn - turn_high.astype(F32)).astype(BF16)
            group_expand = expand[:, lanes]
            drun = drun + mm(turn_high, group_expand, NT) + mm(turn_low, group_expand, NT)
            ddt = ddt + mm((dvalues * xs).astype(BF16), group_expand, NT)
            dxs = dvalues * dt_lanes + table[5:6] * dy
            dc = dxs * (c_sig + xs * (1.0 - c_sig))
            dxbuf[0:length, wide] = dc
            window = dxbuf[:, wide]
            here = xbuf[8:, lanes]
            gchan_ref[4:5, wide] += jnp.sum(dc, axis=0, keepdims=True)
            gchan_ref[3:4, wide] += jnp.sum(dc * here, axis=0, keepdims=True)
            dconv = table[3:4] * dc
            for ahead in range(1, 4):
                moved = pltpu.roll(window, length + 8 - ahead, 0)[:length]
                gchan_ref[3 - ahead : 4 - ahead, wide] += jnp.sum(moved * here, axis=0, keepdims=True)
                dconv = dconv + table[3 - ahead : 4 - ahead] * moved
            out_at = out_at + channels
            dcolumns_ref[:, out_at : out_at + GROUP_LANES] = dconv.astype(BF16)
            dxbuf[length:, wide] = dxbuf[0:8, wide]

        drate = sum(mm(tri, piece, TN) for piece in split3(drun))
        dstep = (ddt + drate * head[1:2]) * sigmoid(step)
        ghead_ref[8 * half_no : 8 * half_no + 1] += jnp.sum(dstep, axis=0, keepdims=True)
        ghead_ref[8 * half_no + 1 : 8 * half_no + 2] += jnp.sum(drate * rate, axis=0, keepdims=True)
        out_at = half_no * (2 * channels + half + 128) + 2 * channels + half
        dcolumns_ref[:, out_at : out_at + 128] = jnp.where(lane < heads, dstep, 0.0).astype(BF16)

    dscores_low = jnp.where(keep, dscores, 0.0).astype(BF16)
    dkeys = dkeys + mm(dscores_low, queries)
    dqueries = dqueries + mm(dscores_low, keys, TN)
    dbc = jnp.concatenate([dkeys, dqueries], axis=1) * (bc_sig + bc_in * bc_sig * (1.0 - bc_sig))
    dsbuf[0:length] = dbc
    window = dsbuf[...]
    here = sbuf[8:]
    gtaps_ref[4:5] += jnp.sum(dbc, axis=0, keepdims=True)
    gtaps_ref[3:4] += jnp.sum(dbc * here, axis=0, keepdims=True)
    dshared = taps[3:4] * dbc
    for ahead in range(1, 4):
        moved = pltpu.roll(window, length + 8 - ahead, 0)[:length]
        gtaps_ref[3 - ahead : 4 - ahead] += jnp.sum(moved * here, axis=0, keepdims=True)
        dshared = dshared + taps[3 - ahead : 4 - ahead] * moved
    for half_no in range(2):
        out_at = half_no * (2 * channels + half + 128) + 2 * channels
        dcolumns_ref[:, out_at : out_at + half] = dshared[:, half_no * half : (half_no + 1) * half].astype(BF16)
    dsbuf[length:] = dsbuf[0:8]
    dtail_ref[...] = dxbuf[0:8]
    dstail_ref[...] = dsbuf[0:8]


def scan_tables(heads, channels):
    row = lax.broadcasted_iota(jnp.int32, (128, channels), 0) % heads
    col = lax.broadcasted_iota(jnp.int32, (128, channels), 1) // (channels // heads)
    return (row == col).astype(BF16), jnp.tril(jnp.ones((CHUNK, CHUNK), BF16))


def whole(array):
    return pl.BlockSpec(array.shape, lambda i: (0,) * array.ndim)


def last_rows(array, count):
    at = array.shape[1] // count - 1
    return pl.BlockSpec((2, count, array.shape[2]), lambda i: (0, at, 0))


def unread(arrays):
    return [pl.BlockSpec(memory_space=pl.ANY) for _ in arrays]


def mixer_forward(columns, small, tables, heads, earlier=None):
    _, tokens, channels = columns.shape
    channels = channels // 2
    shared = tables[1].shape[1]
    blocks = tokens // CHUNK

    def rows(cols):
        return pl.BlockSpec((2, CHUNK, cols), lambda i: (0, i, 0))

    operands = [columns, small, *tables]
    specs = [rows(2 * channels), rows(small.shape[2])] + [whole(table) for table in tables]
    if earlier is not None:
        operands += list(earlier)
        specs += [whole(earlier[0]), last_rows(earlier[1], 16), last_rows(earlier[2], 8)]
    return pl.pallas_call(
        functools.partial(forward_kernel, earlier is None, heads),
        grid=(blocks,),
        in_specs=specs,
        out_specs=[
            rows(channels),
            pl.BlockSpec((CHUNK, 1), lambda i: (i, 0)),
            rows(channels),
            pl.BlockSpec((2, 1, shared // 2, channels), lambda i: (0, i, 0, 0)),
            pl.BlockSpec((shared // 2, 2 * channels), lambda i: (0, 0)),
        ],
        out_shape=[
            jax.ShapeDtypeStruct((2, tokens, channels), BF16),
            jax.ShapeDtypeStruct((tokens, 1), F32),
            jax.ShapeDtypeStruct((2, tokens, channels), F32),
            jax.ShapeDtypeStruct((2, blocks, shared // 2, channels), BF16),
            jax.ShapeDtypeStruct((shared // 2, 2 * channels), F32),
        ],
        scratch_shapes=[
            pltpu.VMEM((CHUNK + 8, 2 * channels), F32),
            pltpu.VMEM((CHUNK + 8, shared), F32),
        ],
        compiler_params=pltpu.CompilerParams(vmem_limit_bytes=48 * 1024 * 1024),
        cost_estimate=pl.CostEstimate(
            flops=tokens * channels * 3000, bytes_accessed=tokens * channels * 8, transcendentals=tokens * channels * 3
        ),
        name="mixer_forward",
    )(*operands)


def mixer_backward(columns, small, y, saved, up, pull, tables, heads, early, carried, after=()):
    _, tokens, channels = y.shape
    shared = tables[1].shape[1]
    blocks = tokens // CHUNK
    thin = small.shape[2]

    def rows(cols):
        return pl.BlockSpec((2, CHUNK, cols), lambda i: (0, blocks - 1 - i, 0))

    def flat_rows(cols):
        return pl.BlockSpec((CHUNK, cols), lambda i: (blocks - 1 - i, 0))

    def halo(count, cols):
        per_block = CHUNK // count
        return pl.BlockSpec((2, count, cols), lambda i: (0, jnp.maximum((blocks - 1 - i) * per_block - 1, 0), 0))

    def fixed(r, c):
        return pl.BlockSpec((r, c), lambda i: (0, 0))

    saved_spec = pl.BlockSpec((2, 1, shared // 2, channels), lambda i: (0, blocks - 1 - i, 0, 0))
    before = (columns, small) if early is None else early
    operands = [columns, small, y, saved, up, pull, *tables, columns, small, *before]
    specs = [rows(2 * channels), rows(thin), rows(channels), saved_spec, rows(channels), flat_rows(1)]
    specs += [whole(table) for table in tables] + [halo(16, 2 * channels), halo(8, thin)]
    specs += [last_rows(before[0], 16), last_rows(before[1], 8)]
    if carried is not None:
        operands += list(carried)
        specs += [whole(array) for array in carried]
    operands += list(after)
    specs += unread(after)
    fixed_shapes = [(shared // 2, 2 * channels), (8, 2 * channels), (8, shared), (8, 2 * channels), (8, shared), (16, 128)]
    return pl.pallas_call(
        functools.partial(backward_kernel, early is None, carried is None, heads),
        grid=(blocks,),
        in_specs=specs,
        out_specs=[flat_rows(4 * channels + 2 * thin)] + [fixed(*shape) for shape in fixed_shapes],
        out_shape=[jax.ShapeDtypeStruct((tokens, 4 * channels + 2 * thin), BF16)]
        + [jax.ShapeDtypeStruct(shape, F32) for shape in fixed_shapes],
        scratch_shapes=[
            pltpu.VMEM((CHUNK + 8, channels), F32),
            pltpu.VMEM((CHUNK + 8, shared), F32),
            pltpu.VMEM((CHUNK + 8, 2 * channels), F32),
            pltpu.VMEM((CHUNK + 8, shared), F32),
        ],
        compiler_params=pltpu.CompilerParams(vmem_limit_bytes=56 * 1024 * 1024),
        cost_estimate=pl.CostEstimate(
            flops=tokens * channels * 6000, bytes_accessed=tokens * channels * 10, transcendentals=tokens * channels * 3
        ),
        name="mixer_backward",
    )(*operands)


def product_call(kernel, grid, specs, outs, out_specs, operands, flops, name):
    moved = flops // 2048
    return pl.pallas_call(
        kernel,
        grid=grid,
        in_specs=specs,
        out_specs=out_specs,
        out_shape=outs,
        compiler_params=pltpu.CompilerParams(vmem_limit_bytes=60 * 1024 * 1024),
        cost_estimate=pl.CostEstimate(flops=flops // 3, bytes_accessed=moved, transcendentals=0),
        name=name,
    )(*operands)


def in_projection(normed, gathered, own, thin):
    tokens, features = normed.shape

    def kernel(normed_ref, main_ref, thin_ref, columns_ref, small_ref):
        rows = normed_ref[...]
        columns_ref[0] = mm(rows, main_ref[...]).astype(BF16)

        @pl.when(pl.program_id(1) == 0)
        def _():
            small_ref[0] = mm(rows, thin_ref[...])

    return product_call(
        kernel,
        (2, 2),
        [
            pl.BlockSpec((tokens, features), lambda s, n: (0, 0)),
            pl.BlockSpec((features, own), lambda s, n: (s, 1 + n)),
            pl.BlockSpec((features, thin), lambda s, n: (s, 3 * own // thin)),
        ],
        [jax.ShapeDtypeStruct((2, tokens, 2 * own), BF16), jax.ShapeDtypeStruct((2, tokens, thin), F32)],
        [
            pl.BlockSpec((1, tokens, own), lambda s, n: (s, 0, n)),
            pl.BlockSpec((1, tokens, thin), lambda s, n: (s, 0, 0)),
        ],
        (normed, gathered, gathered),
        4 * tokens * features * (2 * own + thin),
        "in_projection",
    )


def out_projection(mixed, gathered, own):
    _, tokens, _ = mixed.shape
    features = gathered.shape[0] // 2
    tile = min(512, features)
    tiles = features // tile

    def kernel(mixed_ref, first_ref, second_ref, share_ref):
        share_ref[...] = (mm(mixed_ref[0], first_ref[...], NT) + mm(mixed_ref[1], second_ref[...], NT)).astype(BF16)

    return product_call(
        kernel,
        (tiles,),
        [
            pl.BlockSpec((2, tokens, own), lambda n: (0, 0, 0)),
            pl.BlockSpec((tile, own), lambda n: (n, 0)),
            pl.BlockSpec((tile, own), lambda n: (tiles + n, 0)),
        ],
        jax.ShapeDtypeStruct((tokens, features), BF16),
        pl.BlockSpec((tokens, tile), lambda n: (0, n)),
        (mixed, gathered, gathered),
        4 * tokens * features * own,
        "out_projection",
    )


def mixed_gradient(up, gathered, own, mixed):
    tokens, features = up.shape

    def kernel(up_ref, weight_ref, mixed_ref, grad_ref, pull_ref):
        grad = mm(up_ref[...], weight_ref[...])
        grad_ref[0] = grad.astype(BF16)
        pull = jnp.sum(grad * mixed_ref[0].astype(F32), axis=1, keepdims=True)

        @pl.when(pl.program_id(0) == 0)
        def _():
            pull_ref[...] = pull

        @pl.when(pl.program_id(0) == 1)
        def _():
            pull_ref[...] += pull

    return product_call(
        kernel,
        (2,),
        [
            pl.BlockSpec((tokens, features), lambda s: (0, 0)),
            pl.BlockSpec((features, own), lambda s: (s, 0)),
            pl.BlockSpec((1, tokens, own), lambda s: (s, 0, 0)),
        ],
        [jax.ShapeDtypeStruct((2, tokens, own), BF16), jax.ShapeDtypeStruct((tokens, 1), F32)],
        [pl.BlockSpec((1, tokens, own), lambda s: (s, 0, 0)), pl.BlockSpec((tokens, 1), lambda s: (0, 0))],
        (up, gathered, mixed),
        4 * tokens * features * own,
        "mixed_gradient",
    )


def normed_gradient(dcolumns, gathered, own, thin):
    tokens, columns = dcolumns.shape
    features = gathered.shape[0] // 2
    tile = min(512, features)
    tiles = features // tile

    def kernel(dcolumns_ref, *refs):
        total, at = 0.0, 0
        for ref in refs[:-1]:
            total = total + mm(dcolumns_ref[:, at : at + ref.shape[1]], ref[...], NT)
            at += ref.shape[1]
        refs[-1][...] = total.astype(BF16)

    specs = [pl.BlockSpec((tokens, columns), lambda n: (0, 0))]
    for shard in range(2):
        specs.append(pl.BlockSpec((tile, own), lambda n, s=shard: (s * tiles + n, 1)))
        specs.append(pl.BlockSpec((tile, own), lambda n, s=shard: (s * tiles + n, 2)))
        specs.append(pl.BlockSpec((tile, thin), lambda n, s=shard: (s * tiles + n, 3 * own // thin)))
    return product_call(
        kernel,
        (tiles,),
        specs,
        jax.ShapeDtypeStruct((tokens, features), BF16),
        pl.BlockSpec((tokens, tile), lambda n: (0, n)),
        (dcolumns,) + (gathered,) * 6,
        2 * tokens * features * columns,
        "normed_gradient",
    )


def stacked_product(lhs, rhs, block=None):
    tokens, features = lhs[0].shape
    chunks = len(lhs)
    split = rhs[0].ndim == 3
    columns = rhs[0].shape[-1] if split else rhs[0].shape[1] // 2
    row_tile, core = (min(256, features), jnp.zeros((1,), jnp.int32)) if block is None else block
    stride = 1 if block is None else 2
    steps = features // (row_tile * stride)

    def kernel(core_ref, *refs):
        out_ref = refs[-1]
        for shard in range(2):
            total = 0.0
            for at in range(chunks):
                ref = refs[chunks + at]
                part = ref[shard] if split else ref[:, shard * columns : (shard + 1) * columns]
                total = total + mm(refs[at][...], part, TN)
            out_ref[shard] = total.astype(BF16)

    return pl.pallas_call(
        kernel,
        grid_spec=pltpu.PrefetchScalarGridSpec(
            num_scalar_prefetch=1,
            grid=(steps,),
            in_specs=[pl.BlockSpec((tokens, row_tile), lambda m, core_ref: (0, stride * m + core_ref[0]))] * chunks
            + [pl.BlockSpec(part.shape, lambda m, core_ref, n=part.ndim: (0,) * n) for part in rhs],
            out_specs=pl.BlockSpec((2, row_tile, columns), lambda m, core_ref: (0, m, 0)),
        ),
        out_shape=jax.ShapeDtypeStruct((2, steps * row_tile, columns), BF16),
        compiler_params=pltpu.CompilerParams(vmem_limit_bytes=60 * 1024 * 1024),
        cost_estimate=pl.CostEstimate(
            flops=steps * row_tile * columns * tokens * chunks,
            bytes_accessed=steps * row_tile * columns,
            transcendentals=0,
        ),
        name="stacked_product",
    )(core, *lhs, *rhs)


class Where:
    def __init__(self, chips, groups):
        self.chips, self.groups = chips, groups
        self.dp, self.tensor = lax.axis_index("dp"), lax.axis_index("tensor")
        self.chip, self.core = self.dp // 2, self.dp % 2
        self.shard, self.group = self.tensor % 2, self.tensor // 2

    def other_core(self):
        return (self.dp + 1 - 2 * self.core, self.tensor)

    def pair(self):
        return (self.dp, self.tensor + 1 - 2 * self.shard)

    def chip_at(self, chip):
        return (chip * 2 + self.core, self.tensor)

    def chip_hop(self, hop):
        return self.chip_at((self.chip + hop) % self.chips)

    def group_hop(self, hop):
        return (self.dp, (self.group + hop) % self.groups * 2 + self.shard)

    def meet(self):
        partners = [self.other_core(), self.pair()]
        partners += [self.chip_hop(hop) for hop in range(1, self.chips)]
        partners += [self.group_hop(hop) for hop in range(1, self.groups)]
        barrier = pltpu.get_barrier_semaphore()
        for partner in partners:
            pl.semaphore_signal(barrier, inc=1, device_id=partner, device_id_type=MESH)
        pl.semaphore_wait(barrier, len(partners))


def remote(src, dst, send_sem, recv_sem, device):
    return pltpu.make_async_remote_copy(
        src_ref=src, dst_ref=dst, send_sem=send_sem, recv_sem=recv_sem, device_id=device, device_id_type=MESH
    )


def gather_kernel(chips, groups, block_ref, hidden_ref, all_ref, stream_ref, left_sem, right_sem, pair_sem, core_sem,
                  chain_recv, pair_recv, core_recv, hidden_send, hidden_recv, local_sem):
    at = Where(chips, groups)
    at.meet()
    mine = pltpu.make_async_copy(block_ref, all_ref.at[at.shard, at.dp], local_sem.at[0])
    mine.start()
    rows = pltpu.make_async_copy(hidden_ref.at[at.shard], stream_ref.at[at.tensor], local_sem.at[1])
    rows.start()

    def hidden_copies():
        slot = stream_ref.at[at.tensor]
        copies = [remote(hidden_ref.at[1 - at.shard], slot, hidden_send.at[0], hidden_recv.at[at.tensor], at.pair())]
        for hop in range(1, groups):
            copies.append(
                remote(hidden_ref.at[at.shard], slot, hidden_send.at[hop], hidden_recv.at[at.tensor], at.group_hop(hop))
            )
        return copies

    def hidden_passed():
        other = at.tensor + 1 - 2 * at.shard
        slot = stream_ref.at[other]
        return [
            remote(slot, slot, hidden_send.at[groups - 1 + hop], hidden_recv.at[other], at.group_hop(hop))
            for hop in range(1, groups)
        ]

    def source(chip):
        return chip * 2 + at.core

    def own_or(chip):
        return all_ref.at[at.shard, source(chip)]

    def to_left(chip, src):
        return remote(src, own_or(chip), left_sem.at[chip], chain_recv.at[chip], at.chip_at(jnp.maximum(at.chip - 1, 0)))

    def to_right(chip, src):
        neighbour = at.chip_at(jnp.minimum(at.chip + 1, chips - 1))
        return remote(src, own_or(chip), right_sem.at[chip], chain_recv.at[chip], neighbour)

    def to_pair(chip, src):
        return remote(src, own_or(chip), pair_sem.at[chip], pair_recv.at[chip], at.pair())

    def to_core(shard, chip, src):
        place = all_ref.at[shard, source(chip)]
        return remote(src, place, core_sem.at[shard, chip], core_recv.at[shard, chip], at.other_core())

    has_left, has_right = at.chip > 0, at.chip < chips - 1
    for copy in hidden_copies():
        copy.start()
    to_pair(at.chip, block_ref).start()

    @pl.when(has_left)
    def _():
        to_left(at.chip, block_ref).start()

    @pl.when(has_right)
    def _():
        to_right(at.chip, block_ref).start()

    to_core(at.shard, at.chip, block_ref).start()

    def from_left(step):
        chip = jnp.maximum(at.chip - step, 0)
        return at.chip >= step, chip

    def from_right(step):
        chip = jnp.minimum(at.chip + step, chips - 1)
        return at.chip + step < chips, chip

    for step in range(1, chips):
        there, chip = from_left(step)

        @pl.when(there)
        def _():
            block = own_or(chip)
            to_right(chip, block).wait_recv()

            @pl.when(has_right)
            def _():
                to_right(chip, block).start()

            to_pair(chip, block).start()
            to_core(at.shard, chip, block).start()

        there, chip = from_right(step)

        @pl.when(there)
        def _():
            block = own_or(chip)
            to_left(chip, block).wait_recv()

            @pl.when(has_left)
            def _():
                to_left(chip, block).start()

            to_pair(chip, block).start()
            to_core(at.shard, chip, block).start()

        if step == 1:
            hidden_copies()[0].wait_send()
            other = at.tensor + 1 - 2 * at.shard
            arrived = stream_ref.at[other]
            remote(arrived, arrived, hidden_send.at[0], hidden_recv.at[other], at.pair()).wait_recv()
            for copy in hidden_passed():
                copy.start()

    def pair_block(chip):
        return all_ref.at[1 - at.shard, source(chip)]

    def pass_pair(chip):
        block = pair_block(chip)
        remote(block, block, pair_sem.at[chip], pair_recv.at[chip], at.pair()).wait_recv()
        to_core(1 - at.shard, chip, block).start()

    pass_pair(at.chip)
    for step in range(1, chips):
        there, chip = from_left(step)

        @pl.when(there)
        def _():
            pass_pair(chip)

        there, chip = from_right(step)

        @pl.when(there)
        def _():
            pass_pair(chip)

    mine.wait()
    rows.wait()
    for copy in hidden_copies()[1:]:
        copy.wait_send()
    for copy in hidden_passed():
        copy.wait_send()
    for hop in range(1, groups):
        for shard in range(2):
            member = (at.group + hop) % groups * 2 + shard
            arrived = stream_ref.at[member]
            remote(arrived, arrived, hidden_send.at[0], hidden_recv.at[member], at.pair()).wait_recv()
    far_core = 1 - at.core
    for chip in range(chips):
        block = own_or(chip)
        to_pair(chip, block).wait_send()
        for shard in range(2):
            to_core(shard, chip, all_ref.at[shard, source(chip)]).wait_send()
            arrived = all_ref.at[shard, chip * 2 + far_core]
            remote(arrived, arrived, core_sem.at[shard, chip], core_recv.at[shard, chip], at.other_core()).wait_recv()

        @pl.when(has_right & (at.chip >= chip))
        def _():
            to_right(chip, block).wait_send()

        @pl.when(has_left & (at.chip <= chip))
        def _():
            to_left(chip, block).wait_send()


def gathered_first(place, block, hidden):
    chips, groups, members = place.chips, place.groups, place.members
    anywhere = pl.BlockSpec(memory_space=pl.ANY)
    dma = pltpu.SemaphoreType.DMA
    both, stream = pl.pallas_call(
        functools.partial(gather_kernel, chips, groups),
        in_specs=[anywhere] * 2,
        out_specs=[anywhere] * 2,
        out_shape=[
            jax.ShapeDtypeStruct((2, 2 * chips) + block.shape, BF16),
            jax.ShapeDtypeStruct((members,) + hidden.shape[1:], BF16),
        ],
        scratch_shapes=[
            dma((chips,)), dma((chips,)), dma((chips,)), dma((2, chips)),
            dma((chips,)), dma((chips,)), dma((2, chips)),
            dma((2 * groups,)), dma((members,)), dma((2,)),
        ],
        compiler_params=pltpu.CompilerParams(collective_id=1, has_side_effects=True),
        cost_estimate=pl.CostEstimate(flops=0, bytes_accessed=300 * 1024 * 1024, transcendentals=0),
        name="gathered_first",
    )(block, hidden)
    return both.reshape(-1, block.shape[1]), stream.reshape(-1, hidden.shape[2])


def reduce_kernel(chips, groups, orders, parts, *refs):
    lhs, rhs, halves_ref, common_ref = refs[:parts], refs[parts : 2 * parts], refs[2 * parts], refs[2 * parts + 1]
    (out_ref, half_out, common_out, pair_out, pair_in, own, chain_in, half_buf, half_in, common_buf, common_in,
     pair_send, pair_recv, chain_send, chain_recv, half_send, half_recv, common_send, common_recv) = refs[2 * parts + 2 :]
    rows, columns = out_ref.shape
    tile = columns // 2 if columns % 256 == 0 else columns
    at = Where(chips, groups)
    at.meet()

    stages = [[at.other_core()], [at.pair()], [at.chip_hop(hop) for hop in range(1, chips)]]
    stages.append([at.group_hop(hop) for hop in range(1, groups)])
    firsts = [sum(len(stage) for stage in stages[:no]) for no in range(4)]

    def small_copies(stage):
        copies = []
        for step, device in enumerate(stages[stage]):
            slot = firsts[stage] + step
            copies.append(
                remote(common_buf.at[stage], common_in.at[slot], common_send.at[slot], common_recv.at[slot], device)
            )
            if stage == 0:
                for shard in range(2):
                    copies.append(
                        remote(half_buf.at[0, shard], half_in.at[shard], half_send.at[shard], half_recv.at[shard], device)
                    )
            elif stage == 1:
                copies.append(
                    remote(half_buf.at[1, 1 - at.shard], half_in.at[2], half_send.at[2], half_recv.at[2], device)
                )
            elif stage == 2:
                copies.append(
                    remote(half_buf.at[2, 0], half_in.at[3 + step], half_send.at[3 + step], half_recv.at[3 + step], device)
                )
        return copies

    def small_start(stage):
        for copy in small_copies(stage):
            copy.start()

    def small_finish(stage):
        for copy in small_copies(stage):
            copy.wait()
        total = common_buf[stage]
        for step in range(len(stages[stage])):
            total = total + common_in[firsts[stage] + step]
        if stage < 3:
            common_buf[stage + 1] = total
        else:
            common_out[...] = total
        if stage == 0:
            for shard in range(2):
                half_buf[1, shard] = half_buf[0, shard] + half_in[shard]
        elif stage == 1:
            half_buf[2, 0] = jnp.where(at.shard == 0, half_buf[1, 0], half_buf[1, 1]) + half_in[2]
        elif stage == 2:
            total = half_buf[2, 0]
            for step in range(chips - 1):
                total = total + half_in[3 + step]
            half_out[...] = total
        if stage < 3:
            small_start(stage + 1)

    half_buf[0] = halves_ref[...]
    common_buf[0] = common_ref[...]
    small_start(0)

    def target(step):
        chip = 0
        for number, order in enumerate(orders):
            chip = chip + jnp.where(at.chip == number, order[step], 0)
        return chip

    def pair_copy(step):
        return remote(pair_out.at[step], pair_in.at[step], pair_send.at[step], pair_recv.at[step], at.pair())

    def chain_copy(step):
        chip = target(step)
        right = chip > at.chip
        neighbour = jnp.clip(jnp.where(right, at.chip + 1, at.chip - 1), 0, chips - 1)
        slot = jnp.where(right | (neighbour != chip), chip, chips)
        return remote(pair_out.at[step], chain_in.at[slot], chain_send.at[step], chain_recv.at[slot], at.chip_at(neighbour))

    def arrival(slot):
        block = chain_in.at[slot]
        return remote(block, block, chain_send.at[0], chain_recv.at[slot], at.pair())

    def multiply(step):
        chip = target(step)
        features = pl.ds(pl.multiple_of((2 * chip + at.core) * rows, 128), rows)

        def product(column):
            total = 0.0
            for part in range(parts):
                total = total + mm(lhs[part][:, features], rhs[part][:, pl.ds(column, tile)], TN)
            return total

        @pl.loop(0, columns // tile)
        def _(tile_no):
            first = pl.multiple_of(tile_no * tile, 128)
            column = pl.multiple_of((1 - at.shard) * columns + first, 128)
            pair_out[step, :, pl.ds(first, tile)] = product(column).astype(BF16)

        pair_copy(step).start()

        @pl.loop(0, columns // tile)
        def _(tile_no):
            first = pl.multiple_of(tile_no * tile, 128)
            column = pl.multiple_of(at.shard * columns + first, 128)
            own[step % 3, :, pl.ds(first, tile)] = product(column)

    def in_tiles(body):
        @pl.loop(0, columns // 128)
        def _(tile_no):
            body(pl.ds(pl.multiple_of(tile_no * 128, 128), 128))

    def add_to_own(step, block, slot):
        def body(lanes):
            own[step % 3, :, lanes] = own[step % 3, :, lanes] + block[slot, :, lanes].astype(F32)

        in_tiles(body)

    def pass_on(step):
        pair_copy(step).wait()
        add_to_own(step, pair_in, step)
        chip = target(step)
        if step < chips - 1:

            @pl.when(((chip > at.chip) & (at.chip > 0)) | ((chip < at.chip) & (at.chip < chips - 1)))
            def _():
                arrival(chip).wait_recv()
                add_to_own(step, chain_in, chip)

            def body(lanes):
                pair_out[step, :, lanes] = own[step % 3, :, lanes].astype(BF16)

            in_tiles(body)
            chain_copy(step).start()
        else:

            @pl.when(at.chip > 0)
            def _():
                arrival(at.chip).wait_recv()
                add_to_own(step, chain_in, at.chip)

            @pl.when(at.chip < chips - 1)
            def _():
                arrival(chips).wait_recv()
                add_to_own(step, chain_in, chips)

            def body(lanes):
                out_ref[:, lanes] = own[step % 3, :, lanes]

            in_tiles(body)

    for step in range(chips):
        multiply(step)
        if step >= 2:
            pass_on(step - 2)
        if step < 3:
            small_finish(step)
    for stage in range(chips, 3):
        small_finish(stage)
    for step in range(max(0, chips - 2), chips):
        pass_on(step)
    small_finish(3)
    for step in range(chips - 1):
        chain_copy(step).wait_send()


def reduced_product(place, lhs, rhs, halves, common, number):
    chips, groups = place.chips, place.groups
    rows, columns = lhs[0].shape[1] // (2 * chips), rhs[0].shape[1] // 2
    orders = []
    for chip in range(chips):
        due = {to: chip + chips - 1 - to if to > chip else chips - 1 - chip + to for to in range(chips) if to != chip}
        orders.append(sorted(due, key=due.get) + [chip])
    parts = len(lhs)
    slots = 1 + 1 + (chips - 1) + (groups - 1)
    vmem = pl.BlockSpec(memory_space=pltpu.VMEM)
    dma = pltpu.SemaphoreType.DMA
    half = halves.shape[1:]
    return pl.pallas_call(
        functools.partial(reduce_kernel, chips, groups, orders, parts),
        in_specs=[vmem] * (2 * parts + 2),
        out_specs=[vmem] * 3,
        out_shape=[
            jax.ShapeDtypeStruct((rows, columns), F32),
            jax.ShapeDtypeStruct(half, F32),
            jax.ShapeDtypeStruct(common.shape, F32),
        ],
        scratch_shapes=[
            pltpu.VMEM((chips, rows, columns), BF16),
            pltpu.VMEM((chips, rows, columns), BF16),
            pltpu.VMEM((3, rows, columns), F32),
            pltpu.VMEM((chips + 1, rows, columns), BF16),
            pltpu.VMEM((3, 2) + half, F32),
            pltpu.VMEM((2 + chips,) + half, F32),
            pltpu.VMEM((4,) + common.shape, F32),
            pltpu.VMEM((slots,) + common.shape, F32),
            dma((chips,)), dma((chips,)), dma((chips,)), dma((chips + 1,)),
            dma((2 + chips,)), dma((2 + chips,)), dma((slots,)), dma((slots,)),
        ],
        compiler_params=pltpu.CompilerParams(
            collective_id=2 + number, has_side_effects=True, vmem_limit_bytes=60 * 1024 * 1024
        ),
        cost_estimate=pl.CostEstimate(
            flops=24 * chips * rows * columns * parts * lhs[0].shape[0], bytes_accessed=100 * 1024 * 1024, transcendentals=0
        ),
        name="reduced_product",
    )(*lhs, *rhs, halves, common)


class Place:
    def __init__(self):
        self.last = ()
        self.due = []
        self.members = lax.axis_size("tensor")
        self.groups = self.members // 2
        self.sequence = lax.axis_index("tensor") % 2
        self.group = lax.axis_index("tensor") // 2
        self.chips = lax.axis_size("dp") // 2
        self.chip = lax.axis_index("dp") // 2
        self.core = lax.axis_index("dp") % 2
        copies = lax.axis_size("dp")
        self.owners = [
            [d * self.members + 2 * g + s for s in range(2) for d in range(copies)] for g in range(self.groups)
        ]

    def now(self, v):
        return lax.optimization_barrier((v, self.last, tuple(self.due)))[0]

    def did(self, v):
        self.last, self.due = (v,), []
        return v

    def soon(self, v):
        self.due.append(v)
        return v

    def to_pair(self, v):
        return lax.ppermute(v, "tensor", [(t, t ^ 1) for t in range(self.members)])

    def to_group(self, v, hop):
        return lax.ppermute(v, "tensor", [(t, (t + 2 * hop) % self.members) for t in range(self.members)])

    def to_core(self, v):
        return lax.ppermute(v, "dp", [(t, t ^ 1) for t in range(2 * self.chips)])

    def to_chip(self, v, hop):
        count = 2 * self.chips
        return lax.ppermute(v, "dp", [(t, (t + 2 * hop) % count) for t in range(count)])

    def gather_owners(self, v):
        return lax.all_gather(v, ("dp", "tensor"), axis=0, axis_index_groups=self.owners, tiled=True)

    def add_groups(self, v):
        return v + sum(self.to_group(v, hop) for hop in range(1, self.groups))

    def sent_to_groups(self, v):
        return [self.to_group(v, hop) for hop in range(1, self.groups)]

    def both(self, v, axis):
        other = self.to_pair(v)
        return jnp.where(
            self.sequence == 0, jnp.concatenate([v, other], axis=axis), jnp.concatenate([other, v], axis=axis)
        )

    def rows_of(self, chunks, hop):
        at = (self.group + hop) % self.groups
        if len(chunks) == self.groups == 2:
            return jnp.where(at == 0, chunks[0], chunks[1])
        total = jnp.concatenate(chunks)
        count = total.shape[0] // self.groups
        return lax.dynamic_slice_in_dim(total, at * count, count, 0)

    def gather_chunks(self, v, chunks):
        if chunks == self.groups == 2:
            other = self.to_group(v, 1)
            return lambda: [jnp.where(self.group == at, v, self.now(other)) for at in range(2)]
        count = v.shape[0]
        total = jnp.zeros((count * self.groups,) + v.shape[1:], v.dtype)
        total = lax.dynamic_update_slice_in_dim(total, v, self.group * count, 0)
        for hop in range(1, self.groups):
            start = (self.group - hop) % self.groups * count
            total = lax.dynamic_update_slice_in_dim(total, self.to_group(v, hop), start, 0)
        return lambda: jnp.split(self.now(total), chunks)

    def take_sequence(self, v):
        mine = jnp.where(self.sequence == 0, v[0], v[1])
        return mine, self.to_pair(jnp.where(self.sequence == 0, v[1], v[0]))

    def in_order(self, mine, other):
        return jnp.where(self.sequence == 0, jnp.concatenate([mine, other]), jnp.concatenate([other, mine]))

    def give_sequence(self, v):
        first, second = jnp.split(v.astype(BF16), 2)
        mine = jnp.where(self.sequence == 0, first, second)
        other = self.to_pair(jnp.where(self.sequence == 0, second, first))
        return mine, other

    def both_sequences(self, given):
        mine, other = self.now(given)
        mine, other = mine.astype(F32), other.astype(F32)
        return jnp.where(self.sequence == 0, jnp.stack([mine, other]), jnp.stack([other, mine]))


def then(v, *earlier):
    return lax.optimization_barrier((v, earlier))[0]


def added(v, arrived):
    return v.astype(F32) + sum(piece.astype(F32) for piece in arrived)


class WeightSum:

    def __init__(self, place, features, columns, far_features=None, far_columns=None):
        self.place = place
        self.lhs = list(features) + (far_features or [place.to_core(part) for part in features])
        self.rhs = list(columns) + (far_columns or [place.to_core(part) for part in columns])

    def to_pair(self):
        place = self.place
        rows = self.lhs[0].shape[1] // (2 * place.chips)
        lhs = list(place.now(tuple(self.lhs)))
        self.stack = place.did(stacked_product(lhs, self.rhs, (rows, place.core.astype(jnp.int32)[None])))
        other = place.soon(lax.dynamic_index_in_dim(self.stack, 1 - place.sequence, 0, keepdims=False))
        self.landed = place.to_pair(other)

    def to_chips(self):
        place = self.place
        own = lax.dynamic_index_in_dim(self.stack, place.sequence, 0, keepdims=False)
        total = (own.astype(F32) + place.now(self.landed).astype(F32)).astype(BF16)
        pieces = total.reshape(place.chips, -1, total.shape[1])
        self.kept = lax.dynamic_index_in_dim(pieces, place.chip, 0, keepdims=False)
        hops = range(1, place.chips)
        self.sent = [
            lax.dynamic_index_in_dim(pieces, (place.chip + hop) % place.chips, 0, keepdims=False) for hop in hops
        ]
        self.arrived = [place.to_chip(place.soon(piece), hop) for piece, hop in zip(self.sent, hops)]

    def total(self):
        return added(self.kept, self.place.now(tuple(self.arrived)))


def norm_rows(row_args, fixed_args, outs, kernel, name, choice=None):
    tokens = row_args[0].shape[0]
    block = min(128, tokens)

    def by_rows(cols):
        return pl.BlockSpec((block, cols), lambda i, *_: (i, 0))

    def fixed(shape):
        return pl.BlockSpec(shape, lambda i, *_: (0, 0))

    scalars = [] if choice is None else [choice]
    return pl.pallas_call(
        kernel,
        grid_spec=pltpu.PrefetchScalarGridSpec(
            num_scalar_prefetch=len(scalars),
            grid=(tokens // block,),
            in_specs=[by_rows(array.shape[1]) for array in row_args] + [fixed(array.shape) for array in fixed_args],
            out_specs=[by_rows(shape[1]) if shape[0] == tokens else fixed(shape) for shape, _ in outs],
        ),
        out_shape=[jax.ShapeDtypeStruct(shape, dtype) for shape, dtype in outs],
        compiler_params=pltpu.CompilerParams(vmem_limit_bytes=48 * 1024 * 1024),
        cost_estimate=pl.CostEstimate(
            flops=20 * row_args[0].size, bytes_accessed=sum(array.size * array.dtype.itemsize for array in row_args), transcendentals=0
        ),
        name=name,
    )(*scalars, *row_args, *fixed_args)


def normed_rows(stream, gain):
    row_scale = lax.rsqrt(jnp.mean(stream * stream, axis=1, keepdims=True) + EPSILON)
    return stream * row_scale, row_scale


def norm_forward(stream, gain, share=None, arrived=(), scale=None):
    shape = stream.shape

    def plain(stream_ref, gain_ref, normed_ref):
        normed_ref[...] = (normed_rows(stream_ref[...].astype(F32), None)[0] * gain_ref[...]).astype(BF16)

    def updated(*refs):
        stream_ref, scale_ref, share_ref = refs[:3]
        gain_ref, out_ref, normed_ref = refs[-3:]
        update = share_ref[...].astype(F32)
        for ref in refs[3:-3]:
            update = update + ref[...].astype(F32)
        rows = stream_ref[...].astype(F32) + update * scale_ref[...]
        out_ref[...] = rows
        normed_ref[...] = (normed_rows(rows, None)[0] * gain_ref[...]).astype(BF16)

    if share is None:
        return stream, norm_rows([stream], [gain], [(shape, BF16)], plain, "norm_forward")[0]
    outs = [(shape, F32), (shape, BF16)]
    return norm_rows([stream, scale, share, *arrived], [gain], outs, updated, "norm_forward")


def norm_backward(streams, grads, share, arrived, gain, choice=None, entry=None, inner=None):
    features = gain.shape[1]
    tokens = share.shape[0]
    pick = 0 if choice is None else 1
    scale, parts = entry if entry else (None, ())

    def kernel(*refs):
        choice_ref, refs = (refs[0], refs[1:]) if pick else (None, refs)

        def chosen(pair):
            return pair[0][...].astype(F32) if not pick else jnp.where(choice_ref[0] == 0, pair[0][...].astype(F32), pair[1][...].astype(F32))

        count = 1 + pick
        stream, grad = chosen(refs[:count]), chosen(refs[count : 2 * count])
        refs = refs[2 * count :]
        grad_normed = refs[0][...].astype(F32)
        for ref in refs[1 : 1 + len(arrived)]:
            grad_normed = grad_normed + ref[...].astype(F32)
        refs = refs[1 + len(arrived) :]
        if entry:
            scale_ref, part_refs, refs = refs[0], refs[1 : 1 + len(parts)], refs[1 + len(parts) :]
        gain_ref, grad_ref, sum_ref = refs[:3]
        unit, row_scale = normed_rows(stream, None)
        lifted = grad_normed * gain_ref[...]
        grad = grad + row_scale * (lifted - unit * jnp.mean(lifted * unit, axis=1, keepdims=True))
        grad_ref[...] = grad

        @pl.when(pl.program_id(0) == 0)
        def _():
            sum_ref[...] = jnp.zeros_like(sum_ref)

        sum_ref[0:1] += jnp.sum(grad_normed * unit, axis=0, keepdims=True)
        if entry:
            up_ref, pull_ref = refs[3:5]
            row = scale_ref[...]
            up = (grad * row).astype(BF16)
            up_ref[...] = up
            update = sum(ref[...].astype(F32) for ref in part_refs)
            pull_ref[...] = jnp.sum(up.astype(F32) * update, axis=1, keepdims=True) * (row * row / inner)

    outs = [((tokens, features), F32), ((8, features), F32)]
    rows = [*streams, *grads, share, *arrived]
    if entry:
        outs += [((tokens, features), BF16), ((tokens, 1), F32)]
        rows += [scale, *parts]
    return norm_rows(rows, [gain], outs, kernel, "norm_backward", choice)


class Forward:
    def __init__(self, place, weights, tables, heads, inner):
        self.place, self.weights, self.tables, self.heads, self.inner = place, weights, tables, heads, inner
        self.kept = {}
        self.earlier = None

    def keep(self, **values):
        for key, value in values.items():
            self.kept.setdefault(key, []).append(value)

    def chunk(self, stream, normed):
        place, (gathered, _, own, thin) = self.place, self.weights
        columns, small = in_projection(place.now(normed), gathered, own, thin)
        mixed, square, y, saved, state = mixer_forward(columns, small, self.tables, self.heads, self.earlier)
        self.earlier = (state, columns, small)
        squares = [square] + place.sent_to_groups(square)
        share = place.did(out_projection(place.now(mixed), gathered, own))
        self.keep(stream=stream, normed=normed, columns=columns, small=small, mixed=mixed, y=y, saved=saved)
        self.keep(squares=squares, share=share, sent=place.sent_to_groups(share))

    def scale(self, at):
        if "scale" not in self.kept:
            self.kept["scale"] = [None] * PIECES
        if self.kept["scale"][at] is None:
            square = sum(self.place.now(tuple(self.kept["squares"][at])))
            self.kept["scale"][at] = lax.rsqrt(square / self.inner + EPSILON)
        return self.kept["scale"][at]


class Backward:
    def __init__(self, place, weights, tables, heads, inner, kept):
        self.place, self.weights, self.tables, self.heads, self.inner, self.kept = place, weights, tables, heads, inner, kept
        self.ups, self.grad_mixed, self.pulls = [None] * PIECES, [None] * PIECES, [None] * PIECES
        self.dcolumns, self.shares = [None] * PIECES, [None] * PIECES
        self.carried = None

    def enter(self, at, up, pull=None):
        gathered, _, own, _ = self.weights
        self.ups[at] = up
        self.grad_mixed[at], sums = mixed_gradient(self.place.now(up), gathered, own, self.kept["mixed"][at])
        self.place.did(self.grad_mixed[at])
        self.pulls[at] = [sums] + self.place.sent_to_groups(sums) if pull is None else pull

    def mix(self, at):
        kept, place = self.kept, self.place
        pull = self.pulls[at]
        if isinstance(pull, list):
            scale = kept["scale"][at]
            pull = sum(place.now(tuple(pull))) * (scale * scale / self.inner)
        result = mixer_backward(
            kept["columns"][at],
            kept["small"][at],
            kept["y"][at],
            kept["saved"][at],
            self.grad_mixed[at],
            place.now(pull),
            self.tables,
            self.heads,
            (kept["columns"][at - 1], kept["small"][at - 1]) if at else None,
            self.carried,
        )
        self.dcolumns[at], self.carried = place.did(result[0]), result[1:]

    def share(self, columns):
        gathered, _, own, thin = self.weights
        return self.place.did(normed_gradient(self.place.now(columns), gathered, own, thin))


def local(
    hidden,
    cotangent,
    norm_gain,
    in_weights,
    state_weight,
    step_weight,
    channel_taps,
    state_taps,
    step_bias,
    decay_log,
    skip_gain,
    inner_gain,
    out_weight,
):
    place = Place()
    layers = in_weights.shape[0]
    rows = in_weights.shape[2]
    heads = step_bias.shape[1]
    own_cols = in_weights.shape[3]
    width = own_cols // heads
    inner = own_cols * place.members
    shared = state_weight.shape[2]
    half = shared // 2
    copies = 128 // heads
    main = 2 * own_cols
    expand, tri = scan_tables(heads, own_cols)

    weights = []
    for layer in range(layers):
        if layer == 1:
            in_weights = then(in_weights, gathered)
        state_half = lax.dynamic_slice_in_dim(state_weight[layer], place.sequence * half, half, 1)
        thin = [step_weight[layer]] * 2
        blank = jnp.zeros((rows, 127 - 2 * heads), BF16)
        block = [out_weight[layer].T, in_weights[layer, 0], in_weights[layer, 1], state_half, *thin, blank]
        block = jnp.concatenate(block + [norm_gain[layer][:, None]], axis=1)
        if layer:
            gathered = place.gather_owners(block)
        else:
            gathered, sequence_rows = gathered_first(place, block, hidden)
        gain = gathered[: gathered.shape[0] // 2, -1].astype(F32)[None]
        weights.append((gathered, gain, own_cols, half + 128))

    per_channel = place.both(jnp.concatenate([channel_taps, inner_gain[:, None]], axis=1), 2)
    per_head = jnp.stack([step_bias, decay_log, skip_gain], axis=1)
    per_head = place.both(per_head[:, None], 1)
    tables = []
    for layer in range(layers):
        wide_skip = jnp.repeat(per_head[layer, :, 2].reshape(-1), width)[None]
        blank = jnp.zeros((1, main), F32)
        chan = jnp.concatenate([per_channel[layer, :5], wide_skip, per_channel[layer, 5:6], blank], axis=0)
        taps = jnp.concatenate([state_taps[layer], jnp.zeros((3, shared), F32)], axis=0)
        head = []
        for part in range(2):
            pair = jnp.stack([per_head[layer, part, 0], -jnp.exp(per_head[layer, part, 1])])
            pair = jnp.concatenate([pair, pair, jnp.zeros((2, 128 - 2 * heads), F32)], axis=1)
            head += [pair, jnp.zeros((6, 128), F32)]
        tables.append((chan, taps, jnp.concatenate(head), expand, tri))

    rows_in = jnp.split(sequence_rows, PIECES)
    kept = []
    for layer in range(layers):
        final = layer == layers - 1
        gathered, gain = weights[layer][:2]
        if layer:
            weights[layer] = (place.now(gathered),) + weights[layer][1:]
            before = kept[-1]
            for at in range(PIECES):
                place.soon(previous.scale(at))
        forward = Forward(place, weights[layer], tables[layer], heads, inner)
        for at in range(PIECES):
            if layer:
                landed = list(place.now(tuple(before["sent"][at])))
                before.setdefault("update", []).append([before["share"][at], *landed])
                stream, normed = norm_forward(
                    before["stream"][at], gain, before["share"][at], landed, previous.scale(at)
                )
            else:
                stream, normed = norm_forward(place.now(rows_in[at]), gain)
            if final and at == 0:
                taken = place.take_sequence(then(cotangent, normed))
            forward.chunk(stream, normed)
            if final and at == 0:
                last_up = place.gather_chunks(place.in_order(*place.now(taken)), PIECES)
        kept.append(forward.kept)
        previous = forward
    for at in range(PIECES):
        previous.scale(at)
    shares = kept[-1]["share"]
    mixed_sent = [place.to_group(place.soon(place.rows_of(shares, hop)), hop) for hop in range(1, place.groups)]
    grads = last_up()
    in_sums, out_sums, gain_grads, carried = [None] * layers, [None] * layers, [0.0] * layers, [None] * layers
    half_totals, common_totals = [None] * layers, [None] * layers
    pending = None

    def small_sums(layer):
        gchan, gtaps, ghead = carried[layer]
        blank = jnp.zeros((1, own_cols - 256), F32)
        parts = []
        for part in range(2):
            per_head_row = jnp.concatenate([ghead[8 * part : 8 * part + 1], ghead[8 * part + 1 : 8 * part + 2], blank], axis=1)
            parts.append(jnp.concatenate([gchan[:7, part * own_cols : (part + 1) * own_cols], per_head_row]))
        return jnp.stack(parts), gtaps

    for layer in reversed(range(layers)):
        final = layer == layers - 1
        back = Backward(place, weights[layer], tables[layer], heads, inner, kept[layer])
        for at in reversed(range(PIECES)):
            scale = kept[layer]["scale"][at]
            if final:
                back.enter(at, (grads[at].astype(F32) * scale).astype(BF16))
                continue
            share, arrived = pending[at]
            grads[at], gain_grad, up, pull = norm_backward(
                [kept[layer + 1]["stream"][at]],
                [grads[at]],
                share,
                list(place.now(tuple(arrived))),
                weights[layer + 1][1],
                None,
                (scale, kept[layer]["update"][at]),
                inner,
            )
            gain_grads[layer + 1] = gain_grads[layer + 1] + jnp.where(place.group == 0, gain_grad[0], 0.0)
            back.enter(at, up, pull)
        normed, mixed = kept[layer]["normed"], kept[layer]["mixed"]
        out_sum = out_sums[layer] = WeightSum(place, back.ups, mixed)
        far_normed = [place.to_core(part) for part in normed]
        out_sum.to_pair()
        far_columns, pending = [None] * PIECES, [None] * PIECES
        for at in reversed(range(PIECES)):
            back.mix(at)
            far_columns[at] = place.to_core(back.dcolumns[at])
            if at == PIECES - 1:
                for later in out_sums[layer + 1 :]:
                    later.owned = later.total()
            if layer:
                share = back.share(back.dcolumns[at])
                pending[at] = (share, place.sent_to_groups(share))
                if at == PIECES - 1:
                    out_sum.to_chips()
        carried[layer] = back.carried[3:]
        in_sum = in_sums[layer] = WeightSum(place, normed, back.dcolumns, far_normed, far_columns)
        if layer:
            halves, common = small_sums(layer)
            in_sum.owned, half_totals[layer], common_totals[layer] = reduced_product(
                place, in_sum.lhs, in_sum.rhs, place.now(halves), common, layer
            )
            place.did(in_sum.owned)
            if final:
                own_rows = place.rows_of(kept[-1]["stream"], 0).astype(F32)
                update = added(place.rows_of(shares, 0), place.now(tuple(mixed_sent)))
                mixed_out = place.give_sequence(own_rows + update * place.rows_of(kept[-1]["scale"], 0))
            continue
        mixed_out = place.both_sequences(mixed_out)
        if PIECES == place.groups:
            sent = [back.share(place.rows_of(back.dcolumns, hop)) for hop in range(1, place.groups)]
            arrived = [place.to_group(piece, hop) for hop, piece in enumerate(sent, 1)]
            own = back.share(place.rows_of(back.dcolumns, 0))
        else:
            done = [back.share(columns) for columns in back.dcolumns]
            arrived = [place.to_group(place.rows_of(done, hop), hop) for hop in range(1, place.groups)]
            own = place.rows_of(done, 0)
        out_sum.to_chips()
        stream_parts, grad_parts, choice = kept[layer]["stream"], grads, place.group.astype(jnp.int32)[None]
        if PIECES != place.groups:
            stream_parts, grad_parts, choice = [place.rows_of(stream_parts, 0)], [place.rows_of(grads, 0)], None
        arrived = list(place.now(tuple(arrived)))
        grad, gain_grad = norm_backward(stream_parts, grad_parts, own, arrived, weights[layer][1], choice)
        place.did(grad)
        gain_grads[layer] = gain_grad[0]
    grad_hidden = place.give_sequence(grad)

    halves, common = small_sums(0)
    gains = jnp.stack(gain_grads).reshape(-1, shared)
    common = jnp.concatenate([common, gains, jnp.zeros((-gains.shape[0] % 8, shared), F32)])
    common = then(place.now(common), *out_sums[0].sent)
    in_sums[0].owned, half_totals[0], common_totals[0] = reduced_product(
        place, in_sum.lhs, in_sum.rhs, halves, common, 0
    )
    place.did(in_sums[0].owned)
    out_sums[0].owned = out_sums[0].total()
    gain_total = common_totals[0][8 : 8 + gains.shape[0]].reshape(layers, -1)

    state_parts = jnp.concatenate([in_sum.owned[:, main : main + half] for in_sum in in_sums])
    state_parts = place.both(place.add_groups(place.now(state_parts)), 1).reshape(layers, rows, shared)
    outs = []
    for layer in range(layers):
        per_channel_part = half_totals[layer]
        gain_part = lax.dynamic_slice_in_dim(gain_total[layer], lax.axis_index("dp") * rows, rows, 0)
        taps_part = common_totals[layer][:5]
        in_owned, out_owned = in_sums[layer].owned, out_sums[layer].owned
        outs.append(
            (
                gain_part,
                jnp.stack([in_owned[:, :own_cols], in_owned[:, own_cols:main]]),
                state_parts[layer],
                in_owned[:, main + half : main + half + heads],
                per_channel_part[:5],
                taps_part,
                per_channel_part[7, :heads],
                per_channel_part[7, 128 : 128 + heads],
                per_channel_part[5].reshape(heads, width).sum(axis=1),
                per_channel_part[6],
                out_owned.T,
            )
        )
    grad_hidden = place.both_sequences(grad_hidden)
    return (mixed_out, grad_hidden) + tuple(jnp.stack(parts) for parts in zip(*outs))


def solution(mesh):
    placed = (
        P("dp", "tensor", None),
        P("dp", "tensor", None),
        P(None, "dp"),
        P(None, None, "dp", "tensor"),
        P(None, "dp", None),
        P(None, "dp", "tensor"),
        P(None, None, "tensor"),
        P(),
        P(None, "tensor"),
        P(None, "tensor"),
        P(None, "tensor"),
        P(None, "tensor"),
        P(None, "tensor", "dp"),
    )
    return jax.shard_map(
        local,
        mesh=mesh,
        in_specs=placed,
        out_specs=(
            P("dp", "tensor", None),
            P("dp", "tensor", None),
            P(None, "dp"),
            P(None, None, "dp", "tensor"),
            P(None, "dp", None),
            P(None, "dp", "tensor"),
            P(None, None, "tensor"),
            P(),
            P(None, "tensor"),
            P(None, "tensor"),
            P(None, "tensor"),
            P(None, "tensor"),
            P(None, "tensor", "dp"),
        ),
        check_vma=False,
    )
```

```python
import functools

import jax
import jax.numpy as jnp
from jax import lax
from jax.experimental import pallas as pl
from jax.experimental.pallas import tpu as pltpu
from jax.sharding import PartitionSpec as P

EPSILON = 1e-05
CHUNK = 128
PIECES = 2
GROUP_LANES = 256
SMALL_COST = pl.CostEstimate(flops=1000, bytes_accessed=1000, transcendentals=0)
LARGE_COST = pl.CostEstimate(flops=10**11, bytes_accessed=10**8, transcendentals=0)
LOG2E = 1.4426950408889634
F32 = jnp.float32
BF16 = jnp.bfloat16
NN = (((1,), (0,)), ((), ()))
NT = (((1,), (1,)), ((), ()))
MESH = pl.DeviceIdType.MESH
TN = (((0,), (0,)), ((), ()))


def mm(a, b, dims=NN):
    return lax.dot_general(a, b, dims, preferred_element_type=F32)


def sigmoid(v):
    return 0.5 * jnp.tanh(0.5 * v) + 0.5


def softplus(v):
    return jnp.maximum(v, 0.0) + jnp.log(1.0 + jnp.exp(-jnp.abs(v)))


def split3(v):
    high = v.astype(BF16)
    rest = v - high.astype(F32)
    mid = rest.astype(BF16)
    return high, mid, (rest - mid.astype(F32)).astype(BF16)


def spread(v, expand, heads):
    high = v.astype(BF16)
    low = (v - high.astype(F32)).astype(BF16)
    lane = lax.broadcasted_iota(jnp.int32, v.shape, 1)
    parts = jnp.where(lane < heads, high, jnp.where(lane < 2 * heads, low, jnp.zeros_like(low)))
    return mm(parts, expand)


def conv_rows(window, table, length):
    total = table[4:5] + table[3:4] * window[8 : 8 + length]
    for back in range(1, 4):
        total = total + table[3 - back : 4 - back] * pltpu.roll(window, back, 0)[8 : 8 + length]
    return total


def causal(length, flip):
    row = lax.broadcasted_iota(jnp.int32, (length, length), 0)
    col = lax.broadcasted_iota(jnp.int32, (length, length), 1)
    return (row <= col) if flip else (row >= col)


def head_masks(lanes, width):
    lane = lax.broadcasted_iota(jnp.int32, (1, lanes), 1)
    return [(lane >= j * width) & (lane < (j + 1) * width) for j in range(lanes // width)]


def both_halves(ref):
    half = ref.shape[2] - 128
    return jnp.concatenate([ref[0, :, :half], ref[1, :, :half]], axis=1)


def forward_kernel(first, heads, *refs):
    columns_ref, small_ref, chan_ref, taps_ref, head_ref, expand_ref, tri_ref = refs[:7]
    refs = refs[7:]
    if not first:
        start_ref, tail_ref, stail_ref = refs[:3]
    mixed_ref, square_ref, y_ref, saved_ref, state, xbuf, sbuf = refs[-7:]
    length, channels = y_ref.shape[1:]
    width = channels // heads
    shared = taps_ref.shape[1]
    half = shared // 2

    @pl.when(pl.program_id(0) == 0)
    def _():
        if first:
            state[...] = jnp.zeros_like(state)
            xbuf[0:8] = jnp.zeros((8, 2 * channels), F32)
            sbuf[0:8] = jnp.zeros((8, shared), F32)
        else:
            state[...] = start_ref[...]
            for half_no in range(2):
                xbuf[0:8, half_no * channels : (half_no + 1) * channels] = tail_ref[half_no, :, channels:].astype(F32)[-8:]
            sbuf[0:8] = both_halves(stail_ref)

    sbuf[8:] = both_halves(small_ref)
    tri = tri_ref[...]
    expand = expand_ref[...]
    taps = taps_ref[...]
    bc = conv_rows(sbuf[...], taps, length)
    bc = (bc * sigmoid(bc)).astype(BF16)
    keys, queries = bc[:, :half], bc[:, half:]
    scores = jnp.where(causal(length, False), mm(queries, keys, NT), 0.0)
    squares = jnp.zeros((length, 128), F32)
    masks = head_masks(GROUP_LANES, width)
    for half_no in range(2):
        head = head_ref[8 * half_no : 8 * half_no + 8]
        dt = softplus(small_ref[half_no, :, half:] + head[0:1])
        running = sum(mm(tri, piece) for piece in split3(dt * (head[1:2] * LOG2E)))
        running_t = running.T
        decay_in = jnp.exp2(running)
        decay_out = jnp.exp2(running[length - 1 :] - running)
        dt_wide = spread(dt, expand, heads)
        in_wide = spread(decay_in, expand, heads)
        out_wide = spread(dt * decay_out, expand, heads)
        for start in range(0, channels, GROUP_LANES):
            lanes = slice(start, start + GROUP_LANES)
            conv_at = slice(channels + start, channels + start + GROUP_LANES)
            wide = slice(half_no * channels + start, half_no * channels + start + GROUP_LANES)
            table = chan_ref[:, wide]
            xbuf[8:, wide] = columns_ref[half_no, :, conv_at].astype(F32)
            c = conv_rows(xbuf[:, wide], table, length)
            xbuf[0:8, wide] = xbuf[length:, wide]
            xs = c * sigmoid(c)
            values = (xs * dt_wide[:, lanes]).astype(BF16)
            weights, parts = [], []
            for j in range(GROUP_LANES // width):
                h = start // width + j
                gap = jnp.minimum(running[:, h : h + 1] - running_t[h : h + 1, :], 0.0)
                weights.append((scores * jnp.exp2(gap)).astype(BF16))
                parts.append(jnp.where(masks[j], values, jnp.zeros_like(values)))
            before = state[:, wide]
            before_low = before.astype(BF16)
            saved_ref[half_no, 0, :, lanes] = before_low
            y = mm(jnp.concatenate(weights, axis=1), jnp.concatenate(parts, axis=0))
            y = y + mm(queries, before_low) * in_wide[:, lanes]
            y_ref[half_no, :, lanes] = y
            z = columns_ref[half_no, :, lanes].astype(F32)
            gated = (y + table[5:6] * xs) * (z * sigmoid(z))
            mixed_ref[half_no, :, lanes] = (gated * table[6:7]).astype(BF16)
            power = gated * gated
            for at in range(0, GROUP_LANES, 128):
                squares = squares + power[:, at : at + 128]
            fresh = mm(keys, (xs * out_wide[:, lanes]).astype(BF16), TN)
            state[:, wide] = before * in_wide[length - 1 :, lanes] + fresh
    square_ref[...] = jnp.sum(squares, axis=1, keepdims=True)
    sbuf[0:8] = sbuf[length:]


def backward_kernel(first, last, heads, *refs):
    columns_ref, small_ref, y_ref, saved_ref, up_ref, pull_ref = refs[:6]
    chan_ref, taps_ref, head_ref, expand_ref, tri_ref, halo_ref, shalo_ref, early_ref, searly_ref = refs[6:15]
    refs = refs[15:]
    if not last:
        carried_refs = refs[:6]
    dcolumns_ref, dstate, dtail_ref, dstail_ref, gchan_ref, gtaps_ref, ghead_ref, xbuf, sbuf, dxbuf, dsbuf = refs[-11:]
    length, channels = y_ref.shape[1:]
    width = channels // heads
    shared = taps_ref.shape[1]
    half = shared // 2
    step_no = pl.program_id(0)
    first_block = step_no == pl.num_programs(0) - 1

    @pl.when(step_no == 0)
    def _():
        if last:
            dstate[...] = jnp.zeros_like(dstate)
            dxbuf[length:] = jnp.zeros((8, 2 * channels), F32)
            dsbuf[length:] = jnp.zeros((8, shared), F32)
            gchan_ref[...] = jnp.zeros_like(gchan_ref)
            gtaps_ref[...] = jnp.zeros_like(gtaps_ref)
            ghead_ref[...] = jnp.zeros_like(ghead_ref)
        else:
            dstate[...] = carried_refs[0][...]
            dxbuf[length:] = carried_refs[1][...]
            dsbuf[length:] = carried_refs[2][...]
            gchan_ref[...] = carried_refs[3][...]
            gtaps_ref[...] = carried_refs[4][...]
            ghead_ref[...] = carried_refs[5][...]

    def outside(rows):
        return jnp.zeros_like(rows) if first else rows

    sbuf[8:] = both_halves(small_ref)
    sbuf[0:8] = jnp.where(first_block, outside(both_halves(searly_ref)), both_halves(shalo_ref))
    tri = tri_ref[...]
    expand = expand_ref[...]
    taps = taps_ref[...]
    bc_in = conv_rows(sbuf[...], taps, length)
    bc_sig = sigmoid(bc_in)
    bc = (bc_in * bc_sig).astype(BF16)
    keys, queries = bc[:, :half], bc[:, half:]
    keep = causal(length, True)
    scores = jnp.where(keep, mm(keys, queries, NT), 0.0)
    pull = pull_ref[...]
    masks = head_masks(GROUP_LANES, width)
    dscores = jnp.zeros((length, length), F32)
    dkeys = jnp.zeros((length, half), F32)
    dqueries = jnp.zeros((length, half), F32)
    last_row = lax.broadcasted_iota(jnp.int32, (length, 1), 0) == length - 1
    lane = lax.broadcasted_iota(jnp.int32, (length, 128), 1)
    per_group = GROUP_LANES // width
    for half_no in range(2):
        head = head_ref[8 * half_no : 8 * half_no + 8]
        step = small_ref[half_no, :, half:] + head[0:1]
        dt = softplus(step)
        rate = dt * head[1:2]
        running = sum(mm(tri, piece) for piece in split3(rate * LOG2E))
        running_t = running.T
        decay_in = jnp.exp2(running)
        decay_out = jnp.exp2(running[length - 1 :] - running)
        dt_wide = spread(dt, expand, heads)
        in_wide = spread(decay_in, expand, heads)
        out_wide = spread(decay_out, expand, heads)
        drun = jnp.zeros((length, 128), F32)
        ddt = jnp.zeros((length, 128), F32)
        for start in range(0, channels, GROUP_LANES):
            lanes = slice(start, start + GROUP_LANES)
            conv_at = slice(channels + start, channels + start + GROUP_LANES)
            at = half_no * channels + start
            wide = slice(at, at + GROUP_LANES)
            table = chan_ref[:, wide]
            xbuf[8:, lanes] = columns_ref[half_no, :, conv_at].astype(F32)
            xbuf[0:8, lanes] = jnp.where(first_block, outside(early_ref[half_no, :, conv_at].astype(F32)[-8:]), halo_ref[half_no, :, conv_at].astype(F32)[-8:])
            c = conv_rows(xbuf[:, lanes], table, length)
            c_sig = sigmoid(c)
            xs = c * c_sig
            z = columns_ref[half_no, :, lanes].astype(F32)
            z_sig = sigmoid(z)
            z_silu = z * z_sig
            y = y_ref[half_no, :, lanes]
            total = y + table[5:6] * xs
            gated = total * z_silu
            up = up_ref[half_no, :, lanes].astype(F32)
            gchan_ref[6:7, wide] += jnp.sum(up * gated, axis=0, keepdims=True)
            dgated = table[6:7] * up - gated * pull
            out_at = half_no * (2 * channels + half + 128) + start
            dcolumns_ref[:, out_at : out_at + GROUP_LANES] = (
                dgated * total * (z_sig + z_silu * (1.0 - z_sig))
            ).astype(BF16)
            dy = dgated * z_silu
            gchan_ref[5:6, wide] += jnp.sum(dy * xs, axis=0, keepdims=True)
            dy_low = dy.astype(BF16)
            dt_lanes = dt_wide[:, lanes]
            values = (xs * dt_lanes).astype(BF16)
            weights, dparts, vparts, decays = [], [], [], []
            for j in range(per_group):
                h = start // width + j
                decay = jnp.exp2(jnp.minimum(running_t[h : h + 1, :] - running[:, h : h + 1], 0.0))
                decays.append(decay)
                weights.append((scores * decay).astype(BF16))
                dparts.append(jnp.where(masks[j], dy_low, jnp.zeros_like(dy_low)))
                vparts.append(jnp.where(masks[j], values, jnp.zeros_like(values)))
            outer = mm(jnp.concatenate(vparts, axis=0), dy_low, NT)
            for j in range(per_group):
                dscores = dscores + outer[j * length : (j + 1) * length] * decays[j]
            dvalues = mm(jnp.concatenate(weights, axis=1), jnp.concatenate(dparts, axis=0))
            before = saved_ref[half_no, 0, :, lanes]
            dafter = dstate[:, wide]
            dafter_low = dafter.astype(BF16)
            out_lanes = out_wide[:, lanes]
            carried = mm(keys, dafter_low) * out_lanes
            dvalues = dvalues + carried
            values_f = values.astype(F32)
            dkeys = dkeys + mm((values_f * out_lanes).astype(BF16), dafter_low, NT)
            in_lanes = in_wide[:, lanes]
            dy_in = (dy * in_lanes).astype(BF16)
            dqueries = dqueries + mm(dy_in, before, NT)
            end_decay = in_lanes[length - 1 :]
            at_end = jnp.sum(values_f * carried, axis=0, keepdims=True) + end_decay * jnp.sum(
                before.astype(F32) * dafter, axis=0, keepdims=True
            )
            dstate[:, wide] = end_decay * dafter + mm(queries, dy_in, TN)
            turn = dy_low.astype(F32) * y - values_f * dvalues + jnp.where(last_row, at_end, 0.0)
            turn_high = turn.astype(BF16)
            turn_low = (turn - turn_high.astype(F32)).astype(BF16)
            group_expand = expand[:, lanes]
            drun = drun + mm(turn_high, group_expand, NT) + mm(turn_low, group_expand, NT)
            ddt = ddt + mm((dvalues * xs).astype(BF16), group_expand, NT)
            dxs = dvalues * dt_lanes + table[5:6] * dy
            dc = dxs * (c_sig + xs * (1.0 - c_sig))
            dxbuf[0:length, wide] = dc
            window = dxbuf[:, wide]
            here = xbuf[8:, lanes]
            gchan_ref[4:5, wide] += jnp.sum(dc, axis=0, keepdims=True)
            gchan_ref[3:4, wide] += jnp.sum(dc * here, axis=0, keepdims=True)
            dconv = table[3:4] * dc
            for ahead in range(1, 4):
                moved = pltpu.roll(window, length + 8 - ahead, 0)[:length]
                gchan_ref[3 - ahead : 4 - ahead, wide] += jnp.sum(moved * here, axis=0, keepdims=True)
                dconv = dconv + table[3 - ahead : 4 - ahead] * moved
            out_at = out_at + channels
            dcolumns_ref[:, out_at : out_at + GROUP_LANES] = dconv.astype(BF16)
            dxbuf[length:, wide] = dxbuf[0:8, wide]

        drate = sum(mm(tri, piece, TN) for piece in split3(drun))
        dstep = (ddt + drate * head[1:2]) * sigmoid(step)
        ghead_ref[8 * half_no : 8 * half_no + 1] += jnp.sum(dstep, axis=0, keepdims=True)
        ghead_ref[8 * half_no + 1 : 8 * half_no + 2] += jnp.sum(drate * rate, axis=0, keepdims=True)
        out_at = half_no * (2 * channels + half + 128) + 2 * channels + half
        dcolumns_ref[:, out_at : out_at + 128] = jnp.where(lane < heads, dstep, 0.0).astype(BF16)

    dscores_low = jnp.where(keep, dscores, 0.0).astype(BF16)
    dkeys = dkeys + mm(dscores_low, queries)
    dqueries = dqueries + mm(dscores_low, keys, TN)
    dbc = jnp.concatenate([dkeys, dqueries], axis=1) * (bc_sig + bc_in * bc_sig * (1.0 - bc_sig))
    dsbuf[0:length] = dbc
    window = dsbuf[...]
    here = sbuf[8:]
    gtaps_ref[4:5] += jnp.sum(dbc, axis=0, keepdims=True)
    gtaps_ref[3:4] += jnp.sum(dbc * here, axis=0, keepdims=True)
    dshared = taps[3:4] * dbc
    for ahead in range(1, 4):
        moved = pltpu.roll(window, length + 8 - ahead, 0)[:length]
        gtaps_ref[3 - ahead : 4 - ahead] += jnp.sum(moved * here, axis=0, keepdims=True)
        dshared = dshared + taps[3 - ahead : 4 - ahead] * moved
    for half_no in range(2):
        out_at = half_no * (2 * channels + half + 128) + 2 * channels
        dcolumns_ref[:, out_at : out_at + half] = dshared[:, half_no * half : (half_no + 1) * half].astype(BF16)
    dsbuf[length:] = dsbuf[0:8]
    dtail_ref[...] = dxbuf[0:8]
    dstail_ref[...] = dsbuf[0:8]


def scan_tables(heads, channels):
    row = lax.broadcasted_iota(jnp.int32, (128, channels), 0) % heads
    col = lax.broadcasted_iota(jnp.int32, (128, channels), 1) // (channels // heads)
    return (row == col).astype(BF16), jnp.tril(jnp.ones((CHUNK, CHUNK), BF16))


def whole(array):
    return pl.BlockSpec(array.shape, lambda i: (0,) * array.ndim)


def last_rows(array, count):
    at = array.shape[1] // count - 1
    return pl.BlockSpec((2, count, array.shape[2]), lambda i: (0, at, 0))


def unread(arrays):
    return [pl.BlockSpec(memory_space=pl.ANY) for _ in arrays]


def mixer_forward(columns, small, tables, heads, earlier=None):
    _, tokens, channels = columns.shape
    channels = channels // 2
    shared = tables[1].shape[1]
    blocks = tokens // CHUNK

    def rows(cols):
        return pl.BlockSpec((2, CHUNK, cols), lambda i: (0, i, 0))

    operands = [columns, small, *tables]
    specs = [rows(2 * channels), rows(small.shape[2])] + [whole(table) for table in tables]
    if earlier is not None:
        operands += list(earlier)
        specs += [whole(earlier[0]), last_rows(earlier[1], 16), last_rows(earlier[2], 8)]
    return pl.pallas_call(
        functools.partial(forward_kernel, earlier is None, heads),
        grid=(blocks,),
        in_specs=specs,
        out_specs=[
            rows(channels),
            pl.BlockSpec((CHUNK, 1), lambda i: (i, 0)),
            rows(channels),
            pl.BlockSpec((2, 1, shared // 2, channels), lambda i: (0, i, 0, 0)),
            pl.BlockSpec((shared // 2, 2 * channels), lambda i: (0, 0)),
        ],
        out_shape=[
            jax.ShapeDtypeStruct((2, tokens, channels), BF16),
            jax.ShapeDtypeStruct((tokens, 1), F32),
            jax.ShapeDtypeStruct((2, tokens, channels), F32),
            jax.ShapeDtypeStruct((2, blocks, shared // 2, channels), BF16),
            jax.ShapeDtypeStruct((shared // 2, 2 * channels), F32),
        ],
        scratch_shapes=[
            pltpu.VMEM((CHUNK + 8, 2 * channels), F32),
            pltpu.VMEM((CHUNK + 8, shared), F32),
        ],
        compiler_params=pltpu.CompilerParams(vmem_limit_bytes=48 * 1024 * 1024),
        cost_estimate=SMALL_COST,
        name="mixer_forward",
    )(*operands)


def mixer_backward(columns, small, y, saved, up, pull, tables, heads, early, carried, after=()):
    _, tokens, channels = y.shape
    shared = tables[1].shape[1]
    blocks = tokens // CHUNK
    thin = small.shape[2]

    def rows(cols):
        return pl.BlockSpec((2, CHUNK, cols), lambda i: (0, blocks - 1 - i, 0))

    def flat_rows(cols):
        return pl.BlockSpec((CHUNK, cols), lambda i: (blocks - 1 - i, 0))

    def halo(count, cols):
        per_block = CHUNK // count
        return pl.BlockSpec((2, count, cols), lambda i: (0, jnp.maximum((blocks - 1 - i) * per_block - 1, 0), 0))

    def fixed(r, c):
        return pl.BlockSpec((r, c), lambda i: (0, 0))

    saved_spec = pl.BlockSpec((2, 1, shared // 2, channels), lambda i: (0, blocks - 1 - i, 0, 0))
    before = (columns, small) if early is None else early
    operands = [columns, small, y, saved, up, pull, *tables, columns, small, *before]
    specs = [rows(2 * channels), rows(thin), rows(channels), saved_spec, rows(channels), flat_rows(1)]
    specs += [whole(table) for table in tables] + [halo(16, 2 * channels), halo(8, thin)]
    specs += [last_rows(before[0], 16), last_rows(before[1], 8)]
    if carried is not None:
        operands += list(carried)
        specs += [whole(array) for array in carried]
    operands += list(after)
    specs += unread(after)
    fixed_shapes = [(shared // 2, 2 * channels), (8, 2 * channels), (8, shared), (8, 2 * channels), (8, shared), (16, 128)]
    return pl.pallas_call(
        functools.partial(backward_kernel, early is None, carried is None, heads),
        grid=(blocks,),
        in_specs=specs,
        out_specs=[flat_rows(4 * channels + 2 * thin)] + [fixed(*shape) for shape in fixed_shapes],
        out_shape=[jax.ShapeDtypeStruct((tokens, 4 * channels + 2 * thin), BF16)]
        + [jax.ShapeDtypeStruct(shape, F32) for shape in fixed_shapes],
        scratch_shapes=[
            pltpu.VMEM((CHUNK + 8, channels), F32),
            pltpu.VMEM((CHUNK + 8, shared), F32),
            pltpu.VMEM((CHUNK + 8, 2 * channels), F32),
            pltpu.VMEM((CHUNK + 8, shared), F32),
        ],
        compiler_params=pltpu.CompilerParams(vmem_limit_bytes=56 * 1024 * 1024),
        cost_estimate=SMALL_COST,
        name="mixer_backward",
    )(*operands)


def product_call(kernel, grid, specs, outs, out_specs, operands, name, cost=SMALL_COST):
    return pl.pallas_call(
        kernel,
        grid=grid,
        in_specs=specs,
        out_specs=out_specs,
        out_shape=outs,
        compiler_params=pltpu.CompilerParams(vmem_limit_bytes=60 * 1024 * 1024),
        cost_estimate=cost,
        name=name,
    )(*operands)


def in_projection(normed, gathered, own, thin):
    tokens, features = normed.shape

    def kernel(normed_ref, main_ref, thin_ref, columns_ref, small_ref):
        rows = normed_ref[...]
        columns_ref[0] = mm(rows, main_ref[...]).astype(BF16)

        @pl.when(pl.program_id(1) == 0)
        def _():
            small_ref[0] = mm(rows, thin_ref[...])

    return product_call(
        kernel,
        (2, 2),
        [
            pl.BlockSpec((tokens, features), lambda s, n: (0, 0)),
            pl.BlockSpec((features, own), lambda s, n: (s, 1 + n)),
            pl.BlockSpec((features, thin), lambda s, n: (s, 3 * own // thin)),
        ],
        [jax.ShapeDtypeStruct((2, tokens, 2 * own), BF16), jax.ShapeDtypeStruct((2, tokens, thin), F32)],
        [
            pl.BlockSpec((1, tokens, own), lambda s, n: (s, 0, n)),
            pl.BlockSpec((1, tokens, thin), lambda s, n: (s, 0, 0)),
        ],
        (normed, gathered, gathered),
        "in_projection",
    )


def out_projection(mixed, gathered, own):
    _, tokens, _ = mixed.shape
    features = gathered.shape[0] // 2
    tile = min(512, features)
    tiles = features // tile

    def kernel(mixed_ref, first_ref, second_ref, share_ref):
        share_ref[...] = (mm(mixed_ref[0], first_ref[...], NT) + mm(mixed_ref[1], second_ref[...], NT)).astype(BF16)

    return product_call(
        kernel,
        (tiles,),
        [
            pl.BlockSpec((2, tokens, own), lambda n: (0, 0, 0)),
            pl.BlockSpec((tile, own), lambda n: (n, 0)),
            pl.BlockSpec((tile, own), lambda n: (tiles + n, 0)),
        ],
        jax.ShapeDtypeStruct((tokens, features), BF16),
        pl.BlockSpec((tokens, tile), lambda n: (0, n)),
        (mixed, gathered, gathered),
        "out_projection",
    )


def mixed_gradient(up, gathered, own, mixed):
    tokens, features = up.shape

    def kernel(up_ref, weight_ref, mixed_ref, grad_ref, pull_ref):
        grad = mm(up_ref[...], weight_ref[...])
        grad_ref[0] = grad.astype(BF16)
        pull = jnp.sum(grad * mixed_ref[0].astype(F32), axis=1, keepdims=True)

        @pl.when(pl.program_id(0) == 0)
        def _():
            pull_ref[...] = pull

        @pl.when(pl.program_id(0) == 1)
        def _():
            pull_ref[...] += pull

    return product_call(
        kernel,
        (2,),
        [
            pl.BlockSpec((tokens, features), lambda s: (0, 0)),
            pl.BlockSpec((features, own), lambda s: (s, 0)),
            pl.BlockSpec((1, tokens, own), lambda s: (s, 0, 0)),
        ],
        [jax.ShapeDtypeStruct((2, tokens, own), BF16), jax.ShapeDtypeStruct((tokens, 1), F32)],
        [pl.BlockSpec((1, tokens, own), lambda s: (s, 0, 0)), pl.BlockSpec((tokens, 1), lambda s: (0, 0))],
        (up, gathered, mixed),
        "mixed_gradient",
    )


def normed_gradient(dcolumns, gathered, own, thin):
    tokens, columns = dcolumns.shape
    features = gathered.shape[0] // 2
    tile = min(512, features)
    tiles = features // tile

    def kernel(dcolumns_ref, *refs):
        total, at = 0.0, 0
        for ref in refs[:-1]:
            total = total + mm(dcolumns_ref[:, at : at + ref.shape[1]], ref[...], NT)
            at += ref.shape[1]
        refs[-1][...] = total.astype(BF16)

    specs = [pl.BlockSpec((tokens, columns), lambda n: (0, 0))]
    for shard in range(2):
        specs.append(pl.BlockSpec((tile, own), lambda n, s=shard: (s * tiles + n, 1)))
        specs.append(pl.BlockSpec((tile, own), lambda n, s=shard: (s * tiles + n, 2)))
        specs.append(pl.BlockSpec((tile, thin), lambda n, s=shard: (s * tiles + n, 3 * own // thin)))
    return product_call(
        kernel,
        (tiles,),
        specs,
        jax.ShapeDtypeStruct((tokens, features), BF16),
        pl.BlockSpec((tokens, tile), lambda n: (0, n)),
        (dcolumns,) + (gathered,) * 6,
        "normed_gradient",
        LARGE_COST,
    )


def stacked_product(lhs, rhs, block=None):
    tokens, features = lhs[0].shape
    chunks = len(lhs)
    split = rhs[0].ndim == 3
    columns = rhs[0].shape[-1] if split else rhs[0].shape[1] // 2
    row_tile, core = (min(256, features), jnp.zeros((1,), jnp.int32)) if block is None else block
    stride = 1 if block is None else 2
    steps = features // (row_tile * stride)

    def kernel(core_ref, *refs):
        out_ref = refs[-1]
        for shard in range(2):
            total = 0.0
            for at in range(chunks):
                ref = refs[chunks + at]
                part = ref[shard] if split else ref[:, shard * columns : (shard + 1) * columns]
                total = total + mm(refs[at][...], part, TN)
            out_ref[shard] = total.astype(BF16)

    return pl.pallas_call(
        kernel,
        grid_spec=pltpu.PrefetchScalarGridSpec(
            num_scalar_prefetch=1,
            grid=(steps,),
            in_specs=[pl.BlockSpec((tokens, row_tile), lambda m, core_ref: (0, stride * m + core_ref[0]))] * chunks
            + [pl.BlockSpec(part.shape, lambda m, core_ref, n=part.ndim: (0,) * n) for part in rhs],
            out_specs=pl.BlockSpec((2, row_tile, columns), lambda m, core_ref: (0, m, 0)),
        ),
        out_shape=jax.ShapeDtypeStruct((2, steps * row_tile, columns), BF16),
        compiler_params=pltpu.CompilerParams(vmem_limit_bytes=60 * 1024 * 1024),
        cost_estimate=LARGE_COST,
        name="stacked_product",
    )(core, *lhs, *rhs)


class Where:
    def __init__(self, chips, groups):
        self.chips, self.groups = chips, groups
        self.dp, self.tensor = lax.axis_index("dp"), lax.axis_index("tensor")
        self.chip, self.core = self.dp // 2, self.dp % 2
        self.shard, self.group = self.tensor % 2, self.tensor // 2

    def other_core(self):
        return (self.dp + 1 - 2 * self.core, self.tensor)

    def pair(self):
        return (self.dp, self.tensor + 1 - 2 * self.shard)

    def chip_at(self, chip):
        return (chip * 2 + self.core, self.tensor)

    def chip_hop(self, hop):
        return self.chip_at((self.chip + hop) % self.chips)

    def group_hop(self, hop):
        return (self.dp, (self.group + hop) % self.groups * 2 + self.shard)

    def meet(self):
        partners = [self.other_core(), self.pair()]
        partners += [self.chip_hop(hop) for hop in range(1, self.chips)]
        partners += [self.group_hop(hop) for hop in range(1, self.groups)]
        barrier = pltpu.get_barrier_semaphore()
        for partner in partners:
            pl.semaphore_signal(barrier, inc=1, device_id=partner, device_id_type=MESH)
        pl.semaphore_wait(barrier, len(partners))


def remote(src, dst, send_sem, recv_sem, device):
    return pltpu.make_async_remote_copy(
        src_ref=src, dst_ref=dst, send_sem=send_sem, recv_sem=recv_sem, device_id=device, device_id_type=MESH
    )


def gather_kernel(chips, groups, block_ref, hidden_ref, all_ref, stream_ref, left_sem, right_sem, pair_sem, core_sem,
                  chain_recv, pair_recv, core_recv, hidden_send, hidden_recv, local_sem):
    at = Where(chips, groups)
    at.meet()
    mine = pltpu.make_async_copy(block_ref, all_ref.at[at.shard, at.dp], local_sem.at[0])
    mine.start()
    rows = pltpu.make_async_copy(hidden_ref.at[at.shard], stream_ref.at[at.tensor], local_sem.at[1])
    rows.start()

    def hidden_copies():
        slot = stream_ref.at[at.tensor]
        copies = [remote(hidden_ref.at[1 - at.shard], slot, hidden_send.at[0], hidden_recv.at[at.tensor], at.pair())]
        for hop in range(1, groups):
            copies.append(
                remote(hidden_ref.at[at.shard], slot, hidden_send.at[hop], hidden_recv.at[at.tensor], at.group_hop(hop))
            )
        return copies

    def hidden_passed():
        other = at.tensor + 1 - 2 * at.shard
        slot = stream_ref.at[other]
        return [
            remote(slot, slot, hidden_send.at[groups - 1 + hop], hidden_recv.at[other], at.group_hop(hop))
            for hop in range(1, groups)
        ]

    def source(chip):
        return chip * 2 + at.core

    def own_or(chip):
        return all_ref.at[at.shard, source(chip)]

    def to_left(chip, src):
        return remote(src, own_or(chip), left_sem.at[chip], chain_recv.at[chip], at.chip_at(jnp.maximum(at.chip - 1, 0)))

    def to_right(chip, src):
        neighbour = at.chip_at(jnp.minimum(at.chip + 1, chips - 1))
        return remote(src, own_or(chip), right_sem.at[chip], chain_recv.at[chip], neighbour)

    def to_pair(chip, src):
        return remote(src, own_or(chip), pair_sem.at[chip], pair_recv.at[chip], at.pair())

    def to_core(shard, chip, src):
        place = all_ref.at[shard, source(chip)]
        return remote(src, place, core_sem.at[shard, chip], core_recv.at[shard, chip], at.other_core())

    has_left, has_right = at.chip > 0, at.chip < chips - 1
    for copy in hidden_copies():
        copy.start()
    to_pair(at.chip, block_ref).start()

    @pl.when(has_left)
    def _():
        to_left(at.chip, block_ref).start()

    @pl.when(has_right)
    def _():
        to_right(at.chip, block_ref).start()

    to_core(at.shard, at.chip, block_ref).start()

    def from_left(step):
        chip = jnp.maximum(at.chip - step, 0)
        return at.chip >= step, chip

    def from_right(step):
        chip = jnp.minimum(at.chip + step, chips - 1)
        return at.chip + step < chips, chip

    for step in range(1, chips):
        there, chip = from_left(step)

        @pl.when(there)
        def _():
            block = own_or(chip)
            to_right(chip, block).wait_recv()

            @pl.when(has_right)
            def _():
                to_right(chip, block).start()

            to_pair(chip, block).start()
            to_core(at.shard, chip, block).start()

        there, chip = from_right(step)

        @pl.when(there)
        def _():
            block = own_or(chip)
            to_left(chip, block).wait_recv()

            @pl.when(has_left)
            def _():
                to_left(chip, block).start()

            to_pair(chip, block).start()
            to_core(at.shard, chip, block).start()

        if step == 1:
            hidden_copies()[0].wait_send()
            other = at.tensor + 1 - 2 * at.shard
            arrived = stream_ref.at[other]
            remote(arrived, arrived, hidden_send.at[0], hidden_recv.at[other], at.pair()).wait_recv()
            for copy in hidden_passed():
                copy.start()

    def pair_block(chip):
        return all_ref.at[1 - at.shard, source(chip)]

    def pass_pair(chip):
        block = pair_block(chip)
        remote(block, block, pair_sem.at[chip], pair_recv.at[chip], at.pair()).wait_recv()
        to_core(1 - at.shard, chip, block).start()

    pass_pair(at.chip)
    for step in range(1, chips):
        there, chip = from_left(step)

        @pl.when(there)
        def _():
            pass_pair(chip)

        there, chip = from_right(step)

        @pl.when(there)
        def _():
            pass_pair(chip)

    mine.wait()
    rows.wait()
    for copy in hidden_copies()[1:]:
        copy.wait_send()
    for copy in hidden_passed():
        copy.wait_send()
    for hop in range(1, groups):
        for shard in range(2):
            member = (at.group + hop) % groups * 2 + shard
            arrived = stream_ref.at[member]
            remote(arrived, arrived, hidden_send.at[0], hidden_recv.at[member], at.pair()).wait_recv()
    far_core = 1 - at.core
    for chip in range(chips):
        block = own_or(chip)
        to_pair(chip, block).wait_send()
        for shard in range(2):
            to_core(shard, chip, all_ref.at[shard, source(chip)]).wait_send()
            arrived = all_ref.at[shard, chip * 2 + far_core]
            remote(arrived, arrived, core_sem.at[shard, chip], core_recv.at[shard, chip], at.other_core()).wait_recv()

        @pl.when(has_right & (at.chip >= chip))
        def _():
            to_right(chip, block).wait_send()

        @pl.when(has_left & (at.chip <= chip))
        def _():
            to_left(chip, block).wait_send()


def gathered_first(place, block, hidden):
    chips, groups, members = place.chips, place.groups, place.members
    anywhere = pl.BlockSpec(memory_space=pl.ANY)
    dma = pltpu.SemaphoreType.DMA
    both, stream = pl.pallas_call(
        functools.partial(gather_kernel, chips, groups),
        in_specs=[anywhere] * 2,
        out_specs=[anywhere] * 2,
        out_shape=[
            jax.ShapeDtypeStruct((2, 2 * chips) + block.shape, BF16),
            jax.ShapeDtypeStruct((members,) + hidden.shape[1:], BF16),
        ],
        scratch_shapes=[
            dma((chips,)), dma((chips,)), dma((chips,)), dma((2, chips)),
            dma((chips,)), dma((chips,)), dma((2, chips)),
            dma((2 * groups,)), dma((members,)), dma((2,)),
        ],
        compiler_params=pltpu.CompilerParams(collective_id=1, has_side_effects=True),
        cost_estimate=SMALL_COST,
        name="gathered_first",
    )(block, hidden)
    return both.reshape(-1, block.shape[1]), stream.reshape(-1, hidden.shape[2])


def reduce_kernel(chips, groups, orders, parts, *refs):
    lhs, rhs, halves_ref, common_ref = refs[:parts], refs[parts : 2 * parts], refs[2 * parts], refs[2 * parts + 1]
    (out_ref, half_out, common_out, pair_out, pair_in, own, chain_in, half_buf, half_in, common_buf, common_in,
     pair_send, pair_recv, chain_send, chain_recv, half_send, half_recv, common_send, common_recv) = refs[2 * parts + 2 :]
    rows, columns = out_ref.shape
    tile = columns // 2 if columns % 256 == 0 else columns
    at = Where(chips, groups)
    at.meet()

    stages = [[at.other_core()], [at.pair()], [at.chip_hop(hop) for hop in range(1, chips)]]
    stages.append([at.group_hop(hop) for hop in range(1, groups)])
    firsts = [sum(len(stage) for stage in stages[:no]) for no in range(4)]

    def small_copies(stage):
        copies = []
        for step, device in enumerate(stages[stage]):
            slot = firsts[stage] + step
            copies.append(
                remote(common_buf.at[stage], common_in.at[slot], common_send.at[slot], common_recv.at[slot], device)
            )
            if stage == 0:
                for shard in range(2):
                    copies.append(
                        remote(half_buf.at[0, shard], half_in.at[shard], half_send.at[shard], half_recv.at[shard], device)
                    )
            elif stage == 1:
                copies.append(
                    remote(half_buf.at[1, 1 - at.shard], half_in.at[2], half_send.at[2], half_recv.at[2], device)
                )
            elif stage == 2:
                copies.append(
                    remote(half_buf.at[2, 0], half_in.at[3 + step], half_send.at[3 + step], half_recv.at[3 + step], device)
                )
        return copies

    def small_start(stage):
        for copy in small_copies(stage):
            copy.start()

    def small_finish(stage):
        for copy in small_copies(stage):
            copy.wait()
        total = common_buf[stage]
        for step in range(len(stages[stage])):
            total = total + common_in[firsts[stage] + step]
        if stage < 3:
            common_buf[stage + 1] = total
        else:
            common_out[...] = total
        if stage == 0:
            for shard in range(2):
                half_buf[1, shard] = half_buf[0, shard] + half_in[shard]
        elif stage == 1:
            half_buf[2, 0] = jnp.where(at.shard == 0, half_buf[1, 0], half_buf[1, 1]) + half_in[2]
        elif stage == 2:
            total = half_buf[2, 0]
            for step in range(chips - 1):
                total = total + half_in[3 + step]
            half_out[...] = total
        if stage < 3:
            small_start(stage + 1)

    half_buf[0] = halves_ref[...]
    common_buf[0] = common_ref[...]
    small_start(0)

    def target(step):
        chip = 0
        for number, order in enumerate(orders):
            chip = chip + jnp.where(at.chip == number, order[step], 0)
        return chip

    def pair_copy(step):
        return remote(pair_out.at[step], pair_in.at[step], pair_send.at[step], pair_recv.at[step], at.pair())

    def chain_copy(step):
        chip = target(step)
        right = chip > at.chip
        neighbour = jnp.clip(jnp.where(right, at.chip + 1, at.chip - 1), 0, chips - 1)
        slot = jnp.where(right | (neighbour != chip), chip, chips)
        return remote(pair_out.at[step], chain_in.at[slot], chain_send.at[step], chain_recv.at[slot], at.chip_at(neighbour))

    def arrival(slot):
        block = chain_in.at[slot]
        return remote(block, block, chain_send.at[0], chain_recv.at[slot], at.pair())

    def multiply(step):
        chip = target(step)
        features = pl.ds(pl.multiple_of((2 * chip + at.core) * rows, 128), rows)

        def product(column):
            total = 0.0
            for part in range(parts):
                total = total + mm(lhs[part][:, features], rhs[part][:, pl.ds(column, tile)], TN)
            return total

        @pl.loop(0, columns // tile)
        def _(tile_no):
            first = pl.multiple_of(tile_no * tile, 128)
            column = pl.multiple_of((1 - at.shard) * columns + first, 128)
            pair_out[step, :, pl.ds(first, tile)] = product(column).astype(BF16)

        pair_copy(step).start()

        @pl.loop(0, columns // tile)
        def _(tile_no):
            first = pl.multiple_of(tile_no * tile, 128)
            column = pl.multiple_of(at.shard * columns + first, 128)
            own[step % 3, :, pl.ds(first, tile)] = product(column)

    def in_tiles(body):
        @pl.loop(0, columns // 128)
        def _(tile_no):
            body(pl.ds(pl.multiple_of(tile_no * 128, 128), 128))

    def add_to_own(step, block, slot):
        def body(lanes):
            own[step % 3, :, lanes] = own[step % 3, :, lanes] + block[slot, :, lanes].astype(F32)

        in_tiles(body)

    def pass_on(step):
        pair_copy(step).wait()
        add_to_own(step, pair_in, step)
        chip = target(step)
        if step < chips - 1:

            @pl.when(((chip > at.chip) & (at.chip > 0)) | ((chip < at.chip) & (at.chip < chips - 1)))
            def _():
                arrival(chip).wait_recv()
                add_to_own(step, chain_in, chip)

            def body(lanes):
                pair_out[step, :, lanes] = own[step % 3, :, lanes].astype(BF16)

            in_tiles(body)
            chain_copy(step).start()
        else:

            @pl.when(at.chip > 0)
            def _():
                arrival(at.chip).wait_recv()
                add_to_own(step, chain_in, at.chip)

            @pl.when(at.chip < chips - 1)
            def _():
                arrival(chips).wait_recv()
                add_to_own(step, chain_in, chips)

            def body(lanes):
                out_ref[:, lanes] = own[step % 3, :, lanes]

            in_tiles(body)

    for step in range(chips):
        multiply(step)
        if step >= 2:
            pass_on(step - 2)
        if step < 3:
            small_finish(step)
    for stage in range(chips, 3):
        small_finish(stage)
    for step in range(max(0, chips - 2), chips):
        pass_on(step)
    small_finish(3)
    for step in range(chips - 1):
        chain_copy(step).wait_send()


def reduced_product(place, lhs, rhs, halves, common, number):
    chips, groups = place.chips, place.groups
    rows, columns = lhs[0].shape[1] // (2 * chips), rhs[0].shape[1] // 2
    orders = []
    for chip in range(chips):
        due = {to: chip + chips - 1 - to if to > chip else chips - 1 - chip + to for to in range(chips) if to != chip}
        orders.append(sorted(due, key=due.get) + [chip])
    parts = len(lhs)
    slots = 1 + 1 + (chips - 1) + (groups - 1)
    vmem = pl.BlockSpec(memory_space=pltpu.VMEM)
    dma = pltpu.SemaphoreType.DMA
    half = halves.shape[1:]
    return pl.pallas_call(
        functools.partial(reduce_kernel, chips, groups, orders, parts),
        in_specs=[vmem] * (2 * parts + 2),
        out_specs=[vmem] * 3,
        out_shape=[
            jax.ShapeDtypeStruct((rows, columns), F32),
            jax.ShapeDtypeStruct(half, F32),
            jax.ShapeDtypeStruct(common.shape, F32),
        ],
        scratch_shapes=[
            pltpu.VMEM((chips, rows, columns), BF16),
            pltpu.VMEM((chips, rows, columns), BF16),
            pltpu.VMEM((3, rows, columns), F32),
            pltpu.VMEM((chips + 1, rows, columns), BF16),
            pltpu.VMEM((3, 2) + half, F32),
            pltpu.VMEM((2 + chips,) + half, F32),
            pltpu.VMEM((4,) + common.shape, F32),
            pltpu.VMEM((slots,) + common.shape, F32),
            dma((chips,)), dma((chips,)), dma((chips,)), dma((chips + 1,)),
            dma((2 + chips,)), dma((2 + chips,)), dma((slots,)), dma((slots,)),
        ],
        compiler_params=pltpu.CompilerParams(
            collective_id=2 + number, has_side_effects=True, vmem_limit_bytes=60 * 1024 * 1024
        ),
        cost_estimate=LARGE_COST,
        name="reduced_product",
    )(*lhs, *rhs, halves, common)


class Place:
    def __init__(self):
        self.last = ()
        self.due = []
        self.members = lax.axis_size("tensor")
        self.groups = self.members // 2
        self.sequence = lax.axis_index("tensor") % 2
        self.group = lax.axis_index("tensor") // 2
        self.chips = lax.axis_size("dp") // 2
        self.chip = lax.axis_index("dp") // 2
        self.core = lax.axis_index("dp") % 2
        copies = lax.axis_size("dp")
        self.owners = [
            [d * self.members + 2 * g + s for s in range(2) for d in range(copies)] for g in range(self.groups)
        ]

    def now(self, v):
        return lax.optimization_barrier((v, self.last, tuple(self.due)))[0]

    def did(self, v):
        self.last, self.due = (v,), []
        return v

    def soon(self, v):
        self.due.append(v)
        return v

    def to_pair(self, v):
        return lax.ppermute(v, "tensor", [(t, t ^ 1) for t in range(self.members)])

    def to_group(self, v, hop):
        return lax.ppermute(v, "tensor", [(t, (t + 2 * hop) % self.members) for t in range(self.members)])

    def to_core(self, v):
        return lax.ppermute(v, "dp", [(t, t ^ 1) for t in range(2 * self.chips)])

    def to_chip(self, v, hop):
        count = 2 * self.chips
        return lax.ppermute(v, "dp", [(t, (t + 2 * hop) % count) for t in range(count)])

    def scatter_owners(self, v):
        v = v.reshape(-1, v.shape[-1])
        return lax.psum_scatter(v, ("dp", "tensor"), scatter_dimension=0, axis_index_groups=self.owners, tiled=True)

    def gather_owners(self, v):
        return lax.all_gather(v, ("dp", "tensor"), axis=0, axis_index_groups=self.owners, tiled=True)

    def add_groups(self, v):
        return v + sum(self.to_group(v, hop) for hop in range(1, self.groups))

    def sent_to_groups(self, v):
        return [self.to_group(v, hop) for hop in range(1, self.groups)]

    def both(self, v, axis):
        other = self.to_pair(v)
        return jnp.where(
            self.sequence == 0, jnp.concatenate([v, other], axis=axis), jnp.concatenate([other, v], axis=axis)
        )

    def rows_of(self, chunks, hop):
        at = (self.group + hop) % self.groups
        if len(chunks) == self.groups == 2:
            return jnp.where(at == 0, chunks[0], chunks[1])
        total = jnp.concatenate(chunks)
        count = total.shape[0] // self.groups
        return lax.dynamic_slice_in_dim(total, at * count, count, 0)

    def gather_chunks(self, v, chunks):
        if chunks == self.groups == 2:
            other = self.to_group(v, 1)
            return lambda: [jnp.where(self.group == at, v, self.now(other)) for at in range(2)]
        count = v.shape[0]
        total = jnp.zeros((count * self.groups,) + v.shape[1:], v.dtype)
        total = lax.dynamic_update_slice_in_dim(total, v, self.group * count, 0)
        for hop in range(1, self.groups):
            start = (self.group - hop) % self.groups * count
            total = lax.dynamic_update_slice_in_dim(total, self.to_group(v, hop), start, 0)
        return lambda: jnp.split(self.now(total), chunks)

    def take_sequence(self, v):
        mine = jnp.where(self.sequence == 0, v[0], v[1])
        return mine, self.to_pair(jnp.where(self.sequence == 0, v[1], v[0]))

    def in_order(self, mine, other):
        return jnp.where(self.sequence == 0, jnp.concatenate([mine, other]), jnp.concatenate([other, mine]))

    def give_sequence(self, v):
        first, second = jnp.split(v.astype(BF16), 2)
        mine = jnp.where(self.sequence == 0, first, second)
        other = self.to_pair(jnp.where(self.sequence == 0, second, first))
        return mine, other

    def both_sequences(self, given):
        mine, other = self.now(given)
        mine, other = mine.astype(F32), other.astype(F32)
        return jnp.where(self.sequence == 0, jnp.stack([mine, other]), jnp.stack([other, mine]))


def then(v, *earlier):
    return lax.optimization_barrier((v, earlier))[0]


def added(v, arrived):
    return v.astype(F32) + sum(piece.astype(F32) for piece in arrived)


class Owned:
    pass


class WeightSum:

    def __init__(self, place, features, columns, far_features=None, far_columns=None):
        self.place = place
        self.lhs = list(features) + (far_features or [place.to_core(part) for part in features])
        self.rhs = list(columns) + (far_columns or [place.to_core(part) for part in columns])

    def to_pair(self):
        place = self.place
        rows = self.lhs[0].shape[1] // (2 * place.chips)
        lhs = list(place.now(tuple(self.lhs)))
        self.stack = place.did(stacked_product(lhs, self.rhs, (rows, place.core.astype(jnp.int32)[None])))
        other = place.soon(lax.dynamic_index_in_dim(self.stack, 1 - place.sequence, 0, keepdims=False))
        self.landed = place.to_pair(other)

    def to_chips(self):
        place = self.place
        own = lax.dynamic_index_in_dim(self.stack, place.sequence, 0, keepdims=False)
        total = (own.astype(F32) + place.now(self.landed).astype(F32)).astype(BF16)
        pieces = total.reshape(place.chips, -1, total.shape[1])
        self.kept = lax.dynamic_index_in_dim(pieces, place.chip, 0, keepdims=False)
        hops = range(1, place.chips)
        self.sent = [
            lax.dynamic_index_in_dim(pieces, (place.chip + hop) % place.chips, 0, keepdims=False) for hop in hops
        ]
        self.arrived = [place.to_chip(place.soon(piece), hop) for piece, hop in zip(self.sent, hops)]

    def total(self):
        return added(self.kept, self.place.now(tuple(self.arrived)))


def norm_rows(row_args, fixed_args, outs, kernel, name, choice=None):
    tokens = row_args[0].shape[0]
    block = min(128, tokens)

    def by_rows(cols):
        return pl.BlockSpec((block, cols), lambda i, *_: (i, 0))

    def fixed(shape):
        return pl.BlockSpec(shape, lambda i, *_: (0, 0))

    scalars = [] if choice is None else [choice]
    return pl.pallas_call(
        kernel,
        grid_spec=pltpu.PrefetchScalarGridSpec(
            num_scalar_prefetch=len(scalars),
            grid=(tokens // block,),
            in_specs=[by_rows(array.shape[1]) for array in row_args] + [fixed(array.shape) for array in fixed_args],
            out_specs=[by_rows(shape[1]) if shape[0] == tokens else fixed(shape) for shape, _ in outs],
        ),
        out_shape=[jax.ShapeDtypeStruct(shape, dtype) for shape, dtype in outs],
        compiler_params=pltpu.CompilerParams(vmem_limit_bytes=48 * 1024 * 1024),
        cost_estimate=SMALL_COST,
        name=name,
    )(*scalars, *row_args, *fixed_args)


def normed_rows(stream, gain):
    row_scale = lax.rsqrt(jnp.mean(stream * stream, axis=1, keepdims=True) + EPSILON)
    return stream * row_scale, row_scale


def norm_forward(stream, gain, share=None, arrived=(), scale=None):
    shape = stream.shape

    def plain(stream_ref, gain_ref, normed_ref):
        normed_ref[...] = (normed_rows(stream_ref[...].astype(F32), None)[0] * gain_ref[...]).astype(BF16)

    def updated(*refs):
        stream_ref, scale_ref, share_ref = refs[:3]
        gain_ref, out_ref, normed_ref = refs[-3:]
        update = share_ref[...].astype(F32)
        for ref in refs[3:-3]:
            update = update + ref[...].astype(F32)
        rows = stream_ref[...].astype(F32) + update * scale_ref[...]
        out_ref[...] = rows
        normed_ref[...] = (normed_rows(rows, None)[0] * gain_ref[...]).astype(BF16)

    if share is None:
        return stream, norm_rows([stream], [gain], [(shape, BF16)], plain, "norm_forward")[0]
    outs = [(shape, F32), (shape, BF16)]
    return norm_rows([stream, scale, share, *arrived], [gain], outs, updated, "norm_forward")


def norm_backward(streams, grads, share, arrived, gain, choice=None, entry=None, inner=None):
    features = gain.shape[1]
    tokens = share.shape[0]
    pick = 0 if choice is None else 1
    scale, parts = entry if entry else (None, ())

    def kernel(*refs):
        choice_ref, refs = (refs[0], refs[1:]) if pick else (None, refs)

        def chosen(pair):
            return pair[0][...].astype(F32) if not pick else jnp.where(choice_ref[0] == 0, pair[0][...].astype(F32), pair[1][...].astype(F32))

        count = 1 + pick
        stream, grad = chosen(refs[:count]), chosen(refs[count : 2 * count])
        refs = refs[2 * count :]
        grad_normed = refs[0][...].astype(F32)
        for ref in refs[1 : 1 + len(arrived)]:
            grad_normed = grad_normed + ref[...].astype(F32)
        refs = refs[1 + len(arrived) :]
        if entry:
            scale_ref, part_refs, refs = refs[0], refs[1 : 1 + len(parts)], refs[1 + len(parts) :]
        gain_ref, grad_ref, sum_ref = refs[:3]
        unit, row_scale = normed_rows(stream, None)
        lifted = grad_normed * gain_ref[...]
        grad = grad + row_scale * (lifted - unit * jnp.mean(lifted * unit, axis=1, keepdims=True))
        grad_ref[...] = grad

        @pl.when(pl.program_id(0) == 0)
        def _():
            sum_ref[...] = jnp.zeros_like(sum_ref)

        sum_ref[0:1] += jnp.sum(grad_normed * unit, axis=0, keepdims=True)
        if entry:
            up_ref, pull_ref = refs[3:5]
            row = scale_ref[...]
            up = (grad * row).astype(BF16)
            up_ref[...] = up
            update = sum(ref[...].astype(F32) for ref in part_refs)
            pull_ref[...] = jnp.sum(up.astype(F32) * update, axis=1, keepdims=True) * (row * row / inner)

    outs = [((tokens, features), F32), ((8, features), F32)]
    rows = [*streams, *grads, share, *arrived]
    if entry:
        outs += [((tokens, features), BF16), ((tokens, 1), F32)]
        rows += [scale, *parts]
    return norm_rows(rows, [gain], outs, kernel, "norm_backward", choice)


class Forward:
    def __init__(self, place, weights, tables, heads, inner):
        self.place, self.weights, self.tables, self.heads, self.inner = place, weights, tables, heads, inner
        self.kept = {}
        self.earlier = None

    def keep(self, **values):
        for key, value in values.items():
            self.kept.setdefault(key, []).append(value)

    def chunk(self, stream, normed):
        place, (gathered, _, own, thin) = self.place, self.weights
        columns, small = in_projection(place.now(normed), gathered, own, thin)
        mixed, square, y, saved, state = mixer_forward(columns, small, self.tables, self.heads, self.earlier)
        self.earlier = (state, columns, small)
        squares = [square] + place.sent_to_groups(square)
        share = place.did(out_projection(place.now(mixed), gathered, own))
        self.keep(stream=stream, normed=normed, columns=columns, small=small, mixed=mixed, y=y, saved=saved)
        self.keep(squares=squares, share=share, sent=place.sent_to_groups(share))

    def scale(self, at):
        if "scale" not in self.kept:
            self.kept["scale"] = [None] * PIECES
        if self.kept["scale"][at] is None:
            square = sum(self.place.now(tuple(self.kept["squares"][at])))
            self.kept["scale"][at] = lax.rsqrt(square / self.inner + EPSILON)
        return self.kept["scale"][at]


class Backward:
    def __init__(self, place, weights, tables, heads, inner, kept):
        self.place, self.weights, self.tables, self.heads, self.inner, self.kept = place, weights, tables, heads, inner, kept
        self.ups, self.grad_mixed, self.pulls = [None] * PIECES, [None] * PIECES, [None] * PIECES
        self.dcolumns, self.shares = [None] * PIECES, [None] * PIECES
        self.carried = None

    def enter(self, at, up, pull=None):
        gathered, _, own, _ = self.weights
        self.ups[at] = up
        self.grad_mixed[at], sums = mixed_gradient(self.place.now(up), gathered, own, self.kept["mixed"][at])
        self.place.did(self.grad_mixed[at])
        self.pulls[at] = [sums] + self.place.sent_to_groups(sums) if pull is None else pull

    def mix(self, at):
        kept, place = self.kept, self.place
        pull = self.pulls[at]
        if isinstance(pull, list):
            scale = kept["scale"][at]
            pull = sum(place.now(tuple(pull))) * (scale * scale / self.inner)
        result = mixer_backward(
            kept["columns"][at],
            kept["small"][at],
            kept["y"][at],
            kept["saved"][at],
            self.grad_mixed[at],
            place.now(pull),
            self.tables,
            self.heads,
            (kept["columns"][at - 1], kept["small"][at - 1]) if at else None,
            self.carried,
        )
        self.dcolumns[at], self.carried = place.did(result[0]), result[1:]

    def share(self, columns):
        gathered, _, own, thin = self.weights
        return self.place.did(normed_gradient(self.place.now(columns), gathered, own, thin))


def local(
    hidden,
    cotangent,
    norm_gain,
    in_weights,
    state_weight,
    step_weight,
    channel_taps,
    state_taps,
    step_bias,
    decay_log,
    skip_gain,
    inner_gain,
    out_weight,
):
    place = Place()
    layers = in_weights.shape[0]
    rows = in_weights.shape[2]
    heads = step_bias.shape[1]
    own_cols = in_weights.shape[3]
    width = own_cols // heads
    inner = own_cols * place.members
    shared = state_weight.shape[2]
    half = shared // 2
    copies = 128 // heads
    main = 2 * own_cols
    expand, tri = scan_tables(heads, own_cols)

    weights = []
    for layer in range(layers):
        if layer == 1:
            in_weights = then(in_weights, gathered)
        state_half = lax.dynamic_slice_in_dim(state_weight[layer], place.sequence * half, half, 1)
        thin = [step_weight[layer]] * 2
        blank = jnp.zeros((rows, 127 - 2 * heads), BF16)
        block = [out_weight[layer].T, in_weights[layer, 0], in_weights[layer, 1], state_half, *thin, blank]
        block = jnp.concatenate(block + [norm_gain[layer][:, None]], axis=1)
        if layer:
            gathered = place.gather_owners(block)
        else:
            gathered, sequence_rows = gathered_first(place, block, hidden)
        gain = gathered[: gathered.shape[0] // 2, -1].astype(F32)[None]
        weights.append((gathered, gain, own_cols, half + 128))

    per_channel = place.both(jnp.concatenate([channel_taps, inner_gain[:, None]], axis=1), 2)
    per_head = jnp.stack([step_bias, decay_log, skip_gain], axis=1)
    per_head = place.both(per_head[:, None], 1)
    tables = []
    for layer in range(layers):
        wide_skip = jnp.repeat(per_head[layer, :, 2].reshape(-1), width)[None]
        blank = jnp.zeros((1, main), F32)
        chan = jnp.concatenate([per_channel[layer, :5], wide_skip, per_channel[layer, 5:6], blank], axis=0)
        taps = jnp.concatenate([state_taps[layer], jnp.zeros((3, shared), F32)], axis=0)
        head = []
        for part in range(2):
            pair = jnp.stack([per_head[layer, part, 0], -jnp.exp(per_head[layer, part, 1])])
            pair = jnp.concatenate([pair, pair, jnp.zeros((2, 128 - 2 * heads), F32)], axis=1)
            head += [pair, jnp.zeros((6, 128), F32)]
        tables.append((chan, taps, jnp.concatenate(head), expand, tri))

    rows_in = jnp.split(sequence_rows, PIECES)
    kept = []
    for layer in range(layers):
        final = layer == layers - 1
        gathered, gain = weights[layer][:2]
        if layer:
            weights[layer] = (place.now(gathered),) + weights[layer][1:]
            before = kept[-1]
            for at in range(PIECES):
                place.soon(previous.scale(at))
        forward = Forward(place, weights[layer], tables[layer], heads, inner)
        for at in range(PIECES):
            if layer:
                landed = list(place.now(tuple(before["sent"][at])))
                before.setdefault("update", []).append([before["share"][at], *landed])
                stream, normed = norm_forward(
                    before["stream"][at], gain, before["share"][at], landed, previous.scale(at)
                )
            else:
                stream, normed = norm_forward(place.now(rows_in[at]), gain)
            if final and at == 0:
                taken = place.take_sequence(then(cotangent, normed))
            forward.chunk(stream, normed)
            if final and at == 0:
                last_up = place.gather_chunks(place.in_order(*place.now(taken)), PIECES)
        kept.append(forward.kept)
        previous = forward
    for at in range(PIECES):
        previous.scale(at)
    shares = kept[-1]["share"]
    mixed_sent = [place.to_group(place.soon(place.rows_of(shares, hop)), hop) for hop in range(1, place.groups)]
    grads = last_up()
    in_sums, out_sums, gain_grads, carried = [None] * layers, [None] * layers, [0.0] * layers, [None] * layers
    pending, waiting = None, []

    def small_sums(layer):
        gchan, gtaps, ghead = carried[layer]
        blank = jnp.zeros((1, own_cols - 256), F32)
        parts = []
        for part in range(2):
            per_head_row = jnp.concatenate([ghead[8 * part : 8 * part + 1], ghead[8 * part + 1 : 8 * part + 2], blank], axis=1)
            parts.append(jnp.concatenate([gchan[:7, part * own_cols : (part + 1) * own_cols], per_head_row]))
        return jnp.stack(parts), gtaps

    for layer in reversed(range(layers)):
        final = layer == layers - 1
        back = Backward(place, weights[layer], tables[layer], heads, inner, kept[layer])
        for at in reversed(range(PIECES)):
            scale = kept[layer]["scale"][at]
            if final:
                back.enter(at, (grads[at].astype(F32) * scale).astype(BF16))
                continue
            share, arrived = pending[at]
            grads[at], gain_grad, up, pull = norm_backward(
                [kept[layer + 1]["stream"][at]],
                [grads[at]],
                share,
                list(place.now(tuple(arrived))),
                weights[layer + 1][1],
                None,
                (scale, kept[layer]["update"][at]),
                inner,
            )
            gain_grads[layer + 1] = gain_grads[layer + 1] + jnp.where(place.group == 0, gain_grad[0], 0.0)
            back.enter(at, up, pull)
        normed, mixed = kept[layer]["normed"], kept[layer]["mixed"]
        out_sum = out_sums[layer] = WeightSum(place, back.ups, mixed)
        out_sum.to_pair()
        if layer == 0:
            far_normed = [place.to_core(part) for part in normed]
        far_columns, pending = [None] * PIECES, [None] * PIECES
        for at in reversed(range(PIECES)):
            back.mix(at)
            if layer == 0:
                far_columns[at] = place.to_core(back.dcolumns[at])
            if at == PIECES - 1:
                for later in out_sums[layer + 1 :]:
                    later.owned = later.total()
                if layer == 0:
                    own_rows = place.rows_of(kept[-1]["stream"], 0).astype(F32)
                    update = added(place.rows_of(shares, 0), place.now(tuple(mixed_sent)))
                    mixed_out = place.give_sequence(own_rows + update * place.rows_of(kept[-1]["scale"], 0))
            if layer:
                share = back.share(back.dcolumns[at])
                pending[at] = (share, place.sent_to_groups(share))
                if at == PIECES - 1:
                    out_sum.to_chips()
        carried[layer] = back.carried[3:]
        waiting.append(small_sums(layer))
        if layer:
            in_sum = in_sums[layer] = Owned()
            stack = place.did(stacked_product(list(place.now(tuple(normed))), back.dcolumns))
            in_sum.owned = place.scatter_owners(stack).astype(F32)
            continue
        in_sum = in_sums[layer] = WeightSum(place, normed, back.dcolumns, far_normed, far_columns)
        mixed_out = place.both_sequences(mixed_out)
        if PIECES == place.groups:
            sent = [back.share(place.rows_of(back.dcolumns, hop)) for hop in range(1, place.groups)]
            arrived = [place.to_group(piece, hop) for hop, piece in enumerate(sent, 1)]
            own = back.share(place.rows_of(back.dcolumns, 0))
        else:
            done = [back.share(columns) for columns in back.dcolumns]
            arrived = [place.to_group(place.rows_of(done, hop), hop) for hop in range(1, place.groups)]
            own = place.rows_of(done, 0)
        out_sum.to_chips()
        stream_parts, grad_parts, choice = kept[layer]["stream"], grads, place.group.astype(jnp.int32)[None]
        if PIECES != place.groups:
            stream_parts, grad_parts, choice = [place.rows_of(stream_parts, 0)], [place.rows_of(grads, 0)], None
        arrived = list(place.now(tuple(arrived)))
        grad, gain_grad = norm_backward(stream_parts, grad_parts, own, arrived, weights[layer][1], choice)
        place.did(grad)
        gain_grads[layer] = gain_grad[0]
    grad_hidden = place.give_sequence(grad)

    halves = jnp.concatenate([part for part, _ in reversed(waiting)], axis=1)
    gains = jnp.stack(gain_grads).reshape(-1, shared)
    common = [part for _, part in reversed(waiting)] + [gains, jnp.zeros((-gains.shape[0] % 8, shared), F32)]
    common = then(place.now(jnp.concatenate(common)), *out_sums[0].sent)
    in_sums[0].owned, half_total, common_total = reduced_product(place, in_sum.lhs, in_sum.rhs, halves, common, 0)
    place.did(in_sums[0].owned)
    out_sums[0].owned = out_sums[0].total()
    gain_total = common_total[8 * layers : 8 * layers + gains.shape[0]].reshape(layers, -1)

    state_parts = jnp.concatenate([in_sum.owned[:, main : main + half] for in_sum in in_sums])
    state_parts = place.both(place.add_groups(place.now(state_parts)), 1).reshape(layers, rows, shared)
    outs = []
    for layer in range(layers):
        per_channel_part = half_total[8 * layer : 8 * layer + 8]
        gain_part = lax.dynamic_slice_in_dim(gain_total[layer], lax.axis_index("dp") * rows, rows, 0)
        taps_part = common_total[8 * layer : 8 * layer + 5]
        in_owned, out_owned = in_sums[layer].owned, out_sums[layer].owned
        outs.append(
            (
                gain_part,
                jnp.stack([in_owned[:, :own_cols], in_owned[:, own_cols:main]]),
                state_parts[layer],
                in_owned[:, main + half : main + half + heads],
                per_channel_part[:5],
                taps_part,
                per_channel_part[7, :heads],
                per_channel_part[7, 128 : 128 + heads],
                per_channel_part[5].reshape(heads, width).sum(axis=1),
                per_channel_part[6],
                out_owned.T,
            )
        )
    grad_hidden = place.both_sequences(grad_hidden)
    return (mixed_out, grad_hidden) + tuple(jnp.stack(parts) for parts in zip(*outs))


def solution(mesh):
    placed = (
        P("dp", "tensor", None),
        P("dp", "tensor", None),
        P(None, "dp"),
        P(None, None, "dp", "tensor"),
        P(None, "dp", None),
        P(None, "dp", "tensor"),
        P(None, None, "tensor"),
        P(),
        P(None, "tensor"),
        P(None, "tensor"),
        P(None, "tensor"),
        P(None, "tensor"),
        P(None, "tensor", "dp"),
    )
    return jax.shard_map(
        local,
        mesh=mesh,
        in_specs=placed,
        out_specs=(
            P("dp", "tensor", None),
            P("dp", "tensor", None),
            P(None, "dp"),
            P(None, None, "dp", "tensor"),
            P(None, "dp", None),
            P(None, "dp", "tensor"),
            P(None, None, "tensor"),
            P(),
            P(None, "tensor"),
            P(None, "tensor"),
            P(None, "tensor"),
            P(None, "tensor"),
            P(None, "tensor", "dp"),
        ),
        check_vma=False,
    )
```

```python
import functools

import jax
import jax.numpy as jnp
from jax import lax
from jax.experimental import pallas as pl
from jax.experimental.pallas import tpu as pltpu
from jax.sharding import PartitionSpec as P

EPSILON = 1e-05
CHUNK = 128
PIECES = 2
GROUP_LANES = 256
SMALL_COST = pl.CostEstimate(flops=1000, bytes_accessed=1000, transcendentals=0)
LARGE_COST = pl.CostEstimate(flops=10**11, bytes_accessed=10**8, transcendentals=0)
LOG2E = 1.4426950408889634
F32 = jnp.float32
BF16 = jnp.bfloat16
NN = (((1,), (0,)), ((), ()))
NT = (((1,), (1,)), ((), ()))
MESH = pl.DeviceIdType.MESH
TN = (((0,), (0,)), ((), ()))


def mm(a, b, dims=NN):
    return lax.dot_general(a, b, dims, preferred_element_type=F32)


def sigmoid(v):
    return 0.5 * jnp.tanh(0.5 * v) + 0.5


def softplus(v):
    return jnp.maximum(v, 0.0) + jnp.log(1.0 + jnp.exp(-jnp.abs(v)))


def split3(v):
    high = v.astype(BF16)
    rest = v - high.astype(F32)
    mid = rest.astype(BF16)
    return high, mid, (rest - mid.astype(F32)).astype(BF16)


def spread(v, expand, heads):
    high = v.astype(BF16)
    low = (v - high.astype(F32)).astype(BF16)
    lane = lax.broadcasted_iota(jnp.int32, v.shape, 1)
    parts = jnp.where(lane < heads, high, jnp.where(lane < 2 * heads, low, jnp.zeros_like(low)))
    return mm(parts, expand)


def conv_rows(window, table, length):
    total = table[4:5] + table[3:4] * window[8 : 8 + length]
    for back in range(1, 4):
        total = total + table[3 - back : 4 - back] * pltpu.roll(window, back, 0)[8 : 8 + length]
    return total


def causal(length, flip):
    row = lax.broadcasted_iota(jnp.int32, (length, length), 0)
    col = lax.broadcasted_iota(jnp.int32, (length, length), 1)
    return (row <= col) if flip else (row >= col)


def head_masks(lanes, width):
    lane = lax.broadcasted_iota(jnp.int32, (1, lanes), 1)
    return [(lane >= j * width) & (lane < (j + 1) * width) for j in range(lanes // width)]


def both_halves(ref):
    half = ref.shape[2] - 128
    return jnp.concatenate([ref[0, :, :half], ref[1, :, :half]], axis=1)


def forward_kernel(first, heads, *refs):
    columns_ref, small_ref, chan_ref, taps_ref, head_ref, expand_ref, tri_ref = refs[:7]
    refs = refs[7:]
    if not first:
        start_ref, tail_ref, stail_ref = refs[:3]
    mixed_ref, square_ref, y_ref, saved_ref, state, xbuf, sbuf = refs[-7:]
    length, channels = y_ref.shape[1:]
    width = channels // heads
    shared = taps_ref.shape[1]
    half = shared // 2

    @pl.when(pl.program_id(0) == 0)
    def _():
        if first:
            state[...] = jnp.zeros_like(state)
            xbuf[0:8] = jnp.zeros((8, 2 * channels), F32)
            sbuf[0:8] = jnp.zeros((8, shared), F32)
        else:
            state[...] = start_ref[...]
            for half_no in range(2):
                xbuf[0:8, half_no * channels : (half_no + 1) * channels] = tail_ref[half_no, :, channels:].astype(F32)[-8:]
            sbuf[0:8] = both_halves(stail_ref)

    sbuf[8:] = both_halves(small_ref)
    tri = tri_ref[...]
    expand = expand_ref[...]
    taps = taps_ref[...]
    bc = conv_rows(sbuf[...], taps, length)
    bc = (bc * sigmoid(bc)).astype(BF16)
    keys, queries = bc[:, :half], bc[:, half:]
    scores = jnp.where(causal(length, False), mm(queries, keys, NT), 0.0)
    squares = jnp.zeros((length, 128), F32)
    masks = head_masks(GROUP_LANES, width)
    for half_no in range(2):
        head = head_ref[8 * half_no : 8 * half_no + 8]
        dt = softplus(small_ref[half_no, :, half:] + head[0:1])
        running = sum(mm(tri, piece) for piece in split3(dt * (head[1:2] * LOG2E)))
        running_t = running.T
        decay_in = jnp.exp2(running)
        decay_out = jnp.exp2(running[length - 1 :] - running)
        dt_wide = spread(dt, expand, heads)
        in_wide = spread(decay_in, expand, heads)
        out_wide = spread(dt * decay_out, expand, heads)
        for start in range(0, channels, GROUP_LANES):
            lanes = slice(start, start + GROUP_LANES)
            conv_at = slice(channels + start, channels + start + GROUP_LANES)
            wide = slice(half_no * channels + start, half_no * channels + start + GROUP_LANES)
            table = chan_ref[:, wide]
            xbuf[8:, wide] = columns_ref[half_no, :, conv_at].astype(F32)
            c = conv_rows(xbuf[:, wide], table, length)
            xbuf[0:8, wide] = xbuf[length:, wide]
            xs = c * sigmoid(c)
            values = (xs * dt_wide[:, lanes]).astype(BF16)
            weights, parts = [], []
            for j in range(GROUP_LANES // width):
                h = start // width + j
                gap = jnp.minimum(running[:, h : h + 1] - running_t[h : h + 1, :], 0.0)
                weights.append((scores * jnp.exp2(gap)).astype(BF16))
                parts.append(jnp.where(masks[j], values, jnp.zeros_like(values)))
            before = state[:, wide]
            before_low = before.astype(BF16)
            saved_ref[half_no, 0, :, lanes] = before_low
            y = mm(jnp.concatenate(weights, axis=1), jnp.concatenate(parts, axis=0))
            y = y + mm(queries, before_low) * in_wide[:, lanes]
            y_ref[half_no, :, lanes] = y
            z = columns_ref[half_no, :, lanes].astype(F32)
            gated = (y + table[5:6] * xs) * (z * sigmoid(z))
            mixed_ref[half_no, :, lanes] = (gated * table[6:7]).astype(BF16)
            power = gated * gated
            for at in range(0, GROUP_LANES, 128):
                squares = squares + power[:, at : at + 128]
            fresh = mm(keys, (xs * out_wide[:, lanes]).astype(BF16), TN)
            state[:, wide] = before * in_wide[length - 1 :, lanes] + fresh
    square_ref[...] = jnp.sum(squares, axis=1, keepdims=True)
    sbuf[0:8] = sbuf[length:]


def backward_kernel(first, last, heads, *refs):
    columns_ref, small_ref, y_ref, saved_ref, up_ref, pull_ref = refs[:6]
    chan_ref, taps_ref, head_ref, expand_ref, tri_ref, halo_ref, shalo_ref, early_ref, searly_ref = refs[6:15]
    refs = refs[15:]
    if not last:
        carried_refs = refs[:6]
    dcolumns_ref, dstate, dtail_ref, dstail_ref, gchan_ref, gtaps_ref, ghead_ref, xbuf, sbuf, dxbuf, dsbuf = refs[-11:]
    length, channels = y_ref.shape[1:]
    width = channels // heads
    shared = taps_ref.shape[1]
    half = shared // 2
    step_no = pl.program_id(0)
    first_block = step_no == pl.num_programs(0) - 1

    @pl.when(step_no == 0)
    def _():
        if last:
            dstate[...] = jnp.zeros_like(dstate)
            dxbuf[length:] = jnp.zeros((8, 2 * channels), F32)
            dsbuf[length:] = jnp.zeros((8, shared), F32)
            gchan_ref[...] = jnp.zeros_like(gchan_ref)
            gtaps_ref[...] = jnp.zeros_like(gtaps_ref)
            ghead_ref[...] = jnp.zeros_like(ghead_ref)
        else:
            dstate[...] = carried_refs[0][...]
            dxbuf[length:] = carried_refs[1][...]
            dsbuf[length:] = carried_refs[2][...]
            gchan_ref[...] = carried_refs[3][...]
            gtaps_ref[...] = carried_refs[4][...]
            ghead_ref[...] = carried_refs[5][...]

    def outside(rows):
        return jnp.zeros_like(rows) if first else rows

    sbuf[8:] = both_halves(small_ref)
    sbuf[0:8] = jnp.where(first_block, outside(both_halves(searly_ref)), both_halves(shalo_ref))
    tri = tri_ref[...]
    expand = expand_ref[...]
    taps = taps_ref[...]
    bc_in = conv_rows(sbuf[...], taps, length)
    bc_sig = sigmoid(bc_in)
    bc = (bc_in * bc_sig).astype(BF16)
    keys, queries = bc[:, :half], bc[:, half:]
    keep = causal(length, True)
    scores = jnp.where(keep, mm(keys, queries, NT), 0.0)
    pull = pull_ref[...]
    masks = head_masks(GROUP_LANES, width)
    dscores = jnp.zeros((length, length), F32)
    dkeys = jnp.zeros((length, half), F32)
    dqueries = jnp.zeros((length, half), F32)
    last_row = lax.broadcasted_iota(jnp.int32, (length, 1), 0) == length - 1
    lane = lax.broadcasted_iota(jnp.int32, (length, 128), 1)
    per_group = GROUP_LANES // width
    for half_no in range(2):
        head = head_ref[8 * half_no : 8 * half_no + 8]
        step = small_ref[half_no, :, half:] + head[0:1]
        dt = softplus(step)
        rate = dt * head[1:2]
        running = sum(mm(tri, piece) for piece in split3(rate * LOG2E))
        running_t = running.T
        decay_in = jnp.exp2(running)
        decay_out = jnp.exp2(running[length - 1 :] - running)
        dt_wide = spread(dt, expand, heads)
        in_wide = spread(decay_in, expand, heads)
        out_wide = spread(decay_out, expand, heads)
        drun = jnp.zeros((length, 128), F32)
        ddt = jnp.zeros((length, 128), F32)
        for start in range(0, channels, GROUP_LANES):
            lanes = slice(start, start + GROUP_LANES)
            conv_at = slice(channels + start, channels + start + GROUP_LANES)
            at = half_no * channels + start
            wide = slice(at, at + GROUP_LANES)
            table = chan_ref[:, wide]
            xbuf[8:, lanes] = columns_ref[half_no, :, conv_at].astype(F32)
            xbuf[0:8, lanes] = jnp.where(first_block, outside(early_ref[half_no, :, conv_at].astype(F32)[-8:]), halo_ref[half_no, :, conv_at].astype(F32)[-8:])
            c = conv_rows(xbuf[:, lanes], table, length)
            c_sig = sigmoid(c)
            xs = c * c_sig
            z = columns_ref[half_no, :, lanes].astype(F32)
            z_sig = sigmoid(z)
            z_silu = z * z_sig
            y = y_ref[half_no, :, lanes]
            total = y + table[5:6] * xs
            gated = total * z_silu
            up = up_ref[half_no, :, lanes].astype(F32)
            gchan_ref[6:7, wide] += jnp.sum(up * gated, axis=0, keepdims=True)
            dgated = table[6:7] * up - gated * pull
            out_at = half_no * (2 * channels + half + 128) + start
            dcolumns_ref[:, out_at : out_at + GROUP_LANES] = (
                dgated * total * (z_sig + z_silu * (1.0 - z_sig))
            ).astype(BF16)
            dy = dgated * z_silu
            gchan_ref[5:6, wide] += jnp.sum(dy * xs, axis=0, keepdims=True)
            dy_low = dy.astype(BF16)
            dt_lanes = dt_wide[:, lanes]
            values = (xs * dt_lanes).astype(BF16)
            weights, dparts, vparts, decays = [], [], [], []
            for j in range(per_group):
                h = start // width + j
                decay = jnp.exp2(jnp.minimum(running_t[h : h + 1, :] - running[:, h : h + 1], 0.0))
                decays.append(decay)
                weights.append((scores * decay).astype(BF16))
                dparts.append(jnp.where(masks[j], dy_low, jnp.zeros_like(dy_low)))
                vparts.append(jnp.where(masks[j], values, jnp.zeros_like(values)))
            outer = mm(jnp.concatenate(vparts, axis=0), dy_low, NT)
            for j in range(per_group):
                dscores = dscores + outer[j * length : (j + 1) * length] * decays[j]
            dvalues = mm(jnp.concatenate(weights, axis=1), jnp.concatenate(dparts, axis=0))
            before = saved_ref[half_no, 0, :, lanes]
            dafter = dstate[:, wide]
            dafter_low = dafter.astype(BF16)
            out_lanes = out_wide[:, lanes]
            carried = mm(keys, dafter_low) * out_lanes
            dvalues = dvalues + carried
            values_f = values.astype(F32)
            dkeys = dkeys + mm((values_f * out_lanes).astype(BF16), dafter_low, NT)
            in_lanes = in_wide[:, lanes]
            dy_in = (dy * in_lanes).astype(BF16)
            dqueries = dqueries + mm(dy_in, before, NT)
            end_decay = in_lanes[length - 1 :]
            at_end = jnp.sum(values_f * carried, axis=0, keepdims=True) + end_decay * jnp.sum(
                before.astype(F32) * dafter, axis=0, keepdims=True
            )
            dstate[:, wide] = end_decay * dafter + mm(queries, dy_in, TN)
            turn = dy_low.astype(F32) * y - values_f * dvalues + jnp.where(last_row, at_end, 0.0)
            turn_high = turn.astype(BF16)
            turn_low = (turn - turn_high.astype(F32)).astype(BF16)
            group_expand = expand[:, lanes]
            drun = drun + mm(turn_high, group_expand, NT) + mm(turn_low, group_expand, NT)
            ddt = ddt + mm((dvalues * xs).astype(BF16), group_expand, NT)
            dxs = dvalues * dt_lanes + table[5:6] * dy
            dc = dxs * (c_sig + xs * (1.0 - c_sig))
            dxbuf[0:length, wide] = dc
            window = dxbuf[:, wide]
            here = xbuf[8:, lanes]
            gchan_ref[4:5, wide] += jnp.sum(dc, axis=0, keepdims=True)
            gchan_ref[3:4, wide] += jnp.sum(dc * here, axis=0, keepdims=True)
            dconv = table[3:4] * dc
            for ahead in range(1, 4):
                moved = pltpu.roll(window, length + 8 - ahead, 0)[:length]
                gchan_ref[3 - ahead : 4 - ahead, wide] += jnp.sum(moved * here, axis=0, keepdims=True)
                dconv = dconv + table[3 - ahead : 4 - ahead] * moved
            out_at = out_at + channels
            dcolumns_ref[:, out_at : out_at + GROUP_LANES] = dconv.astype(BF16)
            dxbuf[length:, wide] = dxbuf[0:8, wide]

        drate = sum(mm(tri, piece, TN) for piece in split3(drun))
        dstep = (ddt + drate * head[1:2]) * sigmoid(step)
        ghead_ref[8 * half_no : 8 * half_no + 1] += jnp.sum(dstep, axis=0, keepdims=True)
        ghead_ref[8 * half_no + 1 : 8 * half_no + 2] += jnp.sum(drate * rate, axis=0, keepdims=True)
        out_at = half_no * (2 * channels + half + 128) + 2 * channels + half
        dcolumns_ref[:, out_at : out_at + 128] = jnp.where(lane < heads, dstep, 0.0).astype(BF16)

    dscores_low = jnp.where(keep, dscores, 0.0).astype(BF16)
    dkeys = dkeys + mm(dscores_low, queries)
    dqueries = dqueries + mm(dscores_low, keys, TN)
    dbc = jnp.concatenate([dkeys, dqueries], axis=1) * (bc_sig + bc_in * bc_sig * (1.0 - bc_sig))
    dsbuf[0:length] = dbc
    window = dsbuf[...]
    here = sbuf[8:]
    gtaps_ref[4:5] += jnp.sum(dbc, axis=0, keepdims=True)
    gtaps_ref[3:4] += jnp.sum(dbc * here, axis=0, keepdims=True)
    dshared = taps[3:4] * dbc
    for ahead in range(1, 4):
        moved = pltpu.roll(window, length + 8 - ahead, 0)[:length]
        gtaps_ref[3 - ahead : 4 - ahead] += jnp.sum(moved * here, axis=0, keepdims=True)
        dshared = dshared + taps[3 - ahead : 4 - ahead] * moved
    for half_no in range(2):
        out_at = half_no * (2 * channels + half + 128) + 2 * channels
        dcolumns_ref[:, out_at : out_at + half] = dshared[:, half_no * half : (half_no + 1) * half].astype(BF16)
    dsbuf[length:] = dsbuf[0:8]
    dtail_ref[...] = dxbuf[0:8]
    dstail_ref[...] = dsbuf[0:8]


def scan_tables(heads, channels):
    row = lax.broadcasted_iota(jnp.int32, (128, channels), 0) % heads
    col = lax.broadcasted_iota(jnp.int32, (128, channels), 1) // (channels // heads)
    return (row == col).astype(BF16), jnp.tril(jnp.ones((CHUNK, CHUNK), BF16))


def whole(array):
    return pl.BlockSpec(array.shape, lambda i: (0,) * array.ndim)


def last_rows(array, count):
    at = array.shape[1] // count - 1
    return pl.BlockSpec((2, count, array.shape[2]), lambda i: (0, at, 0))


def unread(arrays):
    return [pl.BlockSpec(memory_space=pl.ANY) for _ in arrays]


def mixer_forward(columns, small, tables, heads, earlier=None):
    _, tokens, channels = columns.shape
    channels = channels // 2
    shared = tables[1].shape[1]
    blocks = tokens // CHUNK

    def rows(cols):
        return pl.BlockSpec((2, CHUNK, cols), lambda i: (0, i, 0))

    operands = [columns, small, *tables]
    specs = [rows(2 * channels), rows(small.shape[2])] + [whole(table) for table in tables]
    if earlier is not None:
        operands += list(earlier)
        specs += [whole(earlier[0]), last_rows(earlier[1], 16), last_rows(earlier[2], 8)]
    return pl.pallas_call(
        functools.partial(forward_kernel, earlier is None, heads),
        grid=(blocks,),
        in_specs=specs,
        out_specs=[
            rows(channels),
            pl.BlockSpec((CHUNK, 1), lambda i: (i, 0)),
            rows(channels),
            pl.BlockSpec((2, 1, shared // 2, channels), lambda i: (0, i, 0, 0)),
            pl.BlockSpec((shared // 2, 2 * channels), lambda i: (0, 0)),
        ],
        out_shape=[
            jax.ShapeDtypeStruct((2, tokens, channels), BF16),
            jax.ShapeDtypeStruct((tokens, 1), F32),
            jax.ShapeDtypeStruct((2, tokens, channels), F32),
            jax.ShapeDtypeStruct((2, blocks, shared // 2, channels), BF16),
            jax.ShapeDtypeStruct((shared // 2, 2 * channels), F32),
        ],
        scratch_shapes=[
            pltpu.VMEM((CHUNK + 8, 2 * channels), F32),
            pltpu.VMEM((CHUNK + 8, shared), F32),
        ],
        compiler_params=pltpu.CompilerParams(vmem_limit_bytes=48 * 1024 * 1024),
        cost_estimate=SMALL_COST,
        name="mixer_forward",
    )(*operands)


def mixer_backward(columns, small, y, saved, up, pull, tables, heads, early, carried, after=()):
    _, tokens, channels = y.shape
    shared = tables[1].shape[1]
    blocks = tokens // CHUNK
    thin = small.shape[2]

    def rows(cols):
        return pl.BlockSpec((2, CHUNK, cols), lambda i: (0, blocks - 1 - i, 0))

    def flat_rows(cols):
        return pl.BlockSpec((CHUNK, cols), lambda i: (blocks - 1 - i, 0))

    def halo(count, cols):
        per_block = CHUNK // count
        return pl.BlockSpec((2, count, cols), lambda i: (0, jnp.maximum((blocks - 1 - i) * per_block - 1, 0), 0))

    def fixed(r, c):
        return pl.BlockSpec((r, c), lambda i: (0, 0))

    saved_spec = pl.BlockSpec((2, 1, shared // 2, channels), lambda i: (0, blocks - 1 - i, 0, 0))
    before = (columns, small) if early is None else early
    operands = [columns, small, y, saved, up, pull, *tables, columns, small, *before]
    specs = [rows(2 * channels), rows(thin), rows(channels), saved_spec, rows(channels), flat_rows(1)]
    specs += [whole(table) for table in tables] + [halo(16, 2 * channels), halo(8, thin)]
    specs += [last_rows(before[0], 16), last_rows(before[1], 8)]
    if carried is not None:
        operands += list(carried)
        specs += [whole(array) for array in carried]
    operands += list(after)
    specs += unread(after)
    fixed_shapes = [(shared // 2, 2 * channels), (8, 2 * channels), (8, shared), (8, 2 * channels), (8, shared), (16, 128)]
    return pl.pallas_call(
        functools.partial(backward_kernel, early is None, carried is None, heads),
        grid=(blocks,),
        in_specs=specs,
        out_specs=[flat_rows(4 * channels + 2 * thin)] + [fixed(*shape) for shape in fixed_shapes],
        out_shape=[jax.ShapeDtypeStruct((tokens, 4 * channels + 2 * thin), BF16)]
        + [jax.ShapeDtypeStruct(shape, F32) for shape in fixed_shapes],
        scratch_shapes=[
            pltpu.VMEM((CHUNK + 8, channels), F32),
            pltpu.VMEM((CHUNK + 8, shared), F32),
            pltpu.VMEM((CHUNK + 8, 2 * channels), F32),
            pltpu.VMEM((CHUNK + 8, shared), F32),
        ],
        compiler_params=pltpu.CompilerParams(vmem_limit_bytes=56 * 1024 * 1024),
        cost_estimate=SMALL_COST,
        name="mixer_backward",
    )(*operands)


def product_call(kernel, grid, specs, outs, out_specs, operands, name, cost=SMALL_COST):
    return pl.pallas_call(
        kernel,
        grid=grid,
        in_specs=specs,
        out_specs=out_specs,
        out_shape=outs,
        compiler_params=pltpu.CompilerParams(vmem_limit_bytes=60 * 1024 * 1024),
        cost_estimate=cost,
        name=name,
    )(*operands)


def in_projection(normed, gathered, own, thin):
    tokens, features = normed.shape

    def kernel(normed_ref, main_ref, thin_ref, columns_ref, small_ref):
        rows = normed_ref[...]
        columns_ref[0] = mm(rows, main_ref[...]).astype(BF16)

        @pl.when(pl.program_id(1) == 0)
        def _():
            small_ref[0] = mm(rows, thin_ref[...])

    return product_call(
        kernel,
        (2, 2),
        [
            pl.BlockSpec((tokens, features), lambda s, n: (0, 0)),
            pl.BlockSpec((features, own), lambda s, n: (s, 1 + n)),
            pl.BlockSpec((features, thin), lambda s, n: (s, 3 * own // thin)),
        ],
        [jax.ShapeDtypeStruct((2, tokens, 2 * own), BF16), jax.ShapeDtypeStruct((2, tokens, thin), F32)],
        [
            pl.BlockSpec((1, tokens, own), lambda s, n: (s, 0, n)),
            pl.BlockSpec((1, tokens, thin), lambda s, n: (s, 0, 0)),
        ],
        (normed, gathered, gathered),
        "in_projection",
    )


def out_projection(mixed, gathered, own):
    _, tokens, _ = mixed.shape
    features = gathered.shape[0] // 2
    tile = min(512, features)
    tiles = features // tile

    def kernel(mixed_ref, first_ref, second_ref, share_ref):
        share_ref[...] = (mm(mixed_ref[0], first_ref[...], NT) + mm(mixed_ref[1], second_ref[...], NT)).astype(BF16)

    return product_call(
        kernel,
        (tiles,),
        [
            pl.BlockSpec((2, tokens, own), lambda n: (0, 0, 0)),
            pl.BlockSpec((tile, own), lambda n: (n, 0)),
            pl.BlockSpec((tile, own), lambda n: (tiles + n, 0)),
        ],
        jax.ShapeDtypeStruct((tokens, features), BF16),
        pl.BlockSpec((tokens, tile), lambda n: (0, n)),
        (mixed, gathered, gathered),
        "out_projection",
    )


def mixed_gradient(up, gathered, own, mixed):
    tokens, features = up.shape

    def kernel(up_ref, weight_ref, mixed_ref, grad_ref, pull_ref):
        grad = mm(up_ref[...], weight_ref[...])
        grad_ref[0] = grad.astype(BF16)
        pull = jnp.sum(grad * mixed_ref[0].astype(F32), axis=1, keepdims=True)

        @pl.when(pl.program_id(0) == 0)
        def _():
            pull_ref[...] = pull

        @pl.when(pl.program_id(0) == 1)
        def _():
            pull_ref[...] += pull

    return product_call(
        kernel,
        (2,),
        [
            pl.BlockSpec((tokens, features), lambda s: (0, 0)),
            pl.BlockSpec((features, own), lambda s: (s, 0)),
            pl.BlockSpec((1, tokens, own), lambda s: (s, 0, 0)),
        ],
        [jax.ShapeDtypeStruct((2, tokens, own), BF16), jax.ShapeDtypeStruct((tokens, 1), F32)],
        [pl.BlockSpec((1, tokens, own), lambda s: (s, 0, 0)), pl.BlockSpec((tokens, 1), lambda s: (0, 0))],
        (up, gathered, mixed),
        "mixed_gradient",
    )


def normed_gradient(dcolumns, gathered, own, thin):
    tokens, columns = dcolumns.shape
    features = gathered.shape[0] // 2
    tile = min(512, features)
    tiles = features // tile

    def kernel(dcolumns_ref, *refs):
        total, at = 0.0, 0
        for ref in refs[:-1]:
            total = total + mm(dcolumns_ref[:, at : at + ref.shape[1]], ref[...], NT)
            at += ref.shape[1]
        refs[-1][...] = total.astype(BF16)

    specs = [pl.BlockSpec((tokens, columns), lambda n: (0, 0))]
    for shard in range(2):
        specs.append(pl.BlockSpec((tile, own), lambda n, s=shard: (s * tiles + n, 1)))
        specs.append(pl.BlockSpec((tile, own), lambda n, s=shard: (s * tiles + n, 2)))
        specs.append(pl.BlockSpec((tile, thin), lambda n, s=shard: (s * tiles + n, 3 * own // thin)))
    return product_call(
        kernel,
        (tiles,),
        specs,
        jax.ShapeDtypeStruct((tokens, features), BF16),
        pl.BlockSpec((tokens, tile), lambda n: (0, n)),
        (dcolumns,) + (gathered,) * 6,
        "normed_gradient",
        LARGE_COST,
    )


def stacked_product(lhs, rhs, block=None):
    tokens, features = lhs[0].shape
    chunks = len(lhs)
    split = rhs[0].ndim == 3
    columns = rhs[0].shape[-1] if split else rhs[0].shape[1] // 2
    row_tile, core = (min(256, features), jnp.zeros((1,), jnp.int32)) if block is None else block
    stride = 1 if block is None else 2
    steps = features // (row_tile * stride)

    def kernel(core_ref, *refs):
        out_ref = refs[-1]
        for shard in range(2):
            total = 0.0
            for at in range(chunks):
                ref = refs[chunks + at]
                part = ref[shard] if split else ref[:, shard * columns : (shard + 1) * columns]
                total = total + mm(refs[at][...], part, TN)
            out_ref[shard] = total.astype(BF16)

    return pl.pallas_call(
        kernel,
        grid_spec=pltpu.PrefetchScalarGridSpec(
            num_scalar_prefetch=1,
            grid=(steps,),
            in_specs=[pl.BlockSpec((tokens, row_tile), lambda m, core_ref: (0, stride * m + core_ref[0]))] * chunks
            + [pl.BlockSpec(part.shape, lambda m, core_ref, n=part.ndim: (0,) * n) for part in rhs],
            out_specs=pl.BlockSpec((2, row_tile, columns), lambda m, core_ref: (0, m, 0)),
        ),
        out_shape=jax.ShapeDtypeStruct((2, steps * row_tile, columns), BF16),
        compiler_params=pltpu.CompilerParams(vmem_limit_bytes=60 * 1024 * 1024),
        cost_estimate=LARGE_COST,
        name="stacked_product",
    )(core, *lhs, *rhs)


class Where:
    def __init__(self, chips, groups):
        self.chips, self.groups = chips, groups
        self.dp, self.tensor = lax.axis_index("dp"), lax.axis_index("tensor")
        self.chip, self.core = self.dp // 2, self.dp % 2
        self.shard, self.group = self.tensor % 2, self.tensor // 2

    def other_core(self):
        return (self.dp + 1 - 2 * self.core, self.tensor)

    def pair(self):
        return (self.dp, self.tensor + 1 - 2 * self.shard)

    def chip_at(self, chip):
        return (chip * 2 + self.core, self.tensor)

    def chip_hop(self, hop):
        return self.chip_at((self.chip + hop) % self.chips)

    def group_hop(self, hop):
        return (self.dp, (self.group + hop) % self.groups * 2 + self.shard)

    def meet(self):
        partners = [self.other_core(), self.pair()]
        partners += [self.chip_hop(hop) for hop in range(1, self.chips)]
        partners += [self.group_hop(hop) for hop in range(1, self.groups)]
        barrier = pltpu.get_barrier_semaphore()
        for partner in partners:
            pl.semaphore_signal(barrier, inc=1, device_id=partner, device_id_type=MESH)
        pl.semaphore_wait(barrier, len(partners))


def remote(src, dst, send_sem, recv_sem, device):
    return pltpu.make_async_remote_copy(
        src_ref=src, dst_ref=dst, send_sem=send_sem, recv_sem=recv_sem, device_id=device, device_id_type=MESH
    )


def gather_kernel(chips, groups, block_ref, hidden_ref, all_ref, stream_ref, left_sem, right_sem, pair_sem, core_sem,
                  chain_recv, pair_recv, core_recv, hidden_send, hidden_recv, local_sem):
    at = Where(chips, groups)
    at.meet()
    mine = pltpu.make_async_copy(block_ref, all_ref.at[at.shard, at.dp], local_sem.at[0])
    mine.start()
    rows = pltpu.make_async_copy(hidden_ref.at[at.shard], stream_ref.at[at.tensor], local_sem.at[1])
    rows.start()

    def hidden_copies():
        slot = stream_ref.at[at.tensor]
        copies = [remote(hidden_ref.at[1 - at.shard], slot, hidden_send.at[0], hidden_recv.at[at.tensor], at.pair())]
        for hop in range(1, groups):
            copies.append(
                remote(hidden_ref.at[at.shard], slot, hidden_send.at[hop], hidden_recv.at[at.tensor], at.group_hop(hop))
            )
        return copies

    def hidden_passed():
        other = at.tensor + 1 - 2 * at.shard
        slot = stream_ref.at[other]
        return [
            remote(slot, slot, hidden_send.at[groups - 1 + hop], hidden_recv.at[other], at.group_hop(hop))
            for hop in range(1, groups)
        ]

    def source(chip):
        return chip * 2 + at.core

    def own_or(chip):
        return all_ref.at[at.shard, source(chip)]

    def to_left(chip, src):
        return remote(src, own_or(chip), left_sem.at[chip], chain_recv.at[chip], at.chip_at(jnp.maximum(at.chip - 1, 0)))

    def to_right(chip, src):
        neighbour = at.chip_at(jnp.minimum(at.chip + 1, chips - 1))
        return remote(src, own_or(chip), right_sem.at[chip], chain_recv.at[chip], neighbour)

    def to_pair(chip, src):
        return remote(src, own_or(chip), pair_sem.at[chip], pair_recv.at[chip], at.pair())

    def to_core(shard, chip, src):
        place = all_ref.at[shard, source(chip)]
        return remote(src, place, core_sem.at[shard, chip], core_recv.at[shard, chip], at.other_core())

    has_left, has_right = at.chip > 0, at.chip < chips - 1
    for copy in hidden_copies():
        copy.start()
    to_pair(at.chip, block_ref).start()

    @pl.when(has_left)
    def _():
        to_left(at.chip, block_ref).start()

    @pl.when(has_right)
    def _():
        to_right(at.chip, block_ref).start()

    to_core(at.shard, at.chip, block_ref).start()

    def from_left(step):
        chip = jnp.maximum(at.chip - step, 0)
        return at.chip >= step, chip

    def from_right(step):
        chip = jnp.minimum(at.chip + step, chips - 1)
        return at.chip + step < chips, chip

    for step in range(1, chips):
        there, chip = from_left(step)

        @pl.when(there)
        def _():
            block = own_or(chip)
            to_right(chip, block).wait_recv()

            @pl.when(has_right)
            def _():
                to_right(chip, block).start()

            to_pair(chip, block).start()
            to_core(at.shard, chip, block).start()

        there, chip = from_right(step)

        @pl.when(there)
        def _():
            block = own_or(chip)
            to_left(chip, block).wait_recv()

            @pl.when(has_left)
            def _():
                to_left(chip, block).start()

            to_pair(chip, block).start()
            to_core(at.shard, chip, block).start()

        if step == 1:
            hidden_copies()[0].wait_send()
            other = at.tensor + 1 - 2 * at.shard
            arrived = stream_ref.at[other]
            remote(arrived, arrived, hidden_send.at[0], hidden_recv.at[other], at.pair()).wait_recv()
            for copy in hidden_passed():
                copy.start()

    def pair_block(chip):
        return all_ref.at[1 - at.shard, source(chip)]

    def pass_pair(chip):
        block = pair_block(chip)
        remote(block, block, pair_sem.at[chip], pair_recv.at[chip], at.pair()).wait_recv()
        to_core(1 - at.shard, chip, block).start()

    pass_pair(at.chip)
    for step in range(1, chips):
        there, chip = from_left(step)

        @pl.when(there)
        def _():
            pass_pair(chip)

        there, chip = from_right(step)

        @pl.when(there)
        def _():
            pass_pair(chip)

    mine.wait()
    rows.wait()
    for copy in hidden_copies()[1:]:
        copy.wait_send()
    for copy in hidden_passed():
        copy.wait_send()
    for hop in range(1, groups):
        for shard in range(2):
            member = (at.group + hop) % groups * 2 + shard
            arrived = stream_ref.at[member]
            remote(arrived, arrived, hidden_send.at[0], hidden_recv.at[member], at.pair()).wait_recv()
    far_core = 1 - at.core
    for chip in range(chips):
        block = own_or(chip)
        to_pair(chip, block).wait_send()
        for shard in range(2):
            to_core(shard, chip, all_ref.at[shard, source(chip)]).wait_send()
            arrived = all_ref.at[shard, chip * 2 + far_core]
            remote(arrived, arrived, core_sem.at[shard, chip], core_recv.at[shard, chip], at.other_core()).wait_recv()

        @pl.when(has_right & (at.chip >= chip))
        def _():
            to_right(chip, block).wait_send()

        @pl.when(has_left & (at.chip <= chip))
        def _():
            to_left(chip, block).wait_send()


def gathered_first(place, block, hidden):
    chips, groups, members = place.chips, place.groups, place.members
    anywhere = pl.BlockSpec(memory_space=pl.ANY)
    dma = pltpu.SemaphoreType.DMA
    both, stream = pl.pallas_call(
        functools.partial(gather_kernel, chips, groups),
        in_specs=[anywhere] * 2,
        out_specs=[anywhere] * 2,
        out_shape=[
            jax.ShapeDtypeStruct((2, 2 * chips) + block.shape, BF16),
            jax.ShapeDtypeStruct((members,) + hidden.shape[1:], BF16),
        ],
        scratch_shapes=[
            dma((chips,)), dma((chips,)), dma((chips,)), dma((2, chips)),
            dma((chips,)), dma((chips,)), dma((2, chips)),
            dma((2 * groups,)), dma((members,)), dma((2,)),
        ],
        compiler_params=pltpu.CompilerParams(collective_id=1, has_side_effects=True),
        cost_estimate=SMALL_COST,
        name="gathered_first",
    )(block, hidden)
    return both.reshape(-1, block.shape[1]), stream.reshape(-1, hidden.shape[2])


def reduce_kernel(chips, groups, orders, parts, *refs):
    lhs, rhs, halves_ref, common_ref = refs[:parts], refs[parts : 2 * parts], refs[2 * parts], refs[2 * parts + 1]
    (out_ref, half_out, common_out, pair_out, pair_in, own, chain_in, half_buf, half_in, common_buf, common_in,
     pair_send, pair_recv, chain_send, chain_recv, half_send, half_recv, common_send, common_recv) = refs[2 * parts + 2 :]
    rows, columns = out_ref.shape
    tile = columns // 2 if columns % 256 == 0 else columns
    at = Where(chips, groups)
    at.meet()

    stages = [[at.other_core()], [at.pair()], [at.chip_hop(hop) for hop in range(1, chips)]]
    stages.append([at.group_hop(hop) for hop in range(1, groups)])
    firsts = [sum(len(stage) for stage in stages[:no]) for no in range(4)]

    def small_copies(stage):
        copies = []
        for step, device in enumerate(stages[stage]):
            slot = firsts[stage] + step
            copies.append(
                remote(common_buf.at[stage], common_in.at[slot], common_send.at[slot], common_recv.at[slot], device)
            )
            if stage == 0:
                for shard in range(2):
                    copies.append(
                        remote(half_buf.at[0, shard], half_in.at[shard], half_send.at[shard], half_recv.at[shard], device)
                    )
            elif stage == 1:
                copies.append(
                    remote(half_buf.at[1, 1 - at.shard], half_in.at[2], half_send.at[2], half_recv.at[2], device)
                )
            elif stage == 2:
                copies.append(
                    remote(half_buf.at[2, 0], half_in.at[3 + step], half_send.at[3 + step], half_recv.at[3 + step], device)
                )
        return copies

    def small_start(stage):
        for copy in small_copies(stage):
            copy.start()

    def small_finish(stage):
        for copy in small_copies(stage):
            copy.wait()
        total = common_buf[stage]
        for step in range(len(stages[stage])):
            total = total + common_in[firsts[stage] + step]
        if stage < 3:
            common_buf[stage + 1] = total
        else:
            common_out[...] = total
        if stage == 0:
            for shard in range(2):
                half_buf[1, shard] = half_buf[0, shard] + half_in[shard]
        elif stage == 1:
            half_buf[2, 0] = jnp.where(at.shard == 0, half_buf[1, 0], half_buf[1, 1]) + half_in[2]
        elif stage == 2:
            total = half_buf[2, 0]
            for step in range(chips - 1):
                total = total + half_in[3 + step]
            half_out[...] = total
        if stage < 3:
            small_start(stage + 1)

    half_buf[0] = halves_ref[...]
    common_buf[0] = common_ref[...]
    small_start(0)

    def target(step):
        chip = 0
        for number, order in enumerate(orders):
            chip = chip + jnp.where(at.chip == number, order[step], 0)
        return chip

    def pair_copy(step):
        return remote(pair_out.at[step], pair_in.at[step], pair_send.at[step], pair_recv.at[step], at.pair())

    def chain_copy(step):
        chip = target(step)
        right = chip > at.chip
        neighbour = jnp.clip(jnp.where(right, at.chip + 1, at.chip - 1), 0, chips - 1)
        slot = jnp.where(right | (neighbour != chip), chip, chips)
        return remote(pair_out.at[step], chain_in.at[slot], chain_send.at[step], chain_recv.at[slot], at.chip_at(neighbour))

    def arrival(slot):
        block = chain_in.at[slot]
        return remote(block, block, chain_send.at[0], chain_recv.at[slot], at.pair())

    def multiply(step):
        chip = target(step)
        features = pl.ds(pl.multiple_of((2 * chip + at.core) * rows, 128), rows)

        def product(column):
            total = 0.0
            for part in range(parts):
                total = total + mm(lhs[part][:, features], rhs[part][:, pl.ds(column, tile)], TN)
            return total

        @pl.loop(0, columns // tile)
        def _(tile_no):
            first = pl.multiple_of(tile_no * tile, 128)
            column = pl.multiple_of((1 - at.shard) * columns + first, 128)
            pair_out[step, :, pl.ds(first, tile)] = product(column).astype(BF16)

        pair_copy(step).start()

        @pl.loop(0, columns // tile)
        def _(tile_no):
            first = pl.multiple_of(tile_no * tile, 128)
            column = pl.multiple_of(at.shard * columns + first, 128)
            own[step % 3, :, pl.ds(first, tile)] = product(column)

    def in_tiles(body):
        @pl.loop(0, columns // 128)
        def _(tile_no):
            body(pl.ds(pl.multiple_of(tile_no * 128, 128), 128))

    def add_to_own(step, block, slot):
        def body(lanes):
            own[step % 3, :, lanes] = own[step % 3, :, lanes] + block[slot, :, lanes].astype(F32)

        in_tiles(body)

    def pass_on(step):
        pair_copy(step).wait()
        add_to_own(step, pair_in, step)
        chip = target(step)
        if step < chips - 1:

            @pl.when(((chip > at.chip) & (at.chip > 0)) | ((chip < at.chip) & (at.chip < chips - 1)))
            def _():
                arrival(chip).wait_recv()
                add_to_own(step, chain_in, chip)

            def body(lanes):
                pair_out[step, :, lanes] = own[step % 3, :, lanes].astype(BF16)

            in_tiles(body)
            chain_copy(step).start()
        else:

            @pl.when(at.chip > 0)
            def _():
                arrival(at.chip).wait_recv()
                add_to_own(step, chain_in, at.chip)

            @pl.when(at.chip < chips - 1)
            def _():
                arrival(chips).wait_recv()
                add_to_own(step, chain_in, chips)

            def body(lanes):
                out_ref[:, lanes] = own[step % 3, :, lanes]

            in_tiles(body)

    for step in range(chips):
        multiply(step)
        if step >= 2:
            pass_on(step - 2)
        if step < 3:
            small_finish(step)
    for stage in range(chips, 3):
        small_finish(stage)
    for step in range(max(0, chips - 2), chips):
        pass_on(step)
    small_finish(3)
    for step in range(chips - 1):
        chain_copy(step).wait_send()


def reduced_product(place, lhs, rhs, halves, common, number):
    chips, groups = place.chips, place.groups
    rows, columns = lhs[0].shape[1] // (2 * chips), rhs[0].shape[1] // 2
    orders = []
    for chip in range(chips):
        due = {to: chip + chips - 1 - to if to > chip else chips - 1 - chip + to for to in range(chips) if to != chip}
        orders.append(sorted(due, key=due.get) + [chip])
    parts = len(lhs)
    slots = 1 + 1 + (chips - 1) + (groups - 1)
    vmem = pl.BlockSpec(memory_space=pltpu.VMEM)
    dma = pltpu.SemaphoreType.DMA
    half = halves.shape[1:]
    return pl.pallas_call(
        functools.partial(reduce_kernel, chips, groups, orders, parts),
        in_specs=[vmem] * (2 * parts + 2),
        out_specs=[vmem] * 3,
        out_shape=[
            jax.ShapeDtypeStruct((rows, columns), F32),
            jax.ShapeDtypeStruct(half, F32),
            jax.ShapeDtypeStruct(common.shape, F32),
        ],
        scratch_shapes=[
            pltpu.VMEM((chips, rows, columns), BF16),
            pltpu.VMEM((chips, rows, columns), BF16),
            pltpu.VMEM((3, rows, columns), F32),
            pltpu.VMEM((chips + 1, rows, columns), BF16),
            pltpu.VMEM((3, 2) + half, F32),
            pltpu.VMEM((2 + chips,) + half, F32),
            pltpu.VMEM((4,) + common.shape, F32),
            pltpu.VMEM((slots,) + common.shape, F32),
            dma((chips,)), dma((chips,)), dma((chips,)), dma((chips + 1,)),
            dma((2 + chips,)), dma((2 + chips,)), dma((slots,)), dma((slots,)),
        ],
        compiler_params=pltpu.CompilerParams(
            collective_id=2 + number, has_side_effects=True, vmem_limit_bytes=60 * 1024 * 1024
        ),
        cost_estimate=LARGE_COST,
        name="reduced_product",
    )(*lhs, *rhs, halves, common)


class Place:
    def __init__(self):
        self.last = ()
        self.due = []
        self.members = lax.axis_size("tensor")
        self.groups = self.members // 2
        self.sequence = lax.axis_index("tensor") % 2
        self.group = lax.axis_index("tensor") // 2
        self.chips = lax.axis_size("dp") // 2
        self.chip = lax.axis_index("dp") // 2
        self.core = lax.axis_index("dp") % 2
        copies = lax.axis_size("dp")
        self.owners = [
            [d * self.members + 2 * g + s for s in range(2) for d in range(copies)] for g in range(self.groups)
        ]

    def now(self, v):
        return lax.optimization_barrier((v, self.last, tuple(self.due)))[0]

    def did(self, v):
        self.last, self.due = (v,), []
        return v

    def soon(self, v):
        self.due.append(v)
        return v

    def to_pair(self, v):
        return lax.ppermute(v, "tensor", [(t, t ^ 1) for t in range(self.members)])

    def to_group(self, v, hop):
        return lax.ppermute(v, "tensor", [(t, (t + 2 * hop) % self.members) for t in range(self.members)])

    def to_core(self, v):
        return lax.ppermute(v, "dp", [(t, t ^ 1) for t in range(2 * self.chips)])

    def to_chip(self, v, hop):
        count = 2 * self.chips
        return lax.ppermute(v, "dp", [(t, (t + 2 * hop) % count) for t in range(count)])

    def scatter_owners(self, v):
        v = v.reshape(-1, v.shape[-1])
        return lax.psum_scatter(v, ("dp", "tensor"), scatter_dimension=0, axis_index_groups=self.owners, tiled=True)

    def gather_owners(self, v):
        return lax.all_gather(v, ("dp", "tensor"), axis=0, axis_index_groups=self.owners, tiled=True)

    def add_groups(self, v):
        return v + sum(self.to_group(v, hop) for hop in range(1, self.groups))

    def sent_to_groups(self, v):
        return [self.to_group(v, hop) for hop in range(1, self.groups)]

    def both(self, v, axis):
        other = self.to_pair(v)
        return jnp.where(
            self.sequence == 0, jnp.concatenate([v, other], axis=axis), jnp.concatenate([other, v], axis=axis)
        )

    def rows_of(self, chunks, hop):
        at = (self.group + hop) % self.groups
        if len(chunks) == self.groups == 2:
            return jnp.where(at == 0, chunks[0], chunks[1])
        total = jnp.concatenate(chunks)
        count = total.shape[0] // self.groups
        return lax.dynamic_slice_in_dim(total, at * count, count, 0)

    def gather_chunks(self, v, chunks):
        if chunks == self.groups == 2:
            other = self.to_group(v, 1)
            return lambda: [jnp.where(self.group == at, v, self.now(other)) for at in range(2)]
        count = v.shape[0]
        total = jnp.zeros((count * self.groups,) + v.shape[1:], v.dtype)
        total = lax.dynamic_update_slice_in_dim(total, v, self.group * count, 0)
        for hop in range(1, self.groups):
            start = (self.group - hop) % self.groups * count
            total = lax.dynamic_update_slice_in_dim(total, self.to_group(v, hop), start, 0)
        return lambda: jnp.split(self.now(total), chunks)

    def take_sequence(self, v):
        mine = jnp.where(self.sequence == 0, v[0], v[1])
        return mine, self.to_pair(jnp.where(self.sequence == 0, v[1], v[0]))

    def in_order(self, mine, other):
        return jnp.where(self.sequence == 0, jnp.concatenate([mine, other]), jnp.concatenate([other, mine]))

    def give_sequence(self, v):
        first, second = jnp.split(v.astype(BF16), 2)
        mine = jnp.where(self.sequence == 0, first, second)
        other = self.to_pair(jnp.where(self.sequence == 0, second, first))
        return mine, other

    def both_sequences(self, given):
        mine, other = self.now(given)
        mine, other = mine.astype(F32), other.astype(F32)
        return jnp.where(self.sequence == 0, jnp.stack([mine, other]), jnp.stack([other, mine]))


def then(v, *earlier):
    return lax.optimization_barrier((v, earlier))[0]


def added(v, arrived):
    return v.astype(F32) + sum(piece.astype(F32) for piece in arrived)


class Owned:
    pass


class WeightSum:

    def __init__(self, place, features, columns, far_features=None, far_columns=None):
        self.place = place
        self.lhs = list(features) + (far_features or [place.to_core(part) for part in features])
        self.rhs = list(columns) + (far_columns or [place.to_core(part) for part in columns])

    def to_pair(self):
        place = self.place
        rows = self.lhs[0].shape[1] // (2 * place.chips)
        lhs = list(place.now(tuple(self.lhs)))
        self.stack = place.did(stacked_product(lhs, self.rhs, (rows, place.core.astype(jnp.int32)[None])))
        other = place.soon(lax.dynamic_index_in_dim(self.stack, 1 - place.sequence, 0, keepdims=False))
        self.landed = place.to_pair(other)

    def to_chips(self):
        place = self.place
        own = lax.dynamic_index_in_dim(self.stack, place.sequence, 0, keepdims=False)
        total = (own.astype(F32) + place.now(self.landed).astype(F32)).astype(BF16)
        pieces = total.reshape(place.chips, -1, total.shape[1])
        self.kept = lax.dynamic_index_in_dim(pieces, place.chip, 0, keepdims=False)
        hops = range(1, place.chips)
        self.sent = [
            lax.dynamic_index_in_dim(pieces, (place.chip + hop) % place.chips, 0, keepdims=False) for hop in hops
        ]
        self.arrived = [place.to_chip(place.soon(piece), hop) for piece, hop in zip(self.sent, hops)]

    def total(self):
        return added(self.kept, self.place.now(tuple(self.arrived)))


def norm_rows(row_args, fixed_args, outs, kernel, name, choice=None):
    tokens = row_args[0].shape[0]
    block = min(128, tokens)

    def by_rows(cols):
        return pl.BlockSpec((block, cols), lambda i, *_: (i, 0))

    def fixed(shape):
        return pl.BlockSpec(shape, lambda i, *_: (0, 0))

    scalars = [] if choice is None else [choice]
    return pl.pallas_call(
        kernel,
        grid_spec=pltpu.PrefetchScalarGridSpec(
            num_scalar_prefetch=len(scalars),
            grid=(tokens // block,),
            in_specs=[by_rows(array.shape[1]) for array in row_args] + [fixed(array.shape) for array in fixed_args],
            out_specs=[by_rows(shape[1]) if shape[0] == tokens else fixed(shape) for shape, _ in outs],
        ),
        out_shape=[jax.ShapeDtypeStruct(shape, dtype) for shape, dtype in outs],
        compiler_params=pltpu.CompilerParams(vmem_limit_bytes=48 * 1024 * 1024),
        cost_estimate=SMALL_COST,
        name=name,
    )(*scalars, *row_args, *fixed_args)


def normed_rows(stream, gain):
    row_scale = lax.rsqrt(jnp.mean(stream * stream, axis=1, keepdims=True) + EPSILON)
    return stream * row_scale, row_scale


def norm_forward(stream, gain, share=None, arrived=(), scale=None):
    shape = stream.shape

    def plain(stream_ref, gain_ref, normed_ref):
        normed_ref[...] = (normed_rows(stream_ref[...].astype(F32), None)[0] * gain_ref[...]).astype(BF16)

    def updated(*refs):
        stream_ref, scale_ref, share_ref = refs[:3]
        gain_ref, out_ref, normed_ref = refs[-3:]
        update = share_ref[...].astype(F32)
        for ref in refs[3:-3]:
            update = update + ref[...].astype(F32)
        rows = stream_ref[...].astype(F32) + update * scale_ref[...]
        out_ref[...] = rows
        normed_ref[...] = (normed_rows(rows, None)[0] * gain_ref[...]).astype(BF16)

    if share is None:
        return stream, norm_rows([stream], [gain], [(shape, BF16)], plain, "norm_forward")[0]
    outs = [(shape, F32), (shape, BF16)]
    return norm_rows([stream, scale, share, *arrived], [gain], outs, updated, "norm_forward")


def norm_backward(streams, grads, share, arrived, gain, choice=None, entry=None, inner=None):
    features = gain.shape[1]
    tokens = share.shape[0]
    pick = 0 if choice is None else 1
    scale, parts = entry if entry else (None, ())

    def kernel(*refs):
        choice_ref, refs = (refs[0], refs[1:]) if pick else (None, refs)

        def chosen(pair):
            return pair[0][...].astype(F32) if not pick else jnp.where(choice_ref[0] == 0, pair[0][...].astype(F32), pair[1][...].astype(F32))

        count = 1 + pick
        stream, grad = chosen(refs[:count]), chosen(refs[count : 2 * count])
        refs = refs[2 * count :]
        grad_normed = refs[0][...].astype(F32)
        for ref in refs[1 : 1 + len(arrived)]:
            grad_normed = grad_normed + ref[...].astype(F32)
        refs = refs[1 + len(arrived) :]
        if entry:
            scale_ref, part_refs, refs = refs[0], refs[1 : 1 + len(parts)], refs[1 + len(parts) :]
        gain_ref, grad_ref, sum_ref = refs[:3]
        unit, row_scale = normed_rows(stream, None)
        lifted = grad_normed * gain_ref[...]
        grad = grad + row_scale * (lifted - unit * jnp.mean(lifted * unit, axis=1, keepdims=True))
        grad_ref[...] = grad

        @pl.when(pl.program_id(0) == 0)
        def _():
            sum_ref[...] = jnp.zeros_like(sum_ref)

        sum_ref[0:1] += jnp.sum(grad_normed * unit, axis=0, keepdims=True)
        if entry:
            up_ref, pull_ref = refs[3:5]
            row = scale_ref[...]
            up = (grad * row).astype(BF16)
            up_ref[...] = up
            update = sum(ref[...].astype(F32) for ref in part_refs)
            pull_ref[...] = jnp.sum(up.astype(F32) * update, axis=1, keepdims=True) * (row * row / inner)

    outs = [((tokens, features), F32), ((8, features), F32)]
    rows = [*streams, *grads, share, *arrived]
    if entry:
        outs += [((tokens, features), BF16), ((tokens, 1), F32)]
        rows += [scale, *parts]
    return norm_rows(rows, [gain], outs, kernel, "norm_backward", choice)


class Forward:
    def __init__(self, place, weights, tables, heads, inner):
        self.place, self.weights, self.tables, self.heads, self.inner = place, weights, tables, heads, inner
        self.kept = {}
        self.earlier = None

    def keep(self, **values):
        for key, value in values.items():
            self.kept.setdefault(key, []).append(value)

    def chunk(self, stream, normed):
        place, (gathered, _, own, thin) = self.place, self.weights
        columns, small = in_projection(place.now(normed), gathered, own, thin)
        mixed, square, y, saved, state = mixer_forward(columns, small, self.tables, self.heads, self.earlier)
        self.earlier = (state, columns, small)
        squares = [square] + place.sent_to_groups(square)
        share = place.did(out_projection(place.now(mixed), gathered, own))
        self.keep(stream=stream, normed=normed, columns=columns, small=small, mixed=mixed, y=y, saved=saved)
        self.keep(squares=squares, share=share, sent=place.sent_to_groups(share))

    def scale(self, at):
        if "scale" not in self.kept:
            self.kept["scale"] = [None] * PIECES
        if self.kept["scale"][at] is None:
            square = sum(self.place.now(tuple(self.kept["squares"][at])))
            self.kept["scale"][at] = lax.rsqrt(square / self.inner + EPSILON)
        return self.kept["scale"][at]


class Backward:
    def __init__(self, place, weights, tables, heads, inner, kept):
        self.place, self.weights, self.tables, self.heads, self.inner, self.kept = place, weights, tables, heads, inner, kept
        self.ups, self.grad_mixed, self.pulls = [None] * PIECES, [None] * PIECES, [None] * PIECES
        self.dcolumns, self.shares = [None] * PIECES, [None] * PIECES
        self.carried = None

    def enter(self, at, up, pull=None):
        gathered, _, own, _ = self.weights
        self.ups[at] = up
        self.grad_mixed[at], sums = mixed_gradient(self.place.now(up), gathered, own, self.kept["mixed"][at])
        self.place.did(self.grad_mixed[at])
        self.pulls[at] = [sums] + self.place.sent_to_groups(sums) if pull is None else pull

    def mix(self, at):
        kept, place = self.kept, self.place
        pull = self.pulls[at]
        if isinstance(pull, list):
            scale = kept["scale"][at]
            pull = sum(place.now(tuple(pull))) * (scale * scale / self.inner)
        result = mixer_backward(
            kept["columns"][at],
            kept["small"][at],
            kept["y"][at],
            kept["saved"][at],
            self.grad_mixed[at],
            place.now(pull),
            self.tables,
            self.heads,
            (kept["columns"][at - 1], kept["small"][at - 1]) if at else None,
            self.carried,
        )
        self.dcolumns[at], self.carried = place.did(result[0]), result[1:]

    def share(self, columns):
        gathered, _, own, thin = self.weights
        return self.place.did(normed_gradient(self.place.now(columns), gathered, own, thin))


def local(
    hidden,
    cotangent,
    norm_gain,
    in_weights,
    state_weight,
    step_weight,
    channel_taps,
    state_taps,
    step_bias,
    decay_log,
    skip_gain,
    inner_gain,
    out_weight,
):
    place = Place()
    layers = in_weights.shape[0]
    rows = in_weights.shape[2]
    heads = step_bias.shape[1]
    own_cols = in_weights.shape[3]
    width = own_cols // heads
    inner = own_cols * place.members
    shared = state_weight.shape[2]
    half = shared // 2
    copies = 128 // heads
    main = 2 * own_cols
    expand, tri = scan_tables(heads, own_cols)

    weights = []
    for layer in range(layers):
        if layer == 1:
            in_weights = then(in_weights, gathered)
        state_half = lax.dynamic_slice_in_dim(state_weight[layer], place.sequence * half, half, 1)
        thin = [step_weight[layer]] * 2
        blank = jnp.zeros((rows, 127 - 2 * heads), BF16)
        block = [out_weight[layer].T, in_weights[layer, 0], in_weights[layer, 1], state_half, *thin, blank]
        block = jnp.concatenate(block + [norm_gain[layer][:, None]], axis=1)
        if layer:
            gathered = place.gather_owners(block)
        else:
            gathered, sequence_rows = gathered_first(place, block, hidden)
        gain = gathered[: gathered.shape[0] // 2, -1].astype(F32)[None]
        weights.append((gathered, gain, own_cols, half + 128))

    per_channel = place.both(jnp.concatenate([channel_taps, inner_gain[:, None]], axis=1), 2)
    per_head = jnp.stack([step_bias, decay_log, skip_gain], axis=1)
    per_head = place.both(per_head[:, None], 1)
    tables = []
    for layer in range(layers):
        wide_skip = jnp.repeat(per_head[layer, :, 2].reshape(-1), width)[None]
        blank = jnp.zeros((1, main), F32)
        chan = jnp.concatenate([per_channel[layer, :5], wide_skip, per_channel[layer, 5:6], blank], axis=0)
        taps = jnp.concatenate([state_taps[layer], jnp.zeros((3, shared), F32)], axis=0)
        head = []
        for part in range(2):
            pair = jnp.stack([per_head[layer, part, 0], -jnp.exp(per_head[layer, part, 1])])
            pair = jnp.concatenate([pair, pair, jnp.zeros((2, 128 - 2 * heads), F32)], axis=1)
            head += [pair, jnp.zeros((6, 128), F32)]
        tables.append((chan, taps, jnp.concatenate(head), expand, tri))

    rows_in = jnp.split(sequence_rows, PIECES)
    kept = []
    for layer in range(layers):
        final = layer == layers - 1
        gathered, gain = weights[layer][:2]
        if layer:
            weights[layer] = (place.now(gathered),) + weights[layer][1:]
            before = kept[-1]
            for at in range(PIECES):
                place.soon(previous.scale(at))
        forward = Forward(place, weights[layer], tables[layer], heads, inner)
        for at in range(PIECES):
            if layer:
                landed = list(place.now(tuple(before["sent"][at])))
                before.setdefault("update", []).append([before["share"][at], *landed])
                stream, normed = norm_forward(
                    before["stream"][at], gain, before["share"][at], landed, previous.scale(at)
                )
            else:
                stream, normed = norm_forward(place.now(rows_in[at]), gain)
            if final and at == 0:
                taken = place.take_sequence(then(cotangent, normed))
            forward.chunk(stream, normed)
            if final and at == 0:
                last_up = place.gather_chunks(place.in_order(*place.now(taken)), PIECES)
        kept.append(forward.kept)
        previous = forward
    for at in range(PIECES):
        previous.scale(at)
    shares = kept[-1]["share"]
    mixed_sent = [place.to_group(place.soon(place.rows_of(shares, hop)), hop) for hop in range(1, place.groups)]
    grads = last_up()
    in_sums, out_sums, gain_grads, carried = [None] * layers, [None] * layers, [0.0] * layers, [None] * layers
    pending, waiting = None, []

    def small_sums(layer):
        gchan, gtaps, ghead = carried[layer]
        blank = jnp.zeros((1, own_cols - 256), F32)
        parts = []
        for part in range(2):
            per_head_row = jnp.concatenate([ghead[8 * part : 8 * part + 1], ghead[8 * part + 1 : 8 * part + 2], blank], axis=1)
            parts.append(jnp.concatenate([gchan[:7, part * own_cols : (part + 1) * own_cols], per_head_row]))
        return jnp.stack(parts), gtaps

    for layer in reversed(range(layers)):
        final = layer == layers - 1
        back = Backward(place, weights[layer], tables[layer], heads, inner, kept[layer])
        for at in reversed(range(PIECES)):
            scale = kept[layer]["scale"][at]
            if final:
                back.enter(at, (grads[at].astype(F32) * scale).astype(BF16))
                continue
            share, arrived = pending[at]
            grads[at], gain_grad, up, pull = norm_backward(
                [kept[layer + 1]["stream"][at]],
                [grads[at]],
                share,
                list(place.now(tuple(arrived))),
                weights[layer + 1][1],
                None,
                (scale, kept[layer]["update"][at]),
                inner,
            )
            gain_grads[layer + 1] = gain_grads[layer + 1] + jnp.where(place.group == 0, gain_grad[0], 0.0)
            back.enter(at, up, pull)
        normed, mixed = kept[layer]["normed"], kept[layer]["mixed"]
        out_sum = out_sums[layer] = WeightSum(place, back.ups, mixed)
        out_sum.to_pair()
        if layer == 0:
            far_normed = [place.to_core(part) for part in normed]
        far_columns, pending = [None] * PIECES, [None] * PIECES
        for at in reversed(range(PIECES)):
            back.mix(at)
            if layer == 0:
                far_columns[at] = place.to_core(back.dcolumns[at])
            if at == PIECES - 1:
                for later in out_sums[layer + 1 :]:
                    later.owned = later.total()
                if layer == 0:
                    own_rows = place.rows_of(kept[-1]["stream"], 0).astype(F32)
                    update = added(place.rows_of(shares, 0), place.now(tuple(mixed_sent)))
                    mixed_out = place.give_sequence(own_rows + update * place.rows_of(kept[-1]["scale"], 0))
            if layer:
                share = back.share(back.dcolumns[at])
                pending[at] = (share, place.sent_to_groups(share))
                if at == PIECES - 1:
                    out_sum.to_chips()
        carried[layer] = back.carried[3:]
        waiting.append(small_sums(layer))
        if layer:
            in_sum = in_sums[layer] = Owned()
            stack = place.did(stacked_product(list(place.now(tuple(normed))), back.dcolumns))
            in_sum.owned = place.scatter_owners(stack).astype(F32)
            continue
        in_sum = in_sums[layer] = WeightSum(place, normed, back.dcolumns, far_normed, far_columns)
        if PIECES == place.groups:
            sent = [back.share(place.rows_of(back.dcolumns, hop)) for hop in range(1, place.groups)]
            arrived = [place.to_group(piece, hop) for hop, piece in enumerate(sent, 1)]
            own = back.share(place.rows_of(back.dcolumns, 0))
        else:
            done = [back.share(columns) for columns in back.dcolumns]
            arrived = [place.to_group(place.rows_of(done, hop), hop) for hop in range(1, place.groups)]
            own = place.rows_of(done, 0)
        out_sum.to_chips()
        stream_parts, grad_parts, choice = kept[layer]["stream"], grads, place.group.astype(jnp.int32)[None]
        if PIECES != place.groups:
            stream_parts, grad_parts, choice = [place.rows_of(stream_parts, 0)], [place.rows_of(grads, 0)], None
        arrived = list(place.now(tuple(arrived)))
        grad, gain_grad = norm_backward(stream_parts, grad_parts, own, arrived, weights[layer][1], choice)
        place.did(grad)
        gain_grads[layer] = gain_grad[0]
    grad_hidden = place.give_sequence(grad)

    halves = jnp.concatenate([part for part, _ in reversed(waiting)], axis=1)
    gains = jnp.stack(gain_grads).reshape(-1, shared)
    common = [part for _, part in reversed(waiting)] + [gains, jnp.zeros((-gains.shape[0] % 8, shared), F32)]
    common = then(place.now(jnp.concatenate(common)), *out_sums[0].sent)
    in_sums[0].owned, half_total, common_total = reduced_product(place, in_sum.lhs, in_sum.rhs, halves, common, 0)
    place.did(in_sums[0].owned)
    out_sums[0].owned = out_sums[0].total()
    gain_total = common_total[8 * layers : 8 * layers + gains.shape[0]].reshape(layers, -1)

    state_parts = jnp.concatenate([in_sum.owned[:, main : main + half] for in_sum in in_sums])
    state_parts = place.both(place.add_groups(place.now(state_parts)), 1).reshape(layers, rows, shared)
    outs = []
    for layer in range(layers):
        per_channel_part = half_total[8 * layer : 8 * layer + 8]
        gain_part = lax.dynamic_slice_in_dim(gain_total[layer], lax.axis_index("dp") * rows, rows, 0)
        taps_part = common_total[8 * layer : 8 * layer + 5]
        in_owned, out_owned = in_sums[layer].owned, out_sums[layer].owned
        outs.append(
            (
                gain_part,
                jnp.stack([in_owned[:, :own_cols], in_owned[:, own_cols:main]]),
                state_parts[layer],
                in_owned[:, main + half : main + half + heads],
                per_channel_part[:5],
                taps_part,
                per_channel_part[7, :heads],
                per_channel_part[7, 128 : 128 + heads],
                per_channel_part[5].reshape(heads, width).sum(axis=1),
                per_channel_part[6],
                out_owned.T,
            )
        )
    mixed_out = place.both_sequences(mixed_out)
    grad_hidden = place.both_sequences(grad_hidden)
    return (mixed_out, grad_hidden) + tuple(jnp.stack(parts) for parts in zip(*outs))


def solution(mesh):
    placed = (
        P("dp", "tensor", None),
        P("dp", "tensor", None),
        P(None, "dp"),
        P(None, None, "dp", "tensor"),
        P(None, "dp", None),
        P(None, "dp", "tensor"),
        P(None, None, "tensor"),
        P(),
        P(None, "tensor"),
        P(None, "tensor"),
        P(None, "tensor"),
        P(None, "tensor"),
        P(None, "tensor", "dp"),
    )
    return jax.shard_map(
        local,
        mesh=mesh,
        in_specs=placed,
        out_specs=(
            P("dp", "tensor", None),
            P("dp", "tensor", None),
            P(None, "dp"),
            P(None, None, "dp", "tensor"),
            P(None, "dp", None),
            P(None, "dp", "tensor"),
            P(None, None, "tensor"),
            P(),
            P(None, "tensor"),
            P(None, "tensor"),
            P(None, "tensor"),
            P(None, "tensor"),
            P(None, "tensor", "dp"),
        ),
        check_vma=False,
    )
```
